32 devices in a mesh: dp: 8 (over z, core), fsdp: 4 (over y, x).
Axes of the slice: x: 2, y: 2, z: 4, core: 2. Of those that a mesh axis runs over, the one named last changes fastest.
Arguments:
- tokens: bfloat16 [8192, 1024], P(('dp', 'fsdp')), may hold values from -6 to 6
- value_first: bfloat16 [8192, 1024], P(('dp', 'fsdp')), may hold values from -6 to 6
- window_split: int32 [8], P('dp'), may hold values from 0 to 1, as said below
- cotangent: bfloat16 [8192, 1024], P(('dp', 'fsdp')), may hold values from -6 to 6
- running_grad: float32 [8192, 1024], P(('dp', 'fsdp')), may hold values from -6 to 6
- gain_attn: bfloat16 [1024], P('fsdp'), may hold values from 0.5 to 1.5
- w_query: bfloat16 [1024, 1024], P('fsdp'), may hold values from -0.1875 to 0.1875
- w_key: bfloat16 [1024, 1024], P('fsdp'), may hold values from -0.1875 to 0.1875
- w_value: bfloat16 [1024, 1024], P('fsdp'), may hold values from -0.1875 to 0.1875
- w_out: bfloat16 [1024, 1024], P('fsdp'), may hold values from -1.5 to 1.5
- gain_mlp: bfloat16 [1024], P('fsdp'), may hold values from 0.5 to 1.5
- w_gate: bfloat16 [1024, 2816], P('fsdp'), may hold values from -0.1875 to 0.1875
- w_up: bfloat16 [1024, 2816], P('fsdp'), may hold values from -0.1875 to 0.1875
- w_down: bfloat16 [2816, 1024], P('fsdp'), may hold values from -0.109375 to 0.109375
Outputs:
- layer_out: bfloat16 [8192, 1024], P(('dp', 'fsdp'))
- input_grad: float32 [8192, 1024], P(('dp', 'fsdp'))
- first_grad: float32 [8192, 1024], P(('dp', 'fsdp'))
- grad_gain_attn: float32 [1024], P('fsdp')
- grad_query: float32 [1024, 1024], P('fsdp')
- grad_key: float32 [1024, 1024], P('fsdp')
- grad_value: float32 [1024, 1024], P('fsdp')
- grad_out: float32 [1024, 1024], P('fsdp')
- grad_gain_mlp: float32 [1024], P('fsdp')
- grad_gate: float32 [1024, 2816], P('fsdp')
- grad_up: float32 [1024, 2816], P('fsdp')
- grad_down: float32 [2816, 1024], P('fsdp')
The draws below stay inside these ranges and needn't reach their ends.
Inputs may be any that keep to these rules, and one draw needn't show every extreme that they name: `window_split`: both values occur in every draw.
All inputs are finite; a program needn't handle non-finite values.
Results may differ from the reference program's by a relative error of at most 0.035.
Values may be sent and summed in bfloat16 or wider, within the bound.
A program may use at most 192 MiB of HBM per device.

```python
import jax
import jax.numpy as jnp
from jax import lax

HD = 64
D = 1024
FF = 2816
WINDOW = 1024
BATCH = 8
TOKENS = 8192


def draw_window_split(key, part):
    key = jax.random.fold_in(key, 11)
    flag_key, order_key = jax.random.split(key)
    flags = jax.random.randint(flag_key, (BATCH,), 0, 2, dtype=jnp.int32)
    order = jax.random.permutation(order_key, BATCH)
    flags = flags.at[order[0]].set(0)
    flags = flags.at[order[1]].set(1)
    return flags


def shard_levels(stream_key, shape, shards, smallest, high):
    loudness = 1.0
    for dim, blocks in shards:
        draws = jax.random.uniform(jax.random.fold_in(jax.random.fold_in(stream_key, 6), dim), (blocks,), jnp.float32, smallest / len(shards), high / len(shards))
        loudness = loudness * jnp.repeat(jnp.exp(draws), shape[dim] // blocks).reshape((-1,) + (1,) * (len(shape) - 1 - dim))
    return loudness


def noise(stream_key, dims, scale, most, cuts=(), held_as=jnp.bfloat16):
    array = jax.random.normal(stream_key, dims, jnp.float32) * scale
    if len(cuts) > 0:
        array = shard_levels(stream_key, dims, cuts, -0.22, 0.18) * array
    return jnp.clip(array, min=-most, max=most).astype(held_as)


def setup_inputs(seed: int = 0) -> dict:
    key_of = jax.random.split(jax.random.key(seed), 15)
    return {
        "tokens": noise(key_of[0], (TOKENS, D), 1.0, 6.0, ((0, 32),)),
        "value_first": noise(key_of[1], (TOKENS, D), 1.0, 6.0, ((0, 32),)),
        "window_split": draw_window_split(jax.random.fold_in(key_of[14], 71), 0),
        "cotangent": noise(key_of[3], (TOKENS, D), 1.0, 6.0, ((0, 32),)),
        "running_grad": noise(key_of[4], (TOKENS, D), 1.0, 6.0, ((0, 32),), jnp.float32),
        "gain_attn": jnp.clip(1.0 + 0.1 * jax.random.normal(key_of[5], (D,), jnp.float32), 0.5, 1.5).astype(jnp.bfloat16),
        "w_query": noise(key_of[6], (D, D), D ** -0.5, 0.1875, ((0, 4),)),
        "w_key": noise(key_of[7], (D, D), D ** -0.5, 0.1875, ((0, 4),)),
        "w_value": noise(key_of[8], (D, D), D ** -0.5, 0.1875, ((0, 4),)),
        "w_out": noise(key_of[9], (D, D), (D // 64) ** -0.5, 1.5, ((0, 4),)),
        "gain_mlp": jnp.clip(1.0 + 0.1 * jax.random.normal(key_of[10], (D,), jnp.float32), 0.5, 1.5).astype(jnp.bfloat16),
        "w_gate": noise(key_of[11], (D, FF), D ** -0.5, 0.1875, ((0, 4),)),
        "w_up": noise(key_of[12], (D, FF), D ** -0.5, 0.1875, ((0, 4),)),
        "w_down": noise(key_of[13], (FF, D), FF ** -0.5, 0.109375, ((0, 4),)),
    }


EPS = 1e-06

@jax.custom_vjp
def low(v):
    return lax.optimization_barrier(v.astype(jnp.bfloat16)).astype(jnp.float32)

@jax.custom_vjp
def low_back(v):
    return v

def low_keep(v):
    return (low(v), None)

def low_pass(kept, grad):
    return (grad,)

def back_keep(v):
    return (v, None)

def back_low(kept, grad):
    return (low(grad),)
low.defvjp(low_keep, low_pass)
low_back.defvjp(back_keep, back_low)

def exact_dot(left_side, right_side):
    return jnp.dot(left_side, right_side, precision=lax.Precision.HIGHEST, preferred_element_type=jnp.float32)

def normalize(hidden, weight):
    return hidden * lax.rsqrt(lax.optimization_barrier(jnp.mean(hidden * hidden, axis=-1, keepdims=True)) + EPS) * weight

def rope_tables(position):
    half_dim = HD // 2
    frequency = 10000.0 ** (-jnp.arange(half_dim, dtype=jnp.float32) / half_dim)
    angles = position.astype(jnp.float32)[:, None] * frequency[None, :]
    return (jnp.cos(angles), jnp.sin(angles))

def rotate(values, cosine, sine_part):
    count_rows = values.shape[0]
    shaped = values.reshape(count_rows, -1, HD)
    first_half = shaped[..., :HD // 2]
    second_half = shaped[..., HD // 2:]
    cos_wide = cosine[:, None, :]
    sin_wide = sine_part[:, None, :]
    turned = jnp.concatenate([first_half * cos_wide - second_half * sin_wide, second_half * cos_wide + first_half * sin_wide], axis=-1)
    return turned.reshape(count_rows, -1)

def window_forward(window_in, value_in, split_flag, gain_attn, w_query, w_key, w_value, w_out, gain_mlp, w_gate, w_up, w_down):
    window_len = window_in.shape[0]
    position = jnp.arange(window_len, dtype=jnp.int32)
    seq_len = jnp.where(split_flag == 1, window_len // 2, window_len).astype(jnp.int32)
    segment = position // seq_len
    allowed = (segment[:, None] == segment[None, :]) & (position[None, :] <= position[:, None])
    cosine, sine_part = rope_tables(position % seq_len)
    normed = low(normalize(window_in, gain_attn))
    query_pre = low_back(exact_dot(normed, w_query))
    key_pre = low_back(exact_dot(normed, w_key))
    value_pre = low_back(exact_dot(normed, w_value))
    queries = low(rotate(query_pre, cosine, sine_part))
    keys_all = low(rotate(key_pre, cosine, sine_part))
    values_all = low(0.5 * value_pre + 0.5 * value_in)
    head_count = w_query.shape[1] // HD
    score_scale = HD ** (-0.5)

    def by_head(matrix):
        return matrix.reshape(window_len, head_count, HD).transpose(1, 0, 2)

    def one_head(operands):
        head_query, head_key, head_value = operands
        scores = low_back(exact_dot(head_query, head_key.T) * score_scale)
        scores = jnp.where(allowed, scores, -1e+30)
        probability = jax.nn.softmax(scores, axis=-1)
        return exact_dot(low(probability), head_value)
    attended = lax.map(jax.checkpoint(one_head), (by_head(queries), by_head(keys_all), by_head(values_all)))
    attended = attended.transpose(1, 0, 2).reshape(window_len, -1)
    attended = low_back(low(attended))
    branch = low_back(exact_dot(attended, w_out))
    middle = window_in + branch
    normed_mlp = low(normalize(middle, gain_mlp))
    gate_act = low_back(exact_dot(normed_mlp, w_gate))
    up_act = low_back(exact_dot(normed_mlp, w_up))
    hidden_act = low(jax.nn.silu(gate_act) * up_act)
    return middle + exact_dot(hidden_act, w_down)

def reference(tokens, value_first, window_split, cotangent, running_grad, gain_attn, w_query, w_key, w_value, w_out, gain_mlp, w_gate, w_up, w_down):

    def shaped(matrix):
        return matrix.astype(jnp.float32).reshape(BATCH, WINDOW, -1)
    per_window = jax.checkpoint(window_forward)

    def layer_forward(window_in, value_in, gain_one, query_w, key_w, value_w, out_w, gain_two, gate_w, up_w, down_w):

        def apply_one(item):
            return per_window(item[0], item[1], item[2], gain_one, query_w, key_w, value_w, out_w, gain_two, gate_w, up_w, down_w)
        return lax.map(apply_one, (window_in, value_in, window_split))
    outputs, pullback = jax.vjp(layer_forward, shaped(tokens), shaped(value_first), gain_attn.astype(jnp.float32), w_query.astype(jnp.float32), w_key.astype(jnp.float32), w_value.astype(jnp.float32), w_out.astype(jnp.float32), gain_mlp.astype(jnp.float32), w_gate.astype(jnp.float32), w_up.astype(jnp.float32), w_down.astype(jnp.float32))
    gradients = pullback(shaped(cotangent))
    layer_out = outputs.reshape(TOKENS, D).astype(jnp.bfloat16)
    input_grad = gradients[0].reshape(TOKENS, D)
    first_grad = running_grad + gradients[1].reshape(TOKENS, D)
    return (layer_out, input_grad, first_grad, gradients[2], gradients[3], gradients[4], gradients[5], gradients[6], gradients[7], gradients[8], gradients[9], gradients[10])
```

```python
import functools

import jax
import jax.numpy as jnp
import numpy as np
from jax import lax
from jax.experimental import pallas as pl
from jax.experimental.pallas import tpu as pltpu
from jax.sharding import PartitionSpec as P

HD = 64
EPS = 1e-06
MESH = pl.DeviceIdType.MESH
BF = jnp.bfloat16
F32 = jnp.float32
LIMIT = 60 * 1024 * 1024


def dot_nn(a, b):
    return lax.dot_general(a, b, (((1,), (0,)), ((), ())), preferred_element_type=F32)


def dot_nt(a, b):
    return lax.dot_general(a, b, (((1,), (1,)), ((), ())), preferred_element_type=F32)


def dot_tn(a, b):
    return lax.dot_general(a, b, (((0,), (0,)), ((), ())), preferred_element_type=F32)


def flip(f, k, n):
    out, bit = 0, 1
    while bit < n:
        have, want = lax.rem(f // bit, 2), (k // bit) % 2
        out = out + (1 - have if want else have) * bit
        bit *= 2
    return out


class Net:
    def __init__(self, n, ssem, rsem, lsem=None):
        self.n, self.ssem, self.rsem, self.lsem = n, ssem, rsem, lsem
        self.d, self.f = lax.axis_index("dp"), lax.axis_index("fsdp")
        self.c = lax.rem(self.d, 2)
        self.mate = (self.d + 1 - 2 * self.c, self.f)
        self.used, self.lused, self.sent = 0, 0, []

    def peer(self, k):
        return (self.d, flip(self.f, k, self.n))

    def take(self, count=1):
        self.used += count
        return self.used - count

    def push(self, src, dst, device, slot=None):
        slot = self.take() if slot is None else slot
        copy = pltpu.make_async_remote_copy(
            src_ref=src,
            dst_ref=dst,
            send_sem=self.ssem.at[slot],
            recv_sem=self.rsem.at[slot],
            device_id=device,
            device_id_type=MESH,
        )
        copy.start()
        self.sent.append(copy)
        return copy

    def local(self, src, dst):
        copy = pltpu.make_async_copy(src, dst, self.lsem.at[self.lused])
        self.lused += 1
        copy.start()
        return copy

    def barrier(self, devices):
        sem = pltpu.get_barrier_semaphore()
        for device in devices:
            pl.semaphore_signal(sem, inc=1, device_id=device, device_id_type=MESH)
        pl.semaphore_wait(sem, len(devices))

    def drain(self):
        for copy in self.sent:
            copy.wait_send()


def rows_of(ref, block, size):
    return ref.at[pl.ds(pl.multiple_of(block * size, size), size)]


class Gather:
    def __init__(self, net, own, into, size):
        self.net, self.into, self.size = net, into, size
        self.direct = [1, 2] if net.n == 4 else list(range(1, net.n))
        self.copies = {k: net.push(own, rows_of(into, net.f, size), net.peer(k)) for k in self.direct}
        self.halves = {}

    def part(self, block, half):
        start = pl.multiple_of(block * self.size + half * (self.size // 2), self.size // 2)
        return self.into.at[pl.ds(start, self.size // 2)]

    def wait(self, k):
        net = self.net
        if k in self.copies:
            self.copies[k].wait_recv()
            if net.n == 4:
                part = self.part(flip(net.f, k, 4), k - 1)
                self.halves[k] = net.push(part, part, net.peer(3 - k))
        else:
            for copy in self.halves.values():
                copy.wait_recv()


def lane_mask(width, head):
    lane = lax.broadcasted_iota(jnp.int32, (1, width), 1)
    return (lane // HD) == head


def turn(values, cos, sin):
    width = values.shape[1]
    lane = lax.broadcasted_iota(jnp.int32, (1, width), 1)
    first = lax.rem(lane, HD) < HD // 2
    other = jnp.where(
        first, pltpu.roll(values, width - HD // 2, 1), pltpu.roll(values, HD // 2, 1)
    )
    return values * cos + other * sin


def table_rows(net, cos_ref, sin_ref, flag, start, size, length, width):
    half = length // 2
    plain = pl.ds(pl.multiple_of(start, size), size)
    split = pl.ds(pl.multiple_of(lax.rem(start, half), size), size)
    out = []
    for ref in (cos_ref, sin_ref):
        rows = jnp.where(flag == 1, ref[split], ref[plain])
        out.append(jnp.concatenate([rows] * (width // rows.shape[1]), axis=1))
    return out


def block_bias(flag, r, kb, size, length):
    half = length // 2
    if kb == r:
        row = lax.broadcasted_iota(jnp.int32, (size, size), 0)
        col = lax.broadcasted_iota(jnp.int32, (size, size), 1)
        return jnp.where(col <= row, 0.0, -1e30)
    if (r * size >= half) != (kb * size >= half):
        return jnp.where(flag == 1, -1e30, 0.0)
    return None


def scores_of(query, key, bias):
    scores = dot_nt(query, key)
    return scores if bias is None else scores + bias


def factor_of(hidden):
    return lax.rsqrt(jnp.mean(hidden * hidden, axis=-1, keepdims=True) + EPS)


def norm_back(hidden, gain, grad):
    factor = factor_of(hidden)
    scaled = grad * gain
    return factor * scaled - hidden * (factor * factor * factor) * jnp.mean(
        scaled * hidden, axis=-1, keepdims=True
    )


def share_columns(net, pieces, into, rows):
    half = rows // 2
    out = []
    for k in range(1, net.n):
        device = net.peer(k)
        src = pieces(device[1]).at[pl.ds(pl.multiple_of(net.c * half, half), half)]
        start = pl.multiple_of(net.f * rows + net.c * half, half)
        out.append((k, net.push(src, into.at[pl.ds(start, half)], device)))
    return out


def forward_columns(net, copies, into, rows):
    half = rows // 2
    out = []
    for k, copy in copies:
        copy.wait_recv()
        start = pl.multiple_of(flip(net.f, k, net.n) * rows + net.c * half, half)
        part = into.at[pl.ds(start, half)]
        out.append(net.push(part, part, net.mate))
    return out


def gain_rows(net, src, dst, rows):
    place = dst.at[:, pl.ds(pl.multiple_of(net.f * rows, rows), rows)]
    dst[:, pl.ds(pl.multiple_of(net.f * rows, rows), rows)] = jnp.broadcast_to(src[...], (16, rows))
    return [net.push(place, place, net.peer(k)) for k in range(1, net.n)]


def send_to(net, r, src, dst, base, away=None):
    return pltpu.make_async_remote_copy(
        src_ref=src,
        dst_ref=dst,
        send_sem=net.ssem.at[base + r],
        recv_sem=net.rsem.at[base + (net.f if away is None else away)],
        device_id=(net.d, r),
        device_id_type=MESH,
    )


def front_kernel(
    n,
    x,
    vf,
    wq,
    wk,
    wv,
    wo,
    g1,
    g2,
    flag_ref,
    cos_ref,
    sin_ref,
    wg,
    wu,
    qkv,
    lse,
    att,
    nrm,
    mid,
    nm,
    wqkv,
    wgc,
    wuc,
    g1_all,
    g2_all,
    x_all,
    vfc,
    sb,
    rb,
    own,
    wgr,
    wur,
    ssem,
    rsem,
    lsem,
):
    net = Net(n, ssem, rsem, lsem)
    size, width = x.shape
    length = n * size
    cols = width // n
    rows = wq.shape[0]
    hidden = wgc.shape[1]
    flag = flag_ref[0]
    net.barrier([net.peer(k) for k in range(1, n)] + [net.mate])
    mine = pl.multiple_of(net.f * cols, cols)
    gains = gain_rows(net, g1, g1_all, rows) + gain_rows(net, g2, g2_all, rows)
    x_gather = Gather(net, x, x_all, size)
    weights = []
    for i, w in enumerate((wq, wk, wv)):
        into = wqkv.at[:, pl.ds(i * cols, cols)]
        pieces = lambda to, w=w: w.at[:, pl.ds(pl.multiple_of(to * cols, cols), cols)]
        weights.append((share_columns(net, pieces, into, rows), into))
    values = []
    for k in range(1, n):
        device = net.peer(k)
        src = vf.at[:, pl.ds(pl.multiple_of(device[1] * cols, cols), cols)]
        values.append(net.push(src, rows_of(vfc, net.f, size), device))
    locals_ = [net.local(x, rows_of(x_all, net.f, size))]
    locals_.append(net.local(vf.at[:, pl.ds(mine, cols)], rows_of(vfc, net.f, size)))
    for i, w in enumerate((wq, wk, wv)):
        into = rows_of(wqkv.at[:, pl.ds(i * cols, cols)], net.f, rows)
        locals_.append(net.local(w.at[:, pl.ds(mine, cols)], into))
    for w, piece in ((wg, wgr), (wu, wur)):
        for r in range(n):
            piece[r] = w[:, r * hidden : (r + 1) * hidden]
    for copy in locals_:
        copy.wait()
    for copy in gains:
        copy.wait_recv()
    gain = g1_all[0:1, :].astype(F32)

    def normalize(block):
        at = pl.ds(pl.multiple_of(block * size, size), size)
        rows_in = x_all[at].astype(F32)
        nrm[at] = (rows_in * factor_of(rows_in) * gain).astype(BF)

    normalize(net.f)
    for k in range(1, n):
        x_gather.wait(k)
        normalize(flip(net.f, k, n))
    mates = []
    for copies, into in weights:
        mates += forward_columns(net, copies, into, rows)
    for copy in mates + values:
        copy.wait_recv()
    gates = []
    for piece, into in ((wgr, wgc), (wur, wuc)):
        gates.append((share_columns(net, lambda to, piece=piece: piece.at[to], into, rows), into))
        into[pl.ds(pl.multiple_of(net.f * rows, rows), rows)] = piece[net.f]

    @pl.loop(0, n)
    def _(block):
        at = pl.ds(pl.multiple_of(block * size, size), size)
        pre = dot_nn(nrm[at], wqkv[...])
        cos, sin = table_rows(net, cos_ref, sin_ref, flag, block * size, size, length, 2 * cols)
        turned = turn(pre[:, : 2 * cols], cos, sin)
        mixed = 0.5 * pre[:, 2 * cols :] + 0.5 * vfc[at].astype(F32)
        qkv[at, :cols] = (turned[:, :cols] * HD**-0.5).astype(BF)
        qkv[at, cols : 2 * cols] = turned[:, cols:].astype(BF)
        qkv[at, 2 * cols :] = mixed.astype(BF)

    heads = cols // HD
    base = net.take(n)
    lane = lax.broadcasted_iota(jnp.int32, (1, 128), 1)
    for r in range(n):
        at = slice(r * size, (r + 1) * size)
        query = qkv[at, :cols]
        total = jnp.zeros((size, cols), F32)
        stats = jnp.zeros((size, 128), F32)
        biases = [block_bias(flag, r, kb, size, length) for kb in range(r + 1)]
        for h in range(heads):
            mask = lane_mask(cols, h)
            masked = jnp.where(mask, query, jnp.zeros_like(query))
            tiles = [
                scores_of(masked, qkv[kb * size : (kb + 1) * size, cols : 2 * cols], biases[kb])
                for kb in range(r + 1)
            ]
            top = tiles[0].max(axis=1, keepdims=True)
            for tile in tiles[1:]:
                top = jnp.maximum(top, tile.max(axis=1, keepdims=True))
            raw = [jnp.exp(tile - top) for tile in tiles]
            whole = raw[0].sum(axis=1, keepdims=True)
            for tile in raw[1:]:
                whole = whole + tile.sum(axis=1, keepdims=True)
            inverse = 1.0 / whole
            mixed = None
            for kb, tile in enumerate(raw):
                term = dot_nn(
                    (tile * inverse).astype(BF), qkv[kb * size : (kb + 1) * size, 2 * cols :]
                )
                mixed = term if mixed is None else mixed + term
            total = jnp.where(mask, mixed, total)
            stats = jnp.where(lane == h, top + jnp.log(whole), stats)
        lse[at] = stats
        att[at] = total.astype(BF)
        part = dot_nn(att[at], wo[...])
        sb[r] = part.astype(BF)

        @pl.when(net.f == r)
        def _():
            own[...] = part

        @pl.when(net.f != r)
        def _():
            send_to(net, r, sb.at[r], rb.at[net.f], base).start()

    sums = x[...].astype(F32) + own[...]
    for k in range(1, n):
        other = flip(net.f, k, n)
        send_to(net, other, sb.at[other], rb.at[other], base, other).wait()
        sums = sums + rb[other].astype(F32)
    mid[...] = sums
    nm[...] = (sums * factor_of(sums) * g2_all[0:1, :].astype(F32)).astype(BF)
    mates = []
    for copies, into in gates:
        mates += forward_columns(net, copies, into, rows)
    for copy in mates:
        copy.wait_recv()
    net.drain()


def middle_kernel(
    n,
    nm,
    mid,
    ct,
    wgc,
    wuc,
    wd,
    g2_all,
    gmid,
    gb,
    base_out,
    sb1,
    grad_gate,
    grad_up,
    grad_down,
    nm_all,
    g_all,
    hid_all,
    gg_all,
    ug_all,
    coef,
    silus,
    sb2,
    rb2,
    own2,
    ssem,
    rsem,
    lsem,
):
    net = Net(n, ssem, rsem, lsem)
    size, width = nm.shape
    net.barrier([net.peer(k) for k in range(1, n)])
    gather = Gather(net, nm, nm_all, size)
    g_gather = Gather(net, ct, g_all, size)
    locals_ = [net.local(nm, rows_of(nm_all, net.f, size)), net.local(ct, rows_of(g_all, net.f, size))]

    def rows_at(k):
        return pl.ds(pl.multiple_of(flip(net.f, k, n) * size, size), size)

    def forward(k):
        at = rows_at(k)
        a = nm_all[at]
        gate = dot_nn(a, wgc[...])
        up = dot_nn(a, wuc[...])
        sig = jax.nn.sigmoid(gate)
        silu = gate * sig
        hid_all[at] = (silu * up).astype(BF)
        coef[at] = up * sig * (1.0 + gate * (1.0 - sig))
        silus[at] = silu
        part = dot_nn(hid_all[at], wd[...])
        if k == 0:
            base_out[...] = mid[...] + part
        else:
            sb1[k] = part.astype(BF)

    soon = []

    def backward(k):
        at = rows_at(k)
        grad = dot_nt(g_all[at], wd[...])
        gg_all[at] = (grad * coef[at]).astype(BF)
        ug_all[at] = (grad * silus[at]).astype(BF)
        back = dot_nt(gg_all[at], wgc[...]) + dot_nt(ug_all[at], wuc[...])
        if k == 0:
            own2[...] = back
        else:
            sb2[k] = back.astype(BF)
            soon.append((k, net.push(sb2.at[k], rb2.at[k], net.peer(k))))

    sb1[0] = jnp.zeros(sb1.shape[1:], BF)
    for copy in locals_:
        copy.wait()
    forward(0)
    backward(0)
    for k in range(1, n):
        gather.wait(k)
        if k == 2 or n == 2:
            forward(1)
        if k >= 2:
            forward(k)
    for k in range(1, n):
        g_gather.wait(k)
        if k == 2 or n == 2:
            backward(1)
        if k >= 2:
            backward(k)
    tile = 256 if width % 256 == 0 else width

    @pl.loop(0, width // tile)
    def _(i):
        at = pl.ds(pl.multiple_of(i * tile, tile), tile)
        lhs = nm_all[:, at]
        grad_gate[at] = dot_tn(lhs, gg_all[...]).astype(BF)
        grad_up[at] = dot_tn(lhs, ug_all[...]).astype(BF)
        grad_down[:, at] = dot_tn(hid_all[...], g_all[:, at]).astype(BF)

    grad = own2[...]
    for k, copy in soon:
        copy.wait_recv()
        grad = grad + rb2[k].astype(F32)
    total = ct[...].astype(F32) + norm_back(mid[...], g2_all[0:1, :].astype(F32), grad)
    gmid[...] = total
    gb[...] = total.astype(BF)
    net.drain()


class Line:
    def __init__(self, net, chips):
        chip, middle = net.d // 2, chips // 2
        left = chip < middle
        inward = jnp.where(left, chip + 1, chip - 1)
        outward = jnp.where(left, chip - 1, chip + 1)
        self.net = net
        self.edge = (chip == 0) | (chip == chips - 1)
        self.middle = (chip == middle - 1) | (chip == middle)
        self.inner = (inward * 2 + net.c, net.f)
        self.outer = (outward * 2 + net.c, net.f)
        self.chunks = []

    def barrier(self, others):
        net, sem = self.net, pltpu.get_barrier_semaphore()
        fixed = others + [self.inner]
        for device in fixed:
            pl.semaphore_signal(sem, inc=1, device_id=device, device_id_type=MESH)

        @pl.when(jnp.logical_not(self.edge))
        def _():
            pl.semaphore_signal(sem, inc=1, device_id=self.outer, device_id_type=MESH)
            pl.semaphore_wait(sem, len(fixed) + 1)

        @pl.when(self.edge)
        def _():
            pl.semaphore_wait(sem, len(fixed))

    def chunk(self, own, outer, out, ready=None):
        slots = [self.net.take() for _ in range(4)]
        self.chunks.append((own, outer, out, ready, slots))

    def copy(self, src, dst, send, recv, device):
        return pltpu.make_async_remote_copy(
            src_ref=src,
            dst_ref=dst,
            send_sem=self.net.ssem.at[send],
            recv_sem=self.net.rsem.at[recv],
            device_id=device,
            device_id_type=MESH,
        )

    def inwards(self, i):
        own, outer, out, ready, (up, down, _, _) = self.chunks[i]
        if ready is not None:
            ready()

        @pl.when(jnp.logical_not(self.edge))
        def _():
            self.copy(own, outer, up, up, self.outer).wait_recv()
            own[...] = (own[...].astype(F32) + outer[...].astype(F32)).astype(BF)

        @pl.when(self.middle)
        def _():
            self.copy(own, out(self.net.c), down, down, self.inner).start()

        @pl.when(jnp.logical_not(self.middle))
        def _():
            self.copy(own, outer, up, up, self.inner).start()

    def outwards(self, i):
        own, outer, out, _, (up, down, away, mate) = self.chunks[i]
        place = out(self.net.c)
        self.copy(own, place, down, down, self.inner).wait_recv()

        @pl.when(self.middle)
        def _():
            place[...] = (own[...].astype(F32) + place[...].astype(F32)).astype(BF)

        @pl.when(jnp.logical_not(self.edge))
        def _():
            self.copy(place, place, away, down, self.outer).start()

        self.copy(place, place, mate, mate, self.net.mate).start()

    def finish(self):
        for own, outer, out, _, (up, down, away, mate) in self.chunks:
            place, other = out(self.net.c), out(1 - self.net.c)
            self.copy(own, place, jnp.where(self.middle, down, up), down, self.inner).wait_send()

            @pl.when(jnp.logical_not(self.edge))
            def _():
                self.copy(place, place, away, down, self.outer).wait_send()

            self.copy(place, other, mate, mate, self.net.mate).wait()


def cut(size):
    if size % 32 == 0:
        return [(0, size // 2), (size // 2, size // 2)]
    return [(0, size)]


def back_kernel(
    n,
    chips,
    gb,
    gmid,
    x,
    qkv,
    lse,
    att,
    nrm,
    wqkv,
    wo,
    flag_ref,
    cos_ref,
    sin_ref,
    rg,
    g1_all,
    base_out,
    sb1,
    grad_gate,
    grad_up,
    grad_down,
    layer_out,
    input_grad,
    first_grad,
    sum_gate,
    sum_up,
    sum_down,
    sum_qkv,
    sum_out,
    gb_all,
    dk,
    dv,
    dqkv,
    vg,
    sb,
    rb,
    own,
    rb1,
    grad_qkv,
    grad_out,
    m_gate,
    m_up,
    m_down,
    m_qkv,
    m_out,
    s_gate,
    s_up,
    s_qkv,
    a_gate,
    a_up,
    l_gate,
    l_up,
    l_down,
    l_qkv,
    l_out,
    o_gate,
    o_up,
    o_down,
    o_qkv,
    o_out,
    ssem,
    rsem,
    lsem,
):
    net = Net(n, ssem, rsem, lsem)
    line = Line(net, chips)
    size, width = gb.shape
    length = n * size
    cols = width // n
    heads = cols // HD
    half, hidden = m_gate.shape[1:]
    flag = flag_ref[0]
    line.barrier([net.peer(k) for k in range(1, n)] + [net.mate])
    gather = Gather(net, gb, gb_all, size)
    local = net.local(gb, rows_of(gb_all, net.f, size))
    mate_down = net.push(grad_down.at[1 - net.c], m_down, net.mate)
    mate_gate = net.push(grad_gate.at[:, 1 - net.c], m_gate, net.mate)
    mate_up = net.push(grad_up.at[:, 1 - net.c], m_up, net.mate)
    dk[...] = jnp.zeros_like(dk)
    dv[...] = jnp.zeros_like(dv)
    local.wait()
    mate_down.wait_recv()
    l_down[...] = (grad_down[net.c].astype(F32) + m_down[...].astype(F32)).astype(BF)
    for start, count in cut(l_down.shape[0]):
        at = pl.ds(start, count)
        line.chunk(l_down.at[at], o_down.at[at], lambda c, at=at: sum_down.at[c, at])
    downs = len(line.chunks)

    def edge_first(i):
        @pl.when(line.edge)
        def _():
            line.inwards(i)

    def rest_first(i):
        @pl.when(jnp.logical_not(line.edge))
        def _():
            line.inwards(i)

    for i in range(downs):
        edge_first(i)
    for mate, grad, m, s in ((mate_gate, grad_gate, m_gate, s_gate), (mate_up, grad_up, m_up, s_up)):
        mate.wait_recv()
        for r in range(n):
            s[r] = (grad[r, net.c].astype(F32) + m[r].astype(F32)).astype(BF)
    for k in range(1, n):
        if k < 3 or n != 4:
            gather.wait(k)
    for s, a, l, o, total in ((s_gate, a_gate, l_gate, o_gate, sum_gate), (s_up, a_up, l_up, o_up, sum_up)):
        for start, count in cut(half):
            at = pl.ds(start, count)
            copies = []
            for k in range(1, n):
                device = net.peer(k)
                copies.append(net.push(s.at[device[1], at], a.at[net.f, at], device))

            def ready(copies=copies, s=s, a=a, l=l, start=start, count=count):
                rows = slice(start, start + count)
                a[net.f, rows] = s[net.f, rows]
                for copy in copies:
                    copy.wait_recv()
                for r in range(n):
                    l[rows, r * hidden : (r + 1) * hidden] = a[r, rows]

            line.chunk(l.at[at], o.at[at], lambda c, at=at, total=total: total.at[c, at], ready)
    gates = len(line.chunks)
    if n == 4:
        gather.wait(3)

    base = net.take(n)
    value_base = net.take(n)

    def attend(r):
        at = slice(r * size, (r + 1) * size)
        query = qkv[at, :cols]
        grad = dot_nt(gb_all[at], wo[...]).astype(BF)
        stats = lse[at]
        total = jnp.zeros((size, cols), F32)
        biases = [block_bias(flag, r, kb, size, length) for kb in range(r + 1)]
        for h in range(heads):
            mask = lane_mask(cols, h)
            qm = jnp.where(mask, query, jnp.zeros_like(query))
            gm = jnp.where(mask, grad, jnp.zeros_like(grad))
            probs, grads = [], []
            inner = None
            for kb in range(r + 1):
                there = slice(kb * size, (kb + 1) * size)
                tile = scores_of(qm, qkv[there, cols : 2 * cols], biases[kb])
                prob = jnp.exp(tile - stats[:, h : h + 1])
                gprob = dot_nt(gm, qkv[there, 2 * cols :])
                part = (prob * gprob).sum(axis=1, keepdims=True)
                inner = part if inner is None else inner + part
                probs.append(prob)
                grads.append(gprob)
            mixed = None
            for kb in range(r + 1):
                there = slice(kb * size, (kb + 1) * size)
                low = (probs[kb] * (grads[kb] - inner)).astype(BF)
                term = dot_nn(low, qkv[there, cols : 2 * cols])
                mixed = term if mixed is None else mixed + term
                dk[there] += dot_tn(low, qm)
                dv[there] += dot_tn(probs[kb].astype(BF), gm)
            total = jnp.where(mask, mixed, total)
        cos, sin = table_rows(net, cos_ref, sin_ref, flag, r * size, size, length, cols)
        dqkv[at, :cols] = turn(total * HD**-0.5, cos, -sin).astype(BF)
        dqkv[at, cols : 2 * cols] = turn(dk[at], cos, -sin).astype(BF)
        dqkv[at, 2 * cols :] = (0.5 * dv[at]).astype(BF)
        part = dot_nt(dqkv[at], wqkv[...])
        sb[r] = part.astype(BF)
        place = vg.at[:, pl.ds(pl.multiple_of(net.f * cols, cols), cols)]

        @pl.when(net.f == r)
        def _():
            own[...] = part
            vg[:, pl.ds(pl.multiple_of(net.f * cols, cols), cols)] = dqkv[at, 2 * cols :]

        @pl.when(net.f != r)
        def _():
            send_to(net, r, sb.at[r], rb.at[net.f], base).start()
            piece = dqkv.at[pl.ds(r * size, size), pl.ds(2 * cols, cols)]
            send_to(net, r, piece, place, value_base).start()

    for i in range(downs):
        rest_first(i)
    attend(n - 1)
    grad_out[...] = dot_tn(att[...], gb_all[...]).astype(BF).reshape(grad_out.shape)
    mate_out = net.push(grad_out.at[1 - net.c], m_out, net.mate)
    up, out = downs, 0

    def step_up():
        nonlocal up
        if up < gates:
            line.inwards(up)
            up += 1

    def step_out():
        nonlocal out
        if out < up - 1:
            @pl.when(jnp.logical_not(line.edge))
            def _(out=out):
                line.outwards(out)
            out += 1

    step_up()
    for r in reversed(range(n - 1)):
        attend(r)
        step_out()
        if r % 2 == 1:
            step_out()
        step_up()
    tile = 256 if width % 256 == 0 else width

    @pl.loop(0, width // tile)
    def _(i):
        at = pl.ds(pl.multiple_of(i * tile, tile), tile)
        grad = dot_tn(nrm[:, at], dqkv[...]).astype(BF)
        for j in range(3):
            grad_qkv[j, at] = grad[:, j * cols : (j + 1) * cols]

    mate_qkv = []
    for j in range(3):
        mate_qkv.append([])
        for r in range(n):
            rows = pl.ds(pl.multiple_of(2 * half * r + half * (1 - net.c), half), half)
            mate_qkv[j].append(net.push(grad_qkv.at[j, rows], m_qkv.at[j, r], net.mate))
    mate_out.wait_recv()
    l_out[...] = (grad_out[net.c].astype(F32) + m_out[...].astype(F32)).astype(BF)
    for j in range(3):
        copies = []
        for r in range(n):
            mate_qkv[j][r].wait_recv()
            rows = pl.ds(pl.multiple_of(2 * half * r + half * net.c, half), half)
            s_qkv[j, r] = (grad_qkv[j, rows].astype(F32) + m_qkv[j, r].astype(F32)).astype(BF)
        place = pl.ds(pl.multiple_of(net.f * cols, cols), cols)
        for k in range(1, n):
            device = net.peer(k)
            copies.append(net.push(s_qkv.at[j, device[1]], l_qkv.at[j, :, place], device))
        l_qkv[j, :, place] = s_qkv[j, net.f]

        def ready(copies=copies):
            for copy in copies:
                copy.wait_recv()

        if j == 0:
            line.chunk(l_out, o_out, lambda c: sum_out.at[c])
        line.chunk(l_qkv.at[j], o_qkv.at[j], lambda c, j=j: sum_qkv.at[j, c], ready)
    late = [(k, net.push(sb1.at[k], rb1.at[k], net.peer(k))) for k in range(1, n)]
    gates = len(line.chunks)
    while up < gates:
        step_up()
        step_out()

    total = own[...]
    for k in range(1, n):
        other = flip(net.f, k, n)
        send_to(net, other, sb.at[other], rb.at[other], base, other).wait()
        total = total + rb[other].astype(F32)
    input_grad[...] = gmid[...] + norm_back(x[...].astype(F32), g1_all[0:1, :].astype(F32), total)
    up += 1
    while out < len(line.chunks):
        step_out()
    for k in range(1, n):
        other = flip(net.f, k, n)
        place = vg.at[:, pl.ds(pl.multiple_of(other * cols, cols), cols)]
        piece = dqkv.at[pl.ds(pl.multiple_of(other * size, size), size), pl.ds(2 * cols, cols)]
        send_to(net, other, piece, place, value_base, other).wait()
    first_grad[...] = rg[...] + vg[...].astype(F32)
    result = base_out[...]
    for k, copy in late:
        copy.wait_recv()
        result = result + rb1[k].astype(F32)
    layer_out[...] = result.astype(BF)
    for i in range(len(line.chunks)):
        @pl.when(line.edge)
        def _(i=i):
            line.outwards(i)
    line.finish()
    net.drain()


def rope_table(length, lanes):
    half = HD // 2
    frequency = np.float32(10000.0) ** (-np.arange(half, dtype=np.float32) / np.float32(half))
    angle = np.arange(length, dtype=np.float32)[:, None] * frequency[None, :].astype(np.float32)
    angle = angle.astype(np.float64)
    cos, sin = np.cos(angle), np.sin(angle)
    cos = np.tile(np.concatenate([cos, cos], axis=1), (1, lanes // HD))
    sin = np.tile(np.concatenate([-sin, sin], axis=1), (1, lanes // HD))
    return cos.astype(np.float32), sin.astype(np.float32)


def call(kernel, name, ident, outs, scratch, args, smem=(), dmas=(64, 8), limit=LIMIT):
    vmem, smem_spec = pl.BlockSpec(memory_space=pltpu.VMEM), pl.BlockSpec(memory_space=pltpu.SMEM)
    return pl.pallas_call(
        kernel,
        out_shape=[jax.ShapeDtypeStruct(shape, dtype) for shape, dtype in outs],
        in_specs=[smem_spec if i in smem else vmem for i in range(len(args))],
        out_specs=[vmem] * len(outs),
        scratch_shapes=[pltpu.VMEM(shape, dtype) for shape, dtype in scratch]
        + [
            pltpu.SemaphoreType.DMA((dmas[0],)),
            pltpu.SemaphoreType.DMA((dmas[0],)),
            pltpu.SemaphoreType.DMA((dmas[1],)),
        ],
        compiler_params=pltpu.CompilerParams(
            collective_id=ident, has_side_effects=True, vmem_limit_bytes=limit
        ),
        name=name,
    )(*args)


def body(
    tokens,
    value_first,
    window_split,
    cotangent,
    running_grad,
    gain_attn,
    w_query,
    w_key,
    w_value,
    w_out,
    gain_mlp,
    w_gate,
    w_up,
    w_down,
):
    n, copies = lax.axis_size("fsdp"), lax.axis_size("dp")
    size, width = tokens.shape
    length, cols = n * size, width // n
    rows = w_query.shape[0]
    half = rows // 2
    hidden = w_down.shape[0]
    cos, sin = (jnp.asarray(t) for t in rope_table(length, 128))
    qkv, lse, att, nrm, mid, nm, wqkv, wgc, wuc, g1_all, g2_all = call(
        functools.partial(front_kernel, n),
        "front",
        1,
        [
            ((length, 3 * cols), BF),
            ((length, 128), F32),
            ((length, cols), BF),
            ((length, width), BF),
            ((size, width), F32),
            ((size, width), BF),
            ((width, 3 * cols), BF),
            ((width, hidden), BF),
            ((width, hidden), BF),
            ((16, width), BF),
            ((16, width), BF),
        ],
        [
            ((length, width), BF),
            ((length, cols), BF),
            ((n, size, width), BF),
            ((n, size, width), BF),
            ((size, width), F32),
            ((n, rows, hidden), BF),
            ((n, rows, hidden), BF),
        ],
        (
            tokens,
            value_first,
            w_query,
            w_key,
            w_value,
            w_out,
            gain_attn[None, :],
            gain_mlp[None, :],
            window_split,
            cos,
            sin,
            w_gate,
            w_up,
        ),
        smem=(8,),
        dmas=(96, 8),
    )
    gmid, gb, base_out, sb1, grad_gate, grad_up, grad_down = call(
        functools.partial(middle_kernel, n),
        "middle",
        2,
        [
            ((size, width), F32),
            ((size, width), BF),
            ((size, width), F32),
            ((n, size, width), BF),
            ((width, hidden), BF),
            ((width, hidden), BF),
            ((hidden, width), BF),
        ],
        [
            ((length, width), BF),
            ((length, width), BF),
            ((length, hidden), BF),
            ((length, hidden), BF),
            ((length, hidden), BF),
            ((length, hidden), F32),
            ((length, hidden), F32),
            ((n, size, width), BF),
            ((n, size, width), BF),
            ((size, width), F32),
        ],
        (nm, mid, cotangent, wgc, wuc, w_down, g2_all),
        dmas=(48, 8),
    )
    pieces, third = (n, half, hidden), (3, n, half, cols)
    lines = [(half, n * hidden), (half, n * hidden), (hidden // 2, width), (3, half, width), (cols // 2, width)]
    layer_out, input_grad, first_grad, sum_gate, sum_up, sum_down, sum_qkv, sum_out = call(
        functools.partial(back_kernel, n, copies // 2),
        "back",
        3,
        [
            ((size, width), BF),
            ((size, width), F32),
            ((size, width), F32),
            ((2, half, n * hidden), BF),
            ((2, half, n * hidden), BF),
            ((2, hidden // 2, width), BF),
            ((3, 2, half, width), BF),
            ((2, cols // 2, width), BF),
        ],
        [
            ((length, width), BF),
            ((length, cols), F32),
            ((length, cols), F32),
            ((length, 3 * cols), BF),
            ((size, width), BF),
            ((n, size, width), BF),
            ((n, size, width), BF),
            ((size, width), F32),
            ((n, size, width), BF),
            ((3, width, cols), BF),
            ((2, cols // 2, width), BF),
            (pieces, BF),
            (pieces, BF),
            (lines[2], BF),
            (third, BF),
            (lines[4], BF),
            (pieces, BF),
            (pieces, BF),
            (third, BF),
            (pieces, BF),
            (pieces, BF),
        ]
        + [(shape, BF) for shape in lines * 2],
        (
            gb,
            gmid,
            tokens,
            qkv,
            lse,
            att,
            nrm,
            wqkv,
            w_out,
            window_split,
            cos,
            sin,
            running_grad,
            g1_all,
            base_out,
            sb1,
            grad_gate.reshape(n, 2, half, hidden),
            grad_up.reshape(n, 2, half, hidden),
            grad_down.reshape(2, hidden // 2, width),
        ),
        smem=(9,),
        dmas=(160, 8),
    )
    grad_query, grad_key, grad_value = (sum_qkv[j].reshape(rows, width).astype(F32) for j in range(3))
    grad_gate, grad_up = (total.reshape(rows, -1).astype(F32) for total in (sum_gate, sum_up))

    def gain_grad(gain, *pairs):
        return sum(jnp.sum(w.astype(F32) * g, axis=1) for w, g in pairs) / gain.astype(F32)

    return (
        layer_out,
        input_grad,
        first_grad,
        gain_grad(gain_attn, (w_query, grad_query), (w_key, grad_key), (w_value, grad_value)),
        grad_query,
        grad_key,
        grad_value,
        sum_out.reshape(rows, width).astype(F32),
        gain_grad(gain_mlp, (w_gate, grad_gate), (w_up, grad_up)),
        grad_gate,
        grad_up,
        sum_down.reshape(hidden, width).astype(F32),
    )


def solution(mesh):
    token, flat, matrix = P(("dp", "fsdp"), None), P("fsdp"), P("fsdp", None)
    return jax.shard_map(
        body,
        mesh=mesh,
        in_specs=(token, token, P("dp"), token, token, flat)
        + (matrix,) * 4
        + (flat,)
        + (matrix,) * 3,
        out_specs=(token, token, token, flat) + (matrix,) * 4 + (flat,) + (matrix,) * 3,
        check_vma=False,
    )
```

```python
import functools

import jax
import jax.numpy as jnp
import numpy as np
from jax import lax
from jax.experimental import pallas as pl
from jax.experimental.pallas import tpu as pltpu
from jax.sharding import PartitionSpec as P

HD = 64
EPS = 1e-06
MESH = pl.DeviceIdType.MESH
BF = jnp.bfloat16
F32 = jnp.float32
LIMIT = 60 * 1024 * 1024


def dot_nn(a, b):
    return lax.dot_general(a, b, (((1,), (0,)), ((), ())), preferred_element_type=F32)


def dot_nt(a, b):
    return lax.dot_general(a, b, (((1,), (1,)), ((), ())), preferred_element_type=F32)


def dot_tn(a, b):
    return lax.dot_general(a, b, (((0,), (0,)), ((), ())), preferred_element_type=F32)


def flip(f, k, n):
    out, bit = 0, 1
    while bit < n:
        have, want = lax.rem(f // bit, 2), (k // bit) % 2
        out = out + (1 - have if want else have) * bit
        bit *= 2
    return out


class Net:
    def __init__(self, n, ssem, rsem, lsem=None):
        self.n, self.ssem, self.rsem, self.lsem = n, ssem, rsem, lsem
        self.d, self.f = lax.axis_index("dp"), lax.axis_index("fsdp")
        self.c = lax.rem(self.d, 2)
        self.mate = (self.d + 1 - 2 * self.c, self.f)
        self.used, self.lused, self.sent = 0, 0, []

    def peer(self, k):
        return (self.d, flip(self.f, k, self.n))

    def take(self, count=1):
        self.used += count
        return self.used - count

    def push(self, src, dst, device, slot=None):
        slot = self.take() if slot is None else slot
        copy = pltpu.make_async_remote_copy(
            src_ref=src,
            dst_ref=dst,
            send_sem=self.ssem.at[slot],
            recv_sem=self.rsem.at[slot],
            device_id=device,
            device_id_type=MESH,
        )
        copy.start()
        self.sent.append(copy)
        return copy

    def local(self, src, dst):
        copy = pltpu.make_async_copy(src, dst, self.lsem.at[self.lused])
        self.lused += 1
        copy.start()
        return copy

    def barrier(self, devices):
        sem = pltpu.get_barrier_semaphore()
        for device in devices:
            pl.semaphore_signal(sem, inc=1, device_id=device, device_id_type=MESH)
        pl.semaphore_wait(sem, len(devices))

    def drain(self):
        for copy in self.sent:
            copy.wait_send()


def rows_of(ref, block, size):
    return ref.at[pl.ds(pl.multiple_of(block * size, size), size)]


class Gather:
    def __init__(self, net, own, into, size):
        self.net, self.into, self.size = net, into, size
        self.direct = [1, 2] if net.n == 4 else list(range(1, net.n))
        self.copies = {k: net.push(own, rows_of(into, net.f, size), net.peer(k)) for k in self.direct}
        self.halves = {}

    def part(self, block, half):
        start = pl.multiple_of(block * self.size + half * (self.size // 2), self.size // 2)
        return self.into.at[pl.ds(start, self.size // 2)]

    def wait(self, k):
        net = self.net
        if k in self.copies:
            self.copies[k].wait_recv()
            if net.n == 4:
                part = self.part(flip(net.f, k, 4), k - 1)
                self.halves[k] = net.push(part, part, net.peer(3 - k))
        else:
            for copy in self.halves.values():
                copy.wait_recv()


def lane_mask(width, head):
    lane = lax.broadcasted_iota(jnp.int32, (1, width), 1)
    return (lane // HD) == head


def turn(values, cos, sin):
    width = values.shape[1]
    lane = lax.broadcasted_iota(jnp.int32, (1, width), 1)
    first = lax.rem(lane, HD) < HD // 2
    other = jnp.where(
        first, pltpu.roll(values, width - HD // 2, 1), pltpu.roll(values, HD // 2, 1)
    )
    return values * cos + other * sin


def table_rows(net, cos_ref, sin_ref, flag, start, size, length, width):
    half = length // 2
    plain = pl.ds(pl.multiple_of(start, size), size)
    split = pl.ds(pl.multiple_of(lax.rem(start, half), size), size)
    out = []
    for ref in (cos_ref, sin_ref):
        rows = jnp.where(flag == 1, ref[split], ref[plain])
        out.append(jnp.concatenate([rows] * (width // rows.shape[1]), axis=1))
    return out


def block_bias(flag, r, kb, size, length):
    half = length // 2
    if kb == r:
        row = lax.broadcasted_iota(jnp.int32, (size, size), 0)
        col = lax.broadcasted_iota(jnp.int32, (size, size), 1)
        return jnp.where(col <= row, 0.0, -1e30)
    if (r * size >= half) != (kb * size >= half):
        return jnp.where(flag == 1, -1e30, 0.0)
    return None


def scores_of(query, key, bias):
    scores = dot_nt(query, key)
    return scores if bias is None else scores + bias


def factor_of(hidden):
    return lax.rsqrt(jnp.mean(hidden * hidden, axis=-1, keepdims=True) + EPS)


def norm_back(hidden, gain, grad):
    factor = factor_of(hidden)
    scaled = grad * gain
    return factor * scaled - hidden * (factor * factor * factor) * jnp.mean(
        scaled * hidden, axis=-1, keepdims=True
    )


class Spread:
    def __init__(self, net, chips, rows, sources):
        self.net, self.rows = net, rows
        self.chip = net.d // 2
        self.chips = chips if rows % (32 * chips) == 0 else 1
        self.share = rows // (2 * self.chips)
        self.part = self.chip if self.chips > 1 else 0
        n = net.n
        self.right, self.left, self.mate = (net.take(self.chips * (n - 1)) for _ in range(3))
        self.into = sources[0][2]
        self.first = []
        for k in range(1, n):
            to = net.peer(k)
            for piece, place, _ in sources:
                mine = pl.ds(self.start(0, self.part, net.c), self.share)
                here = pl.ds(self.start(net.f, self.part, net.c), self.share)
                self.first.append(net.push(piece(to[1]).at[mine], place.at[here], to))

    def start(self, block, part, core):
        return pl.multiple_of(block * self.rows + (2 * part + core) * self.share, self.share)

    def view(self, k, part, core):
        return self.into.at[pl.ds(self.start(flip(self.net.f, k, self.net.n), part, core), self.share)]

    def copy(self, k, part, base, device):
        net = self.net
        slot = base + part * (net.n - 1) + k - 1
        view = self.view(k, part, net.c)
        return pltpu.make_async_remote_copy(
            src_ref=view,
            dst_ref=view,
            send_sem=net.ssem.at[slot],
            recv_sem=net.rsem.at[slot],
            device_id=device,
            device_id_type=MESH,
        )

    def along(self, step):
        return ((self.chip + step) * 2 + self.net.c, self.net.f)

    def pass_on(self, part, base, step, room):
        @pl.when(room)
        def _():
            for k in range(1, self.net.n):
                self.copy(k, part, base, self.along(step)).start()

    def own(self):
        for copy in self.first:
            copy.wait_recv()
        if self.chips > 1:
            self.pass_on(self.part, self.right, 1, self.chip + 1 < self.chips)
            self.pass_on(self.part, self.left, -1, self.chip > 0)
        for k in range(1, self.net.n):
            self.copy(k, self.part, self.mate, self.net.mate).start()

    def hop(self, j):
        if j >= self.chips:
            return
        for base, step in ((self.right, 1), (self.left, -1)):
            part = self.part - step * j

            @pl.when((part >= 0) & (part < self.chips))
            def _(base=base, step=step, part=part):
                for k in range(1, self.net.n):
                    self.copy(k, part, base, self.net.mate).wait_recv()
                room = self.chip + 1 < self.chips if step == 1 else self.chip > 0
                self.pass_on(part, base, step, room)
                for k in range(1, self.net.n):
                    self.copy(k, part, self.mate, self.net.mate).start()

    def finish(self):
        n = self.net.n
        for part in range(self.chips):
            for k in range(1, n):
                self.copy(k, part, self.mate, self.net.mate).wait()
            if self.chips > 1:

                @pl.when((part <= self.chip) & (self.chip + 1 < self.chips))
                def _(part=part):
                    for k in range(1, n):
                        self.copy(k, part, self.right, self.net.mate).wait_send()

                @pl.when((part >= self.chip) & (self.chip > 0))
                def _(part=part):
                    for k in range(1, n):
                        self.copy(k, part, self.left, self.net.mate).wait_send()


def gain_rows(net, src, dst, rows):
    place = dst.at[:, pl.ds(pl.multiple_of(net.f * rows, rows), rows)]
    dst[:, pl.ds(pl.multiple_of(net.f * rows, rows), rows)] = jnp.broadcast_to(src[...].reshape(1, rows), (16, rows))
    return [net.push(place, place, net.peer(k)) for k in range(1, net.n)]


def send_to(net, r, src, dst, base, away=None):
    return pltpu.make_async_remote_copy(
        src_ref=src,
        dst_ref=dst,
        send_sem=net.ssem.at[base + r],
        recv_sem=net.rsem.at[base + (net.f if away is None else away)],
        device_id=(net.d, r),
        device_id_type=MESH,
    )


def front_kernel(
    n,
    chips,
    x,
    vf,
    wq,
    wk,
    wv,
    wo,
    g1,
    g2,
    flag_ref,
    cos_ref,
    sin_ref,
    wg,
    wu,
    ct,
    qkv,
    lse,
    att,
    nrm,
    mid,
    nm,
    wqkv,
    wgc,
    wuc,
    g1_all,
    g2_all,
    g_all,
    x_all,
    vfc,
    wo_all,
    att_own,
    wgr,
    wur,
    ssem,
    rsem,
    lsem,
):
    net = Net(n, ssem, rsem, lsem)
    size, width = x.shape
    length = n * size
    cols = width // n
    rows = wq.shape[0]
    hidden = wgc.shape[1]
    flag = flag_ref[0]
    chip = net.d // 2
    sem = pltpu.get_barrier_semaphore()
    near = [net.peer(k) for k in range(1, n)] + [net.mate]
    for device in near:
        pl.semaphore_signal(sem, inc=1, device_id=device, device_id_type=MESH)
    for step, room in ((1, chip + 1 < chips), (-1, chip > 0)):
        @pl.when(room)
        def _(step=step):
            device = ((chip + step) * 2 + net.c, net.f)
            pl.semaphore_signal(sem, inc=1, device_id=device, device_id_type=MESH)

    edge = (chip == 0) | (chip == chips - 1)

    @pl.when(edge)
    def _():
        pl.semaphore_wait(sem, len(near) + min(chips - 1, 1))

    @pl.when(jnp.logical_not(edge))
    def _():
        pl.semaphore_wait(sem, len(near) + 2)

    mine = pl.ds(pl.multiple_of(net.f * cols, cols), cols)
    sources = []
    for i, w in enumerate((wq, wk, wv)):
        piece = lambda to, w=w: w.at[:, pl.ds(pl.multiple_of(to * cols, cols), cols)]
        sources.append((piece, wqkv.at[:, pl.ds(i * cols, cols)], wqkv))
    spread_qkv = Spread(net, chips, rows, sources)
    gains = gain_rows(net, g1, g1_all, rows) + gain_rows(net, g2, g2_all, rows)
    x_gather = Gather(net, x, x_all, size)
    values = []
    for k in range(1, n):
        device = net.peer(k)
        src = vf.at[:, pl.ds(pl.multiple_of(device[1] * cols, cols), cols)]
        values.append(net.push(src, rows_of(vfc, net.f, size), device))
    locals_ = [net.local(x, rows_of(x_all, net.f, size))]
    locals_.append(net.local(vf.at[:, mine], rows_of(vfc, net.f, size)))
    for i, w in enumerate((wq, wk, wv)):
        into = rows_of(wqkv.at[:, pl.ds(i * cols, cols)], net.f, rows)
        locals_.append(net.local(w.at[:, mine], into))
    locals_.append(net.local(wo, rows_of(wo_all, net.f, rows)))
    locals_.append(net.local(ct, rows_of(g_all, net.f, size)))
    for copy in gains:
        copy.wait_recv()
    spread_qkv.own()
    for w, piece, into in ((wg, wgr, wgc), (wu, wur, wuc)):
        for r in range(n):
            piece[r] = w[:, r * hidden : (r + 1) * hidden]
        into[pl.ds(pl.multiple_of(net.f * rows, rows), rows)] = piece[net.f]
    for copy in locals_:
        copy.wait()
    gain = g1_all[0:1, :].astype(F32)

    def normalize(block):
        at = pl.ds(pl.multiple_of(block * size, size), size)
        rows_in = x_all[at].astype(F32)
        nrm[at] = (rows_in * factor_of(rows_in) * gain).astype(BF)

    normalize(net.f)
    spread_qkv.hop(1)
    for k in range(1, n - 1):
        x_gather.wait(k)
        normalize(flip(net.f, k, n))
        if k == 1:
            spread_qkv.hop(2)
    spread_out = Spread(net, chips, rows, [(lambda to: wo, wo_all, wo_all)])
    spread_gate = Spread(net, chips, rows, [(lambda to: wgr.at[to], wgc, wgc)])
    spread_up = Spread(net, chips, rows, [(lambda to: wur.at[to], wuc, wuc)])
    for j in range(3, chips):
        spread_qkv.hop(j)
    x_gather.wait(n - 1)
    normalize(flip(net.f, n - 1, n))
    g_gather = Gather(net, ct, g_all, size)
    spreads = [spread_out, spread_gate, spread_up]
    for spread in spreads:
        spread.own()
    spread_qkv.finish()
    for copy in values:
        copy.wait_recv()

    @pl.loop(0, n)
    def _(block):
        at = pl.ds(pl.multiple_of(block * size, size), size)
        pre = dot_nn(nrm[at], wqkv[...])
        cos, sin = table_rows(net, cos_ref, sin_ref, flag, block * size, size, length, 2 * cols)
        turned = turn(pre[:, : 2 * cols], cos, sin)
        mixed = 0.5 * pre[:, 2 * cols :] + 0.5 * vfc[at].astype(F32)
        qkv[at, :cols] = (turned[:, :cols] * HD**-0.5).astype(BF)
        qkv[at, cols : 2 * cols] = turned[:, cols:].astype(BF)
        qkv[at, 2 * cols :] = mixed.astype(BF)

    heads = cols // HD
    base = net.take(n)
    lane = lax.broadcasted_iota(jnp.int32, (1, 128), 1)
    hops = 1
    for r in range(n):
        at = slice(r * size, (r + 1) * size)
        query = qkv[at, :cols]
        total = jnp.zeros((size, cols), F32)
        stats = jnp.zeros((size, 128), F32)
        biases = [block_bias(flag, r, kb, size, length) for kb in range(r + 1)]
        for h in range(heads):
            mask = lane_mask(cols, h)
            masked = jnp.where(mask, query, jnp.zeros_like(query))
            tiles = [
                scores_of(masked, qkv[kb * size : (kb + 1) * size, cols : 2 * cols], biases[kb])
                for kb in range(r + 1)
            ]
            top = tiles[0].max(axis=1, keepdims=True)
            for tile in tiles[1:]:
                top = jnp.maximum(top, tile.max(axis=1, keepdims=True))
            raw = [jnp.exp(tile - top) for tile in tiles]
            whole = raw[0].sum(axis=1, keepdims=True)
            for tile in raw[1:]:
                whole = whole + tile.sum(axis=1, keepdims=True)
            inverse = 1.0 / whole
            mixed = None
            for kb, tile in enumerate(raw):
                term = dot_nn(
                    (tile * inverse).astype(BF), qkv[kb * size : (kb + 1) * size, 2 * cols :]
                )
                mixed = term if mixed is None else mixed + term
            total = jnp.where(mask, mixed, total)
            stats = jnp.where(lane == h, top + jnp.log(whole), stats)
        lse[at] = stats
        att[at] = total.astype(BF)

        @pl.when(net.f == r)
        def _():
            att_own[:, mine] = att[at]

        @pl.when(net.f != r)
        def _():
            send_to(net, r, att.at[pl.ds(r * size, size)], att_own.at[:, mine], base).start()

        if r == n // 2 - 1 or r == n - 1:
            g_gather.wait(1 if r < n - 1 else 2)
        if r and hops < chips:
            for spread in spreads:
                spread.hop(hops)
            hops += 1
    for j in range(hops, chips):
        for spread in spreads:
            spread.hop(j)
    spread_out.finish()
    for k in range(1, n):
        other = flip(net.f, k, n)
        place = att_own.at[:, pl.ds(pl.multiple_of(other * cols, cols), cols)]
        src = rows_of(att, other, size)
        send_to(net, other, src, place, base, other).wait()
    sums = x[...].astype(F32) + dot_nn(att_own[...], wo_all[...])
    mid[...] = sums
    nm[...] = (sums * factor_of(sums) * g2_all[0:1, :].astype(F32)).astype(BF)
    for spread in spreads[1:]:
        spread.finish()
    for k in range(3, n):
        g_gather.wait(k)
    net.drain()


def middle_kernel(
    n,
    nm,
    mid,
    g_all,
    wgc,
    wuc,
    wd,
    g2_all,
    gmid,
    gb,
    base_out,
    sb1,
    grad_gate,
    grad_up,
    grad_down,
    nm_all,
    hid_all,
    gg_all,
    ug_all,
    coef,
    silus,
    sb2,
    rb2,
    own2,
    ssem,
    rsem,
    lsem,
):
    net = Net(n, ssem, rsem, lsem)
    size, width = nm.shape
    net.barrier([net.peer(k) for k in range(1, n)])
    gather = Gather(net, nm, nm_all, size)
    local = net.local(nm, rows_of(nm_all, net.f, size))

    def rows_at(k):
        return pl.ds(pl.multiple_of(flip(net.f, k, n) * size, size), size)

    def forward(k):
        at = rows_at(k)
        a = nm_all[at]
        gate = dot_nn(a, wgc[...])
        up = dot_nn(a, wuc[...])
        sig = jax.nn.sigmoid(gate)
        silu = gate * sig
        hid_all[at] = (silu * up).astype(BF)
        coef[at] = up * sig * (1.0 + gate * (1.0 - sig))
        silus[at] = silu
        part = dot_nn(hid_all[at], wd[...])
        if k == 0:
            base_out[...] = mid[...] + part
        else:
            sb1[k] = part.astype(BF)

    soon = []

    def backward(k):
        at = rows_at(k)
        grad = dot_nt(g_all[at], wd[...])
        gg_all[at] = (grad * coef[at]).astype(BF)
        ug_all[at] = (grad * silus[at]).astype(BF)
        back = dot_nt(gg_all[at], wgc[...]) + dot_nt(ug_all[at], wuc[...])
        if k == 0:
            own2[...] = back
        else:
            sb2[k] = back.astype(BF)
            soon.append((k, net.push(sb2.at[k], rb2.at[k], net.peer(k))))

    sb1[0] = jnp.zeros(sb1.shape[1:], BF)
    local.wait()
    forward(0)
    backward(0)
    for k in range(1, n):
        gather.wait(k)
        for j in ([1] if k == 2 or n == 2 else []) + ([k] if k >= 2 else []):
            forward(j)
            backward(j)
    tile = 256 if width % 256 == 0 else width

    @pl.loop(0, width // tile)
    def _(i):
        at = pl.ds(pl.multiple_of(i * tile, tile), tile)
        lhs = nm_all[:, at]
        grad_gate[at] = dot_tn(lhs, gg_all[...]).astype(BF)
        grad_up[at] = dot_tn(lhs, ug_all[...]).astype(BF)
        grad_down[:, at] = dot_tn(hid_all[...], g_all[:, at]).astype(BF)

    grad = own2[...]
    for k, copy in soon:
        copy.wait_recv()
        grad = grad + rb2[k].astype(F32)
    total = g_all[rows_at(0)].astype(F32) + norm_back(mid[...], g2_all[0:1, :].astype(F32), grad)
    gmid[...] = total
    gb[...] = total.astype(BF)
    net.drain()


class Line:
    def __init__(self, net, chips):
        chip, middle = net.d // 2, chips // 2
        left = chip < middle
        inward = jnp.where(left, chip + 1, chip - 1)
        outward = jnp.where(left, chip - 1, chip + 1)
        self.net = net
        self.edge = (chip == 0) | (chip == chips - 1)
        self.middle = (chip == middle - 1) | (chip == middle)
        self.inner = (inward * 2 + net.c, net.f)
        self.outer = (outward * 2 + net.c, net.f)
        self.chunks = []

    def barrier(self, others):
        net, sem = self.net, pltpu.get_barrier_semaphore()
        fixed = others + [self.inner]
        for device in fixed:
            pl.semaphore_signal(sem, inc=1, device_id=device, device_id_type=MESH)

        @pl.when(jnp.logical_not(self.edge))
        def _():
            pl.semaphore_signal(sem, inc=1, device_id=self.outer, device_id_type=MESH)
            pl.semaphore_wait(sem, len(fixed) + 1)

        @pl.when(self.edge)
        def _():
            pl.semaphore_wait(sem, len(fixed))

    def chunk(self, own, outer, out, ready=None):
        slots = [self.net.take() for _ in range(4)]
        self.chunks.append((own, outer, out, ready, slots))

    def copy(self, src, dst, send, recv, device):
        return pltpu.make_async_remote_copy(
            src_ref=src,
            dst_ref=dst,
            send_sem=self.net.ssem.at[send],
            recv_sem=self.net.rsem.at[recv],
            device_id=device,
            device_id_type=MESH,
        )

    def inwards(self, i):
        own, outer, out, ready, (up, down, _, _) = self.chunks[i]
        if ready is not None:
            ready()

        @pl.when(jnp.logical_not(self.edge))
        def _():
            self.copy(own, outer, up, up, self.outer).wait_recv()
            own[...] = (own[...].astype(F32) + outer[...].astype(F32)).astype(BF)

        @pl.when(self.middle)
        def _():
            self.copy(own, out(self.net.c), down, down, self.inner).start()

        @pl.when(jnp.logical_not(self.middle))
        def _():
            self.copy(own, outer, up, up, self.inner).start()

    def outwards(self, i):
        own, outer, out, _, (up, down, away, mate) = self.chunks[i]
        place = out(self.net.c)
        self.copy(own, place, down, down, self.inner).wait_recv()

        @pl.when(self.middle)
        def _():
            place[...] = (own[...].astype(F32) + place[...].astype(F32)).astype(BF)

        @pl.when(jnp.logical_not(self.edge))
        def _():
            self.copy(place, place, away, down, self.outer).start()

        self.copy(place, place, mate, mate, self.net.mate).start()

    def finish(self):
        for own, outer, out, _, (up, down, away, mate) in self.chunks:
            place, other = out(self.net.c), out(1 - self.net.c)
            self.copy(own, place, jnp.where(self.middle, down, up), down, self.inner).wait_send()

            @pl.when(jnp.logical_not(self.edge))
            def _():
                self.copy(place, place, away, down, self.outer).wait_send()

            self.copy(place, other, mate, mate, self.net.mate).wait()


def cut(size):
    if size % 32 == 0:
        return [(0, size // 2), (size // 2, size // 2)]
    return [(0, size)]


def back_kernel(
    n,
    chips,
    gb,
    gmid,
    x,
    qkv,
    lse,
    att,
    nrm,
    wqkv,
    wo,
    flag_ref,
    cos_ref,
    sin_ref,
    rg,
    g1_all,
    base_out,
    sb1,
    grad_gate,
    grad_up,
    grad_down,
    layer_out,
    input_grad,
    first_grad,
    sum_gate,
    sum_up,
    sum_down,
    sum_qkv,
    sum_out,
    gb_all,
    dk,
    dv,
    dqkv,
    vg,
    sb,
    rb,
    own,
    rb1,
    grad_qkv,
    grad_out,
    m_gate,
    m_up,
    m_down,
    m_qkv,
    m_out,
    s_gate,
    s_up,
    s_qkv,
    a_gate,
    a_up,
    l_gate,
    l_up,
    l_down,
    l_qkv,
    l_out,
    o_gate,
    o_up,
    o_down,
    o_qkv,
    o_out,
    ssem,
    rsem,
    lsem,
):
    net = Net(n, ssem, rsem, lsem)
    line = Line(net, chips)
    size, width = gb.shape
    length = n * size
    cols = width // n
    heads = cols // HD
    half, hidden = m_gate.shape[1:]
    flag = flag_ref[0]
    line.barrier([net.peer(k) for k in range(1, n)] + [net.mate])
    gather = Gather(net, gb, gb_all, size)
    local = net.local(gb, rows_of(gb_all, net.f, size))
    mate_down = net.push(grad_down.at[1 - net.c], m_down, net.mate)
    mate_gate = net.push(grad_gate.at[:, 1 - net.c], m_gate, net.mate)
    mate_up = net.push(grad_up.at[:, 1 - net.c], m_up, net.mate)
    dk[...] = jnp.zeros_like(dk)
    dv[...] = jnp.zeros_like(dv)
    local.wait()
    mate_down.wait_recv()
    l_down[...] = (grad_down[net.c].astype(F32) + m_down[...].astype(F32)).astype(BF)
    for start, count in cut(l_down.shape[0]):
        at = pl.ds(start, count)
        line.chunk(l_down.at[at], o_down.at[at], lambda c, at=at: sum_down.at[c, at])
    downs = len(line.chunks)

    def edge_first(i):
        @pl.when(line.edge)
        def _():
            line.inwards(i)

    def rest_first(i):
        @pl.when(jnp.logical_not(line.edge))
        def _():
            line.inwards(i)

    for i in range(downs):
        edge_first(i)
    for mate, grad, m, s in ((mate_gate, grad_gate, m_gate, s_gate), (mate_up, grad_up, m_up, s_up)):
        mate.wait_recv()
        for r in range(n):
            s[r] = (grad[r, net.c].astype(F32) + m[r].astype(F32)).astype(BF)
    for k in range(1, n):
        if k < 3 or n != 4:
            gather.wait(k)
    for s, a, l, o, total in ((s_gate, a_gate, l_gate, o_gate, sum_gate), (s_up, a_up, l_up, o_up, sum_up)):
        for start, count in cut(half):
            at = pl.ds(start, count)
            copies = []
            for k in range(1, n):
                device = net.peer(k)
                copies.append(net.push(s.at[device[1], at], a.at[net.f, at], device))

            def ready(copies=copies, s=s, a=a, l=l, start=start, count=count):
                rows = slice(start, start + count)
                a[net.f, rows] = s[net.f, rows]
                for copy in copies:
                    copy.wait_recv()
                for r in range(n):
                    l[rows, r * hidden : (r + 1) * hidden] = a[r, rows]

            line.chunk(l.at[at], o.at[at], lambda c, at=at, total=total: total.at[c, at], ready)
    gates = len(line.chunks)
    if n == 4:
        gather.wait(3)

    base = net.take(n)
    value_base = net.take(n)

    def attend(r):
        at = slice(r * size, (r + 1) * size)
        query = qkv[at, :cols]
        grad = dot_nt(gb_all[at], wo[...]).astype(BF)
        stats = lse[at]
        total = jnp.zeros((size, cols), F32)
        biases = [block_bias(flag, r, kb, size, length) for kb in range(r + 1)]
        for h in range(heads):
            mask = lane_mask(cols, h)
            qm = jnp.where(mask, query, jnp.zeros_like(query))
            gm = jnp.where(mask, grad, jnp.zeros_like(grad))
            probs, grads = [], []
            inner = None
            for kb in range(r + 1):
                there = slice(kb * size, (kb + 1) * size)
                tile = scores_of(qm, qkv[there, cols : 2 * cols], biases[kb])
                prob = jnp.exp(tile - stats[:, h : h + 1])
                gprob = dot_nt(gm, qkv[there, 2 * cols :])
                part = (prob * gprob).sum(axis=1, keepdims=True)
                inner = part if inner is None else inner + part
                probs.append(prob)
                grads.append(gprob)
            mixed = None
            for kb in range(r + 1):
                there = slice(kb * size, (kb + 1) * size)
                low = (probs[kb] * (grads[kb] - inner)).astype(BF)
                term = dot_nn(low, qkv[there, cols : 2 * cols])
                mixed = term if mixed is None else mixed + term
                dk[there] += dot_tn(low, qm)
                dv[there] += dot_tn(probs[kb].astype(BF), gm)
            total = jnp.where(mask, mixed, total)
        cos, sin = table_rows(net, cos_ref, sin_ref, flag, r * size, size, length, cols)
        dqkv[at, :cols] = turn(total * HD**-0.5, cos, -sin).astype(BF)
        dqkv[at, cols : 2 * cols] = turn(dk[at], cos, -sin).astype(BF)
        dqkv[at, 2 * cols :] = (0.5 * dv[at]).astype(BF)
        part = dot_nt(dqkv[at], wqkv[...])
        sb[r] = part.astype(BF)
        place = vg.at[:, pl.ds(pl.multiple_of(net.f * cols, cols), cols)]

        @pl.when(net.f == r)
        def _():
            own[...] = part
            vg[:, pl.ds(pl.multiple_of(net.f * cols, cols), cols)] = dqkv[at, 2 * cols :]

        @pl.when(net.f != r)
        def _():
            send_to(net, r, sb.at[r], rb.at[net.f], base).start()
            piece = dqkv.at[pl.ds(r * size, size), pl.ds(2 * cols, cols)]
            send_to(net, r, piece, place, value_base).start()

    for i in range(downs):
        rest_first(i)
    attend(n - 1)
    grad_out[...] = dot_tn(att[...], gb_all[...]).astype(BF).reshape(grad_out.shape)
    mate_out = net.push(grad_out.at[1 - net.c], m_out, net.mate)
    up, out = downs, 0

    def step_up():
        nonlocal up
        if up < gates:
            line.inwards(up)
            up += 1

    def step_out():
        nonlocal out
        if out < up - 1:
            @pl.when(jnp.logical_not(line.edge))
            def _(out=out):
                line.outwards(out)
            out += 1

    step_up()
    for r in reversed(range(n - 1)):
        attend(r)
        step_out()
        if r % 2 == 1:
            step_out()
        step_up()
    tile = 256 if width % 256 == 0 else width

    @pl.loop(0, width // tile)
    def _(i):
        at = pl.ds(pl.multiple_of(i * tile, tile), tile)
        grad = dot_tn(nrm[:, at], dqkv[...]).astype(BF)
        for j in range(3):
            grad_qkv[j, at] = grad[:, j * cols : (j + 1) * cols]

    mate_qkv = []
    for j in range(3):
        mate_qkv.append([])
        for r in range(n):
            rows = pl.ds(pl.multiple_of(2 * half * r + half * (1 - net.c), half), half)
            mate_qkv[j].append(net.push(grad_qkv.at[j, rows], m_qkv.at[j, r], net.mate))
    mate_out.wait_recv()
    l_out[...] = (grad_out[net.c].astype(F32) + m_out[...].astype(F32)).astype(BF)
    for j in range(3):
        copies = []
        for r in range(n):
            mate_qkv[j][r].wait_recv()
            rows = pl.ds(pl.multiple_of(2 * half * r + half * net.c, half), half)
            s_qkv[j, r] = (grad_qkv[j, rows].astype(F32) + m_qkv[j, r].astype(F32)).astype(BF)
        place = pl.ds(pl.multiple_of(net.f * cols, cols), cols)
        for k in range(1, n):
            device = net.peer(k)
            copies.append(net.push(s_qkv.at[j, device[1]], l_qkv.at[j, :, place], device))
        l_qkv[j, :, place] = s_qkv[j, net.f]

        def ready(copies=copies):
            for copy in copies:
                copy.wait_recv()

        if j == 0:
            line.chunk(l_out, o_out, lambda c: sum_out.at[c])
        line.chunk(l_qkv.at[j], o_qkv.at[j], lambda c, j=j: sum_qkv.at[j, c], ready)
    late = [(k, net.push(sb1.at[k], rb1.at[k], net.peer(k))) for k in range(1, n)]
    gates = len(line.chunks)
    while up < gates:
        step_up()
        step_out()

    total = own[...]
    for k in range(1, n):
        other = flip(net.f, k, n)
        send_to(net, other, sb.at[other], rb.at[other], base, other).wait()
        total = total + rb[other].astype(F32)
    input_grad[...] = gmid[...] + norm_back(x[...].astype(F32), g1_all[0:1, :].astype(F32), total)
    up += 1
    while out < len(line.chunks):
        step_out()
    for k in range(1, n):
        other = flip(net.f, k, n)
        place = vg.at[:, pl.ds(pl.multiple_of(other * cols, cols), cols)]
        piece = dqkv.at[pl.ds(pl.multiple_of(other * size, size), size), pl.ds(2 * cols, cols)]
        send_to(net, other, piece, place, value_base, other).wait()
    first_grad[...] = rg[...] + vg[...].astype(F32)
    result = base_out[...]
    for k, copy in late:
        copy.wait_recv()
        result = result + rb1[k].astype(F32)
    layer_out[...] = result.astype(BF)
    for i in range(len(line.chunks)):
        @pl.when(line.edge)
        def _(i=i):
            line.outwards(i)
    line.finish()
    net.drain()


def rope_table(length, lanes):
    half = HD // 2
    frequency = np.float32(10000.0) ** (-np.arange(half, dtype=np.float32) / np.float32(half))
    angle = np.arange(length, dtype=np.float32)[:, None] * frequency[None, :].astype(np.float32)
    angle = angle.astype(np.float64)
    cos, sin = np.cos(angle), np.sin(angle)
    cos = np.tile(np.concatenate([cos, cos], axis=1), (1, lanes // HD))
    sin = np.tile(np.concatenate([-sin, sin], axis=1), (1, lanes // HD))
    return cos.astype(np.float32), sin.astype(np.float32)


def call(kernel, name, ident, outs, scratch, args, smem=(), dmas=(64, 8), limit=LIMIT):
    vmem, smem_spec = pl.BlockSpec(memory_space=pltpu.VMEM), pl.BlockSpec(memory_space=pltpu.SMEM)
    return pl.pallas_call(
        kernel,
        out_shape=[jax.ShapeDtypeStruct(shape, dtype) for shape, dtype in outs],
        in_specs=[smem_spec if i in smem else vmem for i in range(len(args))],
        out_specs=[vmem] * len(outs),
        scratch_shapes=[pltpu.VMEM(shape, dtype) for shape, dtype in scratch]
        + [
            pltpu.SemaphoreType.DMA((dmas[0],)),
            pltpu.SemaphoreType.DMA((dmas[0],)),
            pltpu.SemaphoreType.DMA((dmas[1],)),
        ],
        compiler_params=pltpu.CompilerParams(
            collective_id=ident, has_side_effects=True, vmem_limit_bytes=limit
        ),
        name=name,
    )(*args)


def body(
    tokens,
    value_first,
    window_split,
    cotangent,
    running_grad,
    gain_attn,
    w_query,
    w_key,
    w_value,
    w_out,
    gain_mlp,
    w_gate,
    w_up,
    w_down,
):
    n, copies = lax.axis_size("fsdp"), lax.axis_size("dp")
    size, width = tokens.shape
    length, cols = n * size, width // n
    rows = w_query.shape[0]
    half = rows // 2
    hidden = w_down.shape[0]
    cos, sin = (jnp.asarray(t) for t in rope_table(length, 128))
    qkv, lse, att, nrm, mid, nm, wqkv, wgc, wuc, g1_all, g2_all, g_all = call(
        functools.partial(front_kernel, n, copies // 2),
        "front",
        1,
        [
            ((length, 3 * cols), BF),
            ((length, 128), F32),
            ((length, cols), BF),
            ((length, width), BF),
            ((size, width), F32),
            ((size, width), BF),
            ((width, 3 * cols), BF),
            ((width, hidden), BF),
            ((width, hidden), BF),
            ((16, width), BF),
            ((16, width), BF),
            ((length, width), BF),
        ],
        [
            ((length, width), BF),
            ((length, cols), BF),
            ((width, width), BF),
            ((size, width), BF),
            ((n, rows, hidden), BF),
            ((n, rows, hidden), BF),
        ],
        (
            tokens,
            value_first,
            w_query,
            w_key,
            w_value,
            w_out,
            gain_attn,
            gain_mlp,
            window_split,
            cos,
            sin,
            w_gate,
            w_up,
            cotangent,
        ),
        smem=(8,),
        dmas=(256, 8),
    )
    gmid, gb, base_out, sb1, grad_gate, grad_up, grad_down = call(
        functools.partial(middle_kernel, n),
        "middle",
        2,
        [
            ((size, width), F32),
            ((size, width), BF),
            ((size, width), F32),
            ((n, size, width), BF),
            ((width, hidden), BF),
            ((width, hidden), BF),
            ((hidden, width), BF),
        ],
        [
            ((length, width), BF),
            ((length, hidden), BF),
            ((length, hidden), BF),
            ((length, hidden), BF),
            ((length, hidden), F32),
            ((length, hidden), F32),
            ((n, size, width), BF),
            ((n, size, width), BF),
            ((size, width), F32),
        ],
        (nm, mid, g_all, wgc, wuc, w_down, g2_all),
        dmas=(48, 8),
    )
    pieces, third = (n, half, hidden), (3, n, half, cols)
    lines = [(half, n * hidden), (half, n * hidden), (hidden // 2, width), (3, half, width), (cols // 2, width)]
    layer_out, input_grad, first_grad, sum_gate, sum_up, sum_down, sum_qkv, sum_out = call(
        functools.partial(back_kernel, n, copies // 2),
        "back",
        3,
        [
            ((size, width), BF),
            ((size, width), F32),
            ((size, width), F32),
            ((2, half, n * hidden), BF),
            ((2, half, n * hidden), BF),
            ((2, hidden // 2, width), BF),
            ((3, 2, half, width), BF),
            ((2, cols // 2, width), BF),
        ],
        [
            ((length, width), BF),
            ((length, cols), F32),
            ((length, cols), F32),
            ((length, 3 * cols), BF),
            ((size, width), BF),
            ((n, size, width), BF),
            ((n, size, width), BF),
            ((size, width), F32),
            ((n, size, width), BF),
            ((3, width, cols), BF),
            ((2, cols // 2, width), BF),
            (pieces, BF),
            (pieces, BF),
            (lines[2], BF),
            (third, BF),
            (lines[4], BF),
            (pieces, BF),
            (pieces, BF),
            (third, BF),
            (pieces, BF),
            (pieces, BF),
        ]
        + [(shape, BF) for shape in lines * 2],
        (
            gb,
            gmid,
            tokens,
            qkv,
            lse,
            att,
            nrm,
            wqkv,
            w_out,
            window_split,
            cos,
            sin,
            running_grad,
            g1_all,
            base_out,
            sb1,
            grad_gate.reshape(n, 2, half, hidden),
            grad_up.reshape(n, 2, half, hidden),
            grad_down.reshape(2, hidden // 2, width),
        ),
        smem=(9,),
        dmas=(160, 8),
    )
    grad_query, grad_key, grad_value = (sum_qkv[j].reshape(rows, width).astype(F32) for j in range(3))
    grad_gate, grad_up = (total.reshape(rows, -1).astype(F32) for total in (sum_gate, sum_up))

    def gain_grad(gain, *pairs):
        return sum(jnp.sum(w.astype(F32) * g, axis=1) for w, g in pairs) / gain.astype(F32)

    return (
        layer_out,
        input_grad,
        first_grad,
        gain_grad(gain_attn, (w_query, grad_query), (w_key, grad_key), (w_value, grad_value)),
        grad_query,
        grad_key,
        grad_value,
        sum_out.reshape(rows, width).astype(F32),
        gain_grad(gain_mlp, (w_gate, grad_gate), (w_up, grad_up)),
        grad_gate,
        grad_up,
        sum_down.reshape(hidden, width).astype(F32),
    )


def solution(mesh):
    token, flat, matrix = P(("dp", "fsdp"), None), P("fsdp"), P("fsdp", None)
    return jax.shard_map(
        body,
        mesh=mesh,
        in_specs=(token, token, P("dp"), token, token, flat)
        + (matrix,) * 4
        + (flat,)
        + (matrix,) * 3,
        out_specs=(token, token, token, flat) + (matrix,) * 4 + (flat,) + (matrix,) * 3,
        check_vma=False,
    )
```

```python
import functools

import jax
import jax.numpy as jnp
import numpy as np
from jax import lax
from jax.experimental import pallas as pl
from jax.experimental.pallas import tpu as pltpu
from jax.sharding import PartitionSpec as P

HD = 64
EPS = 1e-06
MESH = pl.DeviceIdType.MESH
BF = jnp.bfloat16
F32 = jnp.float32
LIMIT = 60 * 1024 * 1024


def dot_nn(a, b):
    return lax.dot_general(a, b, (((1,), (0,)), ((), ())), preferred_element_type=F32)


def dot_nt(a, b):
    return lax.dot_general(a, b, (((1,), (1,)), ((), ())), preferred_element_type=F32)


def dot_tn(a, b):
    return lax.dot_general(a, b, (((0,), (0,)), ((), ())), preferred_element_type=F32)


def flip(f, k, n):
    out, bit = 0, 1
    while bit < n:
        have, want = lax.rem(f // bit, 2), (k // bit) % 2
        out = out + (1 - have if want else have) * bit
        bit *= 2
    return out


class Net:
    def __init__(self, n, ssem, rsem, lsem=None):
        self.n, self.ssem, self.rsem, self.lsem = n, ssem, rsem, lsem
        self.d, self.f = lax.axis_index("dp"), lax.axis_index("fsdp")
        self.c = lax.rem(self.d, 2)
        self.mate = (self.d + 1 - 2 * self.c, self.f)
        self.used, self.lused, self.sent = 0, 0, []

    def peer(self, k):
        return (self.d, flip(self.f, k, self.n))

    def take(self, count=1):
        self.used += count
        return self.used - count

    def push(self, src, dst, device, slot=None):
        slot = self.take() if slot is None else slot
        copy = pltpu.make_async_remote_copy(
            src_ref=src,
            dst_ref=dst,
            send_sem=self.ssem.at[slot],
            recv_sem=self.rsem.at[slot],
            device_id=device,
            device_id_type=MESH,
        )
        copy.start()
        self.sent.append(copy)
        return copy

    def local(self, src, dst):
        copy = pltpu.make_async_copy(src, dst, self.lsem.at[self.lused])
        self.lused += 1
        copy.start()
        return copy

    def barrier(self, devices):
        sem = pltpu.get_barrier_semaphore()
        for device in devices:
            pl.semaphore_signal(sem, inc=1, device_id=device, device_id_type=MESH)
        pl.semaphore_wait(sem, len(devices))

    def drain(self):
        for copy in self.sent:
            copy.wait_send()


def rows_of(ref, block, size):
    return ref.at[pl.ds(pl.multiple_of(block * size, size), size)]


class Gather:
    def __init__(self, net, own, into, size):
        self.net, self.into, self.size = net, into, size
        self.direct = [1, 2] if net.n == 4 else list(range(1, net.n))
        self.copies = {k: net.push(own, rows_of(into, net.f, size), net.peer(k)) for k in self.direct}
        self.halves = {}

    def part(self, block, half):
        start = pl.multiple_of(block * self.size + half * (self.size // 2), self.size // 2)
        return self.into.at[pl.ds(start, self.size // 2)]

    def wait(self, k):
        net = self.net
        if k in self.copies:
            self.copies[k].wait_recv()
            if net.n == 4:
                part = self.part(flip(net.f, k, 4), k - 1)
                self.halves[k] = net.push(part, part, net.peer(3 - k))
        else:
            for copy in self.halves.values():
                copy.wait_recv()


def lane_mask(width, head):
    lane = lax.broadcasted_iota(jnp.int32, (1, width), 1)
    return (lane // HD) == head


def turn(values, cos, sin):
    width = values.shape[1]
    lane = lax.broadcasted_iota(jnp.int32, (1, width), 1)
    first = lax.rem(lane, HD) < HD // 2
    other = jnp.where(
        first, pltpu.roll(values, width - HD // 2, 1), pltpu.roll(values, HD // 2, 1)
    )
    return values * cos + other * sin


def table_rows(net, cos_ref, sin_ref, flag, start, size, length, width):
    half = length // 2
    plain = pl.ds(pl.multiple_of(start, size), size)
    split = pl.ds(pl.multiple_of(lax.rem(start, half), size), size)
    out = []
    for ref in (cos_ref, sin_ref):
        rows = jnp.where(flag == 1, ref[split], ref[plain])
        out.append(jnp.concatenate([rows] * (width // rows.shape[1]), axis=1))
    return out


def block_bias(flag, r, kb, size, length):
    half = length // 2
    if kb == r:
        row = lax.broadcasted_iota(jnp.int32, (size, size), 0)
        col = lax.broadcasted_iota(jnp.int32, (size, size), 1)
        return jnp.where(col <= row, 0.0, -1e30)
    if (r * size >= half) != (kb * size >= half):
        return jnp.where(flag == 1, -1e30, 0.0)
    return None


def scores_of(query, key, bias):
    scores = dot_nt(query, key)
    return scores if bias is None else scores + bias


def factor_of(hidden):
    return lax.rsqrt(jnp.mean(hidden * hidden, axis=-1, keepdims=True) + EPS)


def norm_back(hidden, gain, grad):
    factor = factor_of(hidden)
    scaled = grad * gain
    return factor * scaled - hidden * (factor * factor * factor) * jnp.mean(
        scaled * hidden, axis=-1, keepdims=True
    )


class Agenda:
    def __init__(self):
        self.clock, self.items = 0.0, []

    def at(self, time, step):
        self.items.append((time, len(self.items), step))

    def until(self, time):
        self.clock = max(self.clock, time)
        due = sorted(item for item in self.items if item[0] <= self.clock)
        self.items = [item for item in self.items if item[0] > self.clock]
        for _, _, step in due:
            step()

    def spend(self, time):
        self.until(self.clock + time)


class Spread:
    def __init__(self, net, chips, rows, sources):
        self.net, self.rows = net, rows
        self.chip = net.d // 2
        self.chips = chips if rows % (32 * chips) == 0 else 1
        self.share = rows // (2 * self.chips)
        self.part = self.chip if self.chips > 1 else 0
        n = net.n
        self.right, self.left, self.mate = (net.take(self.chips * (n - 1)) for _ in range(3))
        self.into = sources[0][2]
        self.first = []
        for k in range(1, n):
            to = net.peer(k)
            for piece, place, _ in sources:
                mine = pl.ds(self.start(0, self.part, net.c), self.share)
                here = pl.ds(self.start(net.f, self.part, net.c), self.share)
                self.first.append(net.push(piece(to[1]).at[mine], place.at[here], to))

    def start(self, block, part, core):
        return pl.multiple_of(block * self.rows + (2 * part + core) * self.share, self.share)

    def view(self, k, part, core):
        return self.into.at[pl.ds(self.start(flip(self.net.f, k, self.net.n), part, core), self.share)]

    def copy(self, k, part, base, device):
        net = self.net
        slot = base + part * (net.n - 1) + k - 1
        view = self.view(k, part, net.c)
        return pltpu.make_async_remote_copy(
            src_ref=view,
            dst_ref=view,
            send_sem=net.ssem.at[slot],
            recv_sem=net.rsem.at[slot],
            device_id=device,
            device_id_type=MESH,
        )

    def along(self, step):
        return ((self.chip + step) * 2 + self.net.c, self.net.f)

    def pass_on(self, part, base, step, room):
        @pl.when(room)
        def _():
            for k in range(1, self.net.n):
                self.copy(k, part, base, self.along(step)).start()

    def own(self):
        for copy in self.first:
            copy.wait_recv()
        if self.chips > 1:
            self.pass_on(self.part, self.right, 1, self.chip + 1 < self.chips)
            self.pass_on(self.part, self.left, -1, self.chip > 0)
        for k in range(1, self.net.n):
            self.copy(k, self.part, self.mate, self.net.mate).start()

    def hop(self, j):
        if j >= self.chips:
            return
        for base, step in ((self.right, 1), (self.left, -1)):
            part = self.part - step * j

            @pl.when((part >= 0) & (part < self.chips))
            def _(base=base, step=step, part=part):
                for k in range(1, self.net.n):
                    self.copy(k, part, base, self.net.mate).wait_recv()
                room = self.chip + 1 < self.chips if step == 1 else self.chip > 0
                self.pass_on(part, base, step, room)
                for k in range(1, self.net.n):
                    self.copy(k, part, self.mate, self.net.mate).start()

    def finish(self):
        n = self.net.n
        for part in range(self.chips):
            for k in range(1, n):
                self.copy(k, part, self.mate, self.net.mate).wait()
            if self.chips > 1:

                @pl.when((part <= self.chip) & (self.chip + 1 < self.chips))
                def _(part=part):
                    for k in range(1, n):
                        self.copy(k, part, self.right, self.net.mate).wait_send()

                @pl.when((part >= self.chip) & (self.chip > 0))
                def _(part=part):
                    for k in range(1, n):
                        self.copy(k, part, self.left, self.net.mate).wait_send()


def gain_rows(net, src, dst, rows):
    place = dst.at[:, pl.ds(pl.multiple_of(net.f * rows, rows), rows)]
    dst[:, pl.ds(pl.multiple_of(net.f * rows, rows), rows)] = jnp.broadcast_to(src[...].reshape(1, rows), (16, rows))
    return [net.push(place, place, net.peer(k)) for k in range(1, net.n)]


def send_to(net, r, src, dst, base, away=None):
    return pltpu.make_async_remote_copy(
        src_ref=src,
        dst_ref=dst,
        send_sem=net.ssem.at[base + r],
        recv_sem=net.rsem.at[base + (net.f if away is None else away)],
        device_id=(net.d, r),
        device_id_type=MESH,
    )


def front_kernel(
    n,
    chips,
    x,
    vf,
    wq,
    wk,
    wv,
    wo,
    g1,
    g2,
    flag_ref,
    cos_hbm,
    sin_hbm,
    wg_hbm,
    wu_hbm,
    ct,
    qkv_out,
    probs,
    att_out,
    nrm_out,
    mid,
    nm,
    wqkv_out,
    wgc_out,
    wuc_out,
    g1_all,
    g2_all,
    g_out,
    qkv,
    att,
    nrm,
    wqkv,
    wgc,
    wuc,
    g_all,
    wg,
    wu,
    cos_ref,
    sin_ref,
    x_all,
    vfc,
    wo_all,
    att_own,
    wgr,
    wur,
    low_probs,
    ssem,
    rsem,
    lsem,
):
    net = Net(n, ssem, rsem, lsem)
    size, width = x.shape
    length = n * size
    cols = width // n
    rows = wq.shape[0]
    hidden = wg.shape[1] // n
    flag = flag_ref[0]
    chip = net.d // 2
    sem = pltpu.get_barrier_semaphore()
    near = [net.peer(k) for k in range(1, n)] + [net.mate]
    for device in near:
        pl.semaphore_signal(sem, inc=1, device_id=device, device_id_type=MESH)
    for step, room in ((1, chip + 1 < chips), (-1, chip > 0)):
        @pl.when(room)
        def _(step=step):
            device = ((chip + step) * 2 + net.c, net.f)
            pl.semaphore_signal(sem, inc=1, device_id=device, device_id_type=MESH)

    edge = (chip == 0) | (chip == chips - 1)

    @pl.when(edge)
    def _():
        pl.semaphore_wait(sem, len(near) + min(chips - 1, 1))

    @pl.when(jnp.logical_not(edge))
    def _():
        pl.semaphore_wait(sem, len(near) + 2)

    mine = pl.ds(pl.multiple_of(net.f * cols, cols), cols)
    sources = []
    for i, w in enumerate((wq, wk, wv)):
        piece = lambda to, w=w: w.at[:, pl.ds(pl.multiple_of(to * cols, cols), cols)]
        sources.append((piece, wqkv.at[:, pl.ds(i * cols, cols)], wqkv))
    spread_qkv = Spread(net, chips, rows, sources)
    gains = gain_rows(net, g1, g1_all, rows) + gain_rows(net, g2, g2_all, rows)
    x_gather = Gather(net, x, x_all, size)
    values = []
    for k in range(1, n):
        device = net.peer(k)
        src = vf.at[:, pl.ds(pl.multiple_of(device[1] * cols, cols), cols)]
        values.append(net.push(src, rows_of(vfc, net.f, size), device))
    spread_out = Spread(net, chips, rows, [(lambda to: wo, wo_all, wo_all)])
    own_x = net.local(x, rows_of(x_all, net.f, size))
    halves = [net.local(wg_hbm, wg), net.local(wu_hbm, wu)]
    locals_ = [net.local(vf.at[:, mine], rows_of(vfc, net.f, size))]
    for i, w in enumerate((wq, wk, wv)):
        into = rows_of(wqkv.at[:, pl.ds(i * cols, cols)], net.f, rows)
        locals_.append(net.local(w.at[:, mine], into))
    locals_.append(net.local(wo, rows_of(wo_all, net.f, rows)))
    locals_.append(net.local(ct, rows_of(g_all, net.f, size)))
    locals_ += [net.local(cos_hbm, cos_ref), net.local(sin_hbm, sin_ref)]
    stores = []
    agenda = Agenda()

    def plan(spread, begin, time):
        agenda.at(begin, spread.own)
        for j in range(1, chips):
            agenda.at(begin + j * time + 0.5, functools.partial(spread.hop, j))

    plan(spread_qkv, 8, 3.6)
    plan(spread_out, 19, 4.4)
    for copy in halves:
        copy.wait()
    for w, piece, into in ((wg, wgr, wgc), (wu, wur, wuc)):
        for r in range(n):
            piece[r, :, :hidden] = w[:, r * hidden : (r + 1) * hidden]
        if piece.shape[2] > hidden:
            piece[:, :, hidden:] = jnp.zeros((n, rows, piece.shape[2] - hidden), BF)
        into[pl.ds(pl.multiple_of(net.f * rows, rows), rows)] = piece[net.f]
    for copy in gains:
        copy.wait_recv()
    agenda.until(8)
    spread_gate = Spread(net, chips, rows, [(lambda to: wgr.at[to], wgc, wgc)])
    spread_up = Spread(net, chips, rows, [(lambda to: wur.at[to], wuc, wuc)])
    plan(spread_gate, 31, 3.4)
    plan(spread_up, 40, 3.4)
    own_x.wait()
    gain = g1_all[0:1, :].astype(F32)

    def normalize(block):
        at = pl.ds(pl.multiple_of(block * size, size), size)
        rows_in = x_all[at].astype(F32)
        nrm[at] = (rows_in * factor_of(rows_in) * gain).astype(BF)

    normalize(net.f)
    agenda.until(16)
    for k in range(1, n - 1):
        x_gather.wait(k)
        normalize(flip(net.f, k, n))
    for copy in locals_:
        copy.wait()
    agenda.until(26)
    x_gather.wait(n - 1)
    normalize(flip(net.f, n - 1, n))
    stores.append(net.local(nrm, nrm_out))
    spreads = [spread_out, spread_gate, spread_up]
    spread_qkv.finish()
    stores.append(net.local(wqkv, wqkv_out))
    for copy in values:
        copy.wait_recv()
    g_gather = Gather(net, ct, g_all, size)
    agenda.until(31)

    @pl.loop(0, n)
    def _(block):
        at = pl.ds(pl.multiple_of(block * size, size), size)
        pre = dot_nn(nrm[at], wqkv[...])
        cos, sin = table_rows(net, cos_ref, sin_ref, flag, block * size, size, length, 2 * cols)
        turned = turn(pre[:, : 2 * cols], cos, sin)
        mixed = 0.5 * pre[:, 2 * cols :] + 0.5 * vfc[at].astype(F32)
        qkv[at, :cols] = (turned[:, :cols] * HD**-0.5).astype(BF)
        qkv[at, cols : 2 * cols] = turned[:, cols:].astype(BF)
        qkv[at, 2 * cols :] = mixed.astype(BF)

    agenda.spend(2.5)
    stores.append(net.local(qkv, qkv_out))
    heads = cols // HD
    base = net.take(n)
    for r in range(n):
        at = slice(r * size, (r + 1) * size)
        query = qkv[at, :cols]
        total = jnp.zeros((size, cols), F32)
        biases = [block_bias(flag, r, kb, size, length) for kb in range(r + 1)]
        for h in range(heads):
            mask = lane_mask(cols, h)
            masked = jnp.where(mask, query, jnp.zeros_like(query))
            tiles = [
                scores_of(masked, qkv[kb * size : (kb + 1) * size, cols : 2 * cols], biases[kb])
                for kb in range(r + 1)
            ]
            top = tiles[0].max(axis=1, keepdims=True)
            for tile in tiles[1:]:
                top = jnp.maximum(top, tile.max(axis=1, keepdims=True))
            raw = [jnp.exp(tile - top) for tile in tiles]
            whole = raw[0].sum(axis=1, keepdims=True)
            for tile in raw[1:]:
                whole = whole + tile.sum(axis=1, keepdims=True)
            inverse = 1.0 / whole
            mixed = None
            for kb, tile in enumerate(raw):
                low = (tile * inverse).astype(BF)
                low_probs[h, r * (r + 1) // 2 + kb] = low
                term = dot_nn(low, qkv[kb * size : (kb + 1) * size, 2 * cols :])
                mixed = term if mixed is None else mixed + term
            total = jnp.where(mask, mixed, total)
        done = pl.ds(r * (r + 1) // 2, r + 1)
        stores.append(net.local(low_probs.at[:, done], probs.at[:, done]))
        att[at] = total.astype(BF)

        @pl.when(net.f == r)
        def _():
            att_own[:, mine] = att[at]

        @pl.when(net.f != r)
        def _():
            send_to(net, r, att.at[pl.ds(r * size, size)], att_own.at[:, mine], base).start()

        agenda.spend(1.2 * (r + 1))
        if r == n - 2:
            for k in (1, 2):
                g_gather.wait(k)
    agenda.spend(100.0)
    stores.append(net.local(att, att_out))
    spread_out.finish()
    rows_at = pl.ds(pl.multiple_of(net.f * size, size), size)
    for k in range(1, n):
        other = flip(net.f, k, n)
        place = att_own.at[:, pl.ds(pl.multiple_of(other * cols, cols), cols)]
        src = rows_of(att, other, size)
        send_to(net, other, src, place, base, other).wait()
    sums = x_all[rows_at].astype(F32) + dot_nn(att_own[...], wo_all[...])
    mid[...] = sums
    nm[...] = (sums * factor_of(sums) * g2_all[0:1, :].astype(F32)).astype(BF)
    for spread, into, out in ((spread_gate, wgc, wgc_out), (spread_up, wuc, wuc_out)):
        spread.finish()
        stores.append(net.local(into, out))
    for k in range(3, n):
        g_gather.wait(k)
    stores.append(net.local(g_all, g_out))
    for copy in stores:
        copy.wait()
    net.drain()


def middle_kernel(
    n,
    nm,
    mid,
    g_all,
    wgc,
    wuc,
    wd,
    partial,
    rest,
    base_out,
    rest_out,
    grad_gate,
    grad_up,
    grad_down,
    nm_all,
    hid_all,
    gg_all,
    ug_all,
    coef,
    silus,
    wd_wide,
    sb1,
    rb1,
    sb2,
    rb2,
    ssem,
    rsem,
    lsem,
):
    net = Net(n, ssem, rsem, lsem)
    size, width = nm.shape
    net.barrier([net.peer(k) for k in range(1, n)])
    gather = Gather(net, nm, nm_all, size)
    hidden = wd.shape[0]
    wd_wide[:hidden] = wd[...]
    if wd_wide.shape[0] > hidden:
        wd_wide[hidden:] = jnp.zeros((wd_wide.shape[0] - hidden, width), BF)
    local = net.local(nm, rows_of(nm_all, net.f, size))

    def rows_at(k):
        return pl.ds(pl.multiple_of(flip(net.f, k, n) * size, size), size)

    def forward(k):
        at = rows_at(k)
        a = nm_all[at]
        gate = dot_nn(a, wgc[...])
        up = dot_nn(a, wuc[...])
        sig = jax.nn.sigmoid(gate)
        silu = gate * sig
        hid_all[at] = (silu * up).astype(BF)
        coef[at] = up * sig * (1.0 + gate * (1.0 - sig))
        silus[at] = silu
        part = dot_nn(hid_all[at], wd_wide[...])
        if k == 0:
            base_out[...] = mid[...] + part
        elif k < 3:
            sb1[k] = part.astype(BF)
        else:
            rest_out[k - 3] = part.astype(BF)

    soon = []

    def backward(k):
        at = rows_at(k)
        grad = dot_nt(g_all[at], wd_wide[...])
        gg_all[at] = (grad * coef[at]).astype(BF)
        ug_all[at] = (grad * silus[at]).astype(BF)
        back = dot_nt(gg_all[at], wgc[...]) + dot_nt(ug_all[at], wuc[...])
        if k == 0:
            partial[...] = back
        elif k < 3:
            sb2[k] = back.astype(BF)
            soon.append((k, net.push(sb2.at[k], rb2.at[k], net.peer(k))))
        else:
            rest[k - 3] = back.astype(BF)

    local.wait()
    forward(0)
    backward(0)
    for k in range(1, n):
        gather.wait(k)
        for j in ([1] if k == 2 or n == 2 else []) + ([k] if k >= 2 else []):
            forward(j)
            backward(j)
    late = [(k, net.push(sb1.at[k], rb1.at[k], net.peer(k))) for k in range(1, 3)]
    tile = 256 if width % 256 == 0 else width

    @pl.loop(0, width // tile)
    def _(i):
        at = pl.ds(pl.multiple_of(i * tile, tile), tile)
        lhs = nm_all[:, at]
        grad_gate[at] = dot_tn(lhs, gg_all[...]).astype(BF)
        grad_up[at] = dot_tn(lhs, ug_all[...]).astype(BF)
        grad_down[:, at] = dot_tn(hid_all[...], g_all[:, at])[:hidden].astype(BF)

    grad = partial[...]
    for k, copy in soon:
        copy.wait_recv()
        grad = grad + rb2[k].astype(F32)
    partial[...] = grad
    result = base_out[...]
    for k, copy in late:
        copy.wait_recv()
        result = result + rb1[k].astype(F32)
    base_out[...] = result
    net.drain()


class Line:
    def __init__(self, net, chips):
        chip, middle = net.d // 2, chips // 2
        left = chip < middle
        inward = jnp.where(left, chip + 1, chip - 1)
        outward = jnp.where(left, chip - 1, chip + 1)
        self.net, self.chip, self.first_middle = net, chip, middle - 1
        self.edge = (chip == 0) | (chip == chips - 1)
        self.middle = (chip == middle - 1) | (chip == middle)
        self.inner = (inward * 2 + net.c, net.f)
        self.outer = (outward * 2 + net.c, net.f)
        self.chunks, self.paced, self.middle_ends = [], set(), chips == 2

    def barrier(self, others):
        net, sem = self.net, pltpu.get_barrier_semaphore()
        fixed = others + [self.inner]
        for device in fixed:
            pl.semaphore_signal(sem, inc=1, device_id=device, device_id_type=MESH)

        @pl.when(jnp.logical_not(self.edge))
        def _():
            pl.semaphore_signal(sem, inc=1, device_id=self.outer, device_id_type=MESH)
            pl.semaphore_wait(sem, len(fixed) + 1)

        @pl.when(self.edge)
        def _():
            pl.semaphore_wait(sem, len(fixed))

    def chunk(self, own, outer, total, deliver, owner=None, swap=None):
        self.chunks.append((own, outer, total, deliver, owner, swap, [self.net.take() for _ in range(4)]))
        return len(self.chunks) - 1

    def copy(self, src, dst, send, recv, device):
        return pltpu.make_async_remote_copy(
            src_ref=src,
            dst_ref=dst,
            send_sem=self.net.ssem.at[send],
            recv_sem=self.net.rsem.at[recv],
            device_id=device,
            device_id_type=MESH,
        )

    def owns(self, owner):
        return self.chip == self.first_middle + owner

    def inwards(self, i):
        own, outer, total, _, owner, _, (up, down, _, _) = self.chunks[i]

        @pl.when(jnp.logical_not(self.edge))
        def _():
            self.copy(own, outer, up, up, self.outer).wait_recv()
            own[...] = own[...] + outer[...]

        sends = self.middle
        if owner is not None:
            sends = sends & jnp.logical_not(self.owns(owner))

        @pl.when(sends)
        def _():
            self.copy(own, total, down, down, self.inner).start()

        @pl.when(jnp.logical_not(self.middle))
        def _():
            self.copy(own, outer, up, up, self.inner).start()

    def pace(self, i):
        own, outer, _, _, _, _, (up, _, _, _) = self.chunks[i]
        self.paced.add(i)
        if self.middle_ends:
            return
        self.copy(own, outer, up, up, self.inner).wait_send()

    def outwards(self, i):
        own, outer, total, deliver, _, _, (up, down, away, _) = self.chunks[i]
        self.copy(own, total, down, down, self.inner).wait_recv()

        @pl.when(self.middle)
        def _():
            total[...] = own[...] + total[...]

        @pl.when(jnp.logical_not(self.edge))
        def _():
            self.copy(total, total, away, down, self.outer).start()

        deliver()

    def make(self, i):
        own, outer, total, _, owner, swap, (_, down, _, _) = self.chunks[i]

        @pl.when(self.owns(owner))
        def _():
            self.copy(own, total, down, down, self.inner).wait_recv()
            total[...] = own[...] + total[...]
            swap.start()

    def pass_on(self, i):
        _, _, _, deliver, owner, swap, (_, down, away, over) = self.chunks[i]
        done = swap.done

        @pl.when(self.owns(owner))
        def _():
            swap.end()
            self.copy(done, done, over, over, self.inner).start()

            @pl.when(jnp.logical_not(self.edge))
            def _():
                self.copy(done, done, away, over, self.outer).start()

            deliver()

    def receive(self, i):
        _, _, _, deliver, owner, swap, (_, down, away, over) = self.chunks[i]
        done = swap.done

        @pl.when(jnp.logical_not(self.owns(owner)))
        def _():
            self.copy(done, done, over, over, self.inner).wait_recv()

            @pl.when(jnp.logical_not(self.edge))
            def _():
                self.copy(done, done, away, over, self.outer).start()

            deliver()

    def finish(self):
        for i, (own, outer, total, _, owner, swap, (up, down, away, over)) in enumerate(self.chunks):
            done = total if owner is None else swap.done
            slot = jnp.where(self.middle, down, up)
            sent = jnp.logical_not(self.edge) | self.middle if i in self.paced else self.chip >= 0
            if owner is not None:
                sent = sent & jnp.logical_not(self.owns(owner))

                @pl.when(self.owns(owner))
                def _():
                    self.copy(done, done, over, over, self.inner).wait_send()

            @pl.when(sent)
            def _():
                self.copy(own, total, slot, down, self.inner).wait_send()

            @pl.when(jnp.logical_not(self.edge))
            def _():
                self.copy(done, done, away, down, self.outer).wait_send()


class Swap:
    def __init__(self, net, line, total, place, done, settle=None):
        self.net, self.line, self.total, self.place = net, line, total, place
        self.done, self.settle = done, settle
        self.base = net.take(net.n)

    def copy(self, k):
        to = self.net.peer(k)
        slot = self.base + k
        return self.line.copy(self.total(to[1]), self.place(self.net.f), slot, slot, to)

    def start(self):
        for k in range(1, self.net.n):
            self.copy(k).start()
        self.place(self.net.f)[...] = self.total(self.net.f)[...]

    def end(self):
        for k in range(1, self.net.n):
            self.copy(k).wait()
        if self.settle is not None:
            self.settle()


def cut(size):
    if size % 32 == 0:
        return [(0, size // 2), (size // 2, size // 2)]
    return [(0, size)]


SWAP = 20.0


def back_kernel(
    n,
    chips,
    rest,
    partial,
    mid,
    ct,
    g2_all,
    flag_ref,
    x_hbm,
    qkv_hbm,
    probs_hbm,
    att_hbm,
    nrm_hbm,
    wqkv_hbm,
    wo_hbm,
    cos_hbm,
    sin_hbm,
    rg_hbm,
    g1_hbm,
    base_hbm,
    rest_out,
    grad_gate,
    grad_up,
    grad_down,
    layer_out,
    input_grad,
    first_grad,
    out_gate,
    out_up,
    out_down,
    out_qkv,
    out_out,
    rest_in,
    x,
    qkv,
    probs,
    att,
    nrm,
    wqkv,
    wo,
    cos_ref,
    sin_ref,
    g1_all,
    base_out,
    gb_all,
    dk,
    dv,
    dqkv,
    vg,
    sb,
    rb,
    own,
    grad_qkv,
    grad_out,
    sum_gate,
    sum_up,
    sum_down,
    sum_qkv,
    sum_out,
    m_gate,
    m_up,
    m_down,
    m_qkv,
    m_out,
    l_gate,
    l_up,
    l_down,
    l_qkv,
    l_out,
    o_gate,
    o_up,
    o_down,
    o_qkv,
    o_out,
    t_gate,
    t_up,
    t_qkv,
    a_gate,
    a_up,
    ssem,
    rsem,
    lsem,
):
    net = Net(n, ssem, rsem, lsem)
    line = Line(net, chips)
    size, width = ct.shape
    length = n * size
    cols = width // n
    heads = cols // HD
    half, hidden = m_gate.shape[1], sum_gate.shape[2] // n
    flag = flag_ref[0]
    line.barrier([net.peer(k) for k in range(1, n)] + [net.mate])
    rests = [net.push(rest.at[k - 3], rest_in.at[k - 3], net.peer(k)) for k in range(3, n)]
    mates = [
        net.push(grad_down.at[1 - net.c], m_down, net.mate),
        net.push(grad_gate.at[:, 1 - net.c], m_gate, net.mate),
        net.push(grad_up.at[:, 1 - net.c], m_up, net.mate),
    ]
    halves = [
        net.local(grad_down.at[net.c], l_down),
        net.local(grad_gate.at[:, net.c], l_gate),
        net.local(grad_up.at[:, net.c], l_up),
    ]
    early = [
        net.local(src, dst)
        for src, dst in (
            (qkv_hbm, qkv),
            (wo_hbm, wo),
            (probs_hbm, probs),
            (cos_hbm, cos_ref),
            (sin_hbm, sin_ref),
            (wqkv_hbm, wqkv),
            (att_hbm, att),
        )
    ]
    later = [
        net.local(src, dst)
        for src, dst in (
            (nrm_hbm, nrm),
            (x_hbm, x),
            (g1_hbm, g1_all),
            (rg_hbm, first_grad),
            (base_hbm, base_out),
        )
    ]
    dk[...] = jnp.zeros_like(dk)
    dv[...] = jnp.zeros_like(dv)
    finals = []

    def to_mate(place):
        slot = net.take()
        finals.append((slot, place))
        return lambda: line.copy(place(net.c), place(net.c), slot, slot, net.mate).start()

    agenda = Agenda()
    hop = 8.2

    def edge_only(time, step, i):
        def run():
            @pl.when(line.edge)
            def _():
                step(i)

        agenda.at(time, run)

    def rest_only(time, step, i):
        def run():
            @pl.when(jnp.logical_not(line.edge))
            def _():
                step(i)

        agenda.at(time, run)

    def launch(i, before):
        if before is not None:
            line.pace(before)
        line.inwards(i)

    def plan(i, start, time, before):
        edge_only(start, functools.partial(launch, before=before), i)
        rest_only(start + time, line.inwards, i)
        rest_only(start + 2 * time, line.outwards, i)
        edge_only(start + 3 * time + 8, line.outwards, i)

    arrivals = []

    def change_over(swap, place):
        send = to_mate(place)

        def arrive():
            swap.end()
            send()

        arrivals.append(arrive)
        return swap.start

    def spread_rows(t, a, total, at, rows):
        def settle():
            for r in range(n):
                total[net.c, rows, r * hidden : (r + 1) * hidden] = a[r, rows, :hidden]

        return Swap(net, line, lambda r: t.at[r, at], lambda f: a.at[f, at], total.at[net.c, at], settle)

    begin, before = 9.0, None
    for mate, load, l, m in zip(mates, halves, (l_down, l_gate, l_up), (m_down, m_gate, m_up)):
        load.wait()
        mate.wait_recv()
        l[...] = l[...] + m[...]
        chunks = []
        if l is l_down:
            for start, count in cut(l_down.shape[0]):
                at = pl.ds(start, count)
                place = lambda c, at=at: sum_down.at[c, at]
                chunks.append(line.chunk(l_down.at[at], o_down.at[at], place(net.c), to_mate(place)))
        else:
            o, t, a, total = (
                (o_gate, t_gate, a_gate, sum_gate) if l is l_gate else (o_up, t_up, a_up, sum_up)
            )
            for owner, (start, count) in enumerate(cut(half)):
                at, rows = pl.ds(start, count), slice(start, start + count)
                place = lambda c, at=at, total=total: total.at[c, at]
                swap = spread_rows(t, a, total, at, rows)
                chunks.append(
                    line.chunk(l.at[:, at], o.at[:, at], t.at[:, at], change_over(swap, place))
                )
        for i in chunks:
            plan(i, begin, hop, before)
            begin, before = begin + hop, i
        agenda.until(9)
    grad = partial[...]
    for i, copy in enumerate(rests):
        copy.wait_recv()
        grad = grad + rest_in[i].astype(F32)
    total = ct[...].astype(F32) + norm_back(mid[...], g2_all[0:1, :].astype(F32), grad)
    input_grad[...] = total
    gb_all[pl.ds(pl.multiple_of(net.f * size, size), size)] = total.astype(BF)
    gather = Gather(net, rows_of(gb_all, net.f, size), gb_all, size)
    for copy in early:
        copy.wait()
    agenda.until(17)
    agenda.until(25)
    for k in range(1, n - 1):
        gather.wait(k)
    agenda.until(29)
    gather.wait(n - 1)
    agenda.until(34)

    base = net.take(n)
    value_base = net.take(n)

    def attend(r):
        at = slice(r * size, (r + 1) * size)
        query = qkv[at, :cols]
        grad = dot_nt(gb_all[at], wo[...]).astype(BF)
        total = jnp.zeros((size, cols), F32)
        for h in range(heads):
            mask = lane_mask(cols, h)
            qm = jnp.where(mask, query, jnp.zeros_like(query))
            gm = jnp.where(mask, grad, jnp.zeros_like(grad))
            tiles, grads = [], []
            inner = None
            for kb in range(r + 1):
                there = slice(kb * size, (kb + 1) * size)
                prob = probs[h, r * (r + 1) // 2 + kb]
                gprob = dot_nt(gm, qkv[there, 2 * cols :])
                part = (prob.astype(F32) * gprob).sum(axis=1, keepdims=True)
                inner = part if inner is None else inner + part
                tiles.append(prob)
                grads.append(gprob)
            mixed = None
            for kb in range(r + 1):
                there = slice(kb * size, (kb + 1) * size)
                low = (tiles[kb].astype(F32) * (grads[kb] - inner)).astype(BF)
                term = dot_nn(low, qkv[there, cols : 2 * cols])
                mixed = term if mixed is None else mixed + term
                dk[there] += dot_tn(low, qm)
                dv[there] += dot_tn(tiles[kb], gm)
            total = jnp.where(mask, mixed, total)
            agenda.spend(0.42 * (r + 1))
        cos, sin = table_rows(net, cos_ref, sin_ref, flag, r * size, size, length, cols)
        dqkv[at, :cols] = turn(total * HD**-0.5, cos, -sin).astype(BF)
        dqkv[at, cols : 2 * cols] = turn(dk[at], cos, -sin).astype(BF)
        dqkv[at, 2 * cols :] = (0.5 * dv[at]).astype(BF)
        part = dot_nt(dqkv[at], wqkv[...])
        sb[r] = part.astype(BF)
        place = vg.at[:, pl.ds(pl.multiple_of(net.f * cols, cols), cols)]

        @pl.when(net.f == r)
        def _():
            own[...] = part
            vg[:, pl.ds(pl.multiple_of(net.f * cols, cols), cols)] = dqkv[at, 2 * cols :]

        @pl.when(net.f != r)
        def _():
            send_to(net, r, sb.at[r], rb.at[net.f], base).start()
            piece = dqkv.at[pl.ds(r * size, size), pl.ds(2 * cols, cols)]
            send_to(net, r, piece, place, value_base).start()

        agenda.spend(1.0)

    attend(n - 1)
    grad_out[...] = dot_tn(att[...], gb_all[...]).astype(BF).reshape(grad_out.shape)
    mate_out = net.push(grad_out.at[1 - net.c], m_out, net.mate)
    for r in reversed(range(n - 1)):
        attend(r)
    for copy in later:
        copy.wait()
    tile = 256 if width % 256 == 0 else width

    @pl.loop(0, width // tile)
    def _(i):
        at = pl.ds(pl.multiple_of(i * tile, tile), tile)
        grad = dot_tn(nrm[:, at], dqkv[...]).astype(BF)
        for j in range(3):
            grad_qkv[j, at] = grad[:, j * cols : (j + 1) * cols]

    mate_qkv = []
    for j in range(3):
        mate_qkv.append([])
        for r in range(n):
            rows = pl.ds(pl.multiple_of(2 * half * r + half * (1 - net.c), half), half)
            mate_qkv[j].append(net.push(grad_qkv.at[j, rows], m_qkv.at[j, r], net.mate))
    agenda.spend(3.0)
    mate_out.wait_recv()
    l_out[...] = grad_out[net.c] + m_out[...]
    out_place = lambda c: sum_out.at[c]
    square = line.chunk(l_out, o_out, out_place(net.c), to_mate(out_place))
    begin, small = agenda.clock, 0.7 * hop
    plan(square, begin, small, before)
    begin, before = begin + small, square
    thirds = []
    for j, start, count, owner in ((0, 0, half, 0), (1, 0, half, 1), (2, 0, half // 2, 0), (2, half // 2, half // 2, 1)):
        if start == 0:
            for r in range(n):
                mate_qkv[j][r].wait_recv()
                rows = pl.ds(pl.multiple_of(2 * half * r + half * net.c, half), half)
                l_qkv[j, r] = grad_qkv[j, rows] + m_qkv[j, r]
        at = pl.ds(start, count)
        place = lambda c, j=j, at=at: sum_qkv.at[j, c, at]
        lanes = lambda f, j=j, at=at: sum_qkv.at[j, net.c, at, pl.ds(pl.multiple_of(f * cols, cols), cols)]
        swap = Swap(net, line, lambda r, j=j, at=at: t_qkv.at[j, r, at], lanes, place(net.c))
        thirds.append(
            line.chunk(l_qkv.at[j, :, at], o_qkv.at[j, :, at], t_qkv.at[j, :, at], change_over(swap, place))
        )
        time = small * count / half
        plan(thirds[-1], begin, time, before)
        begin, before = begin + time, thirds[-1]
        agenda.spend(0.0)
    late = [(k, net.push(rest_out.at[k - 3], rest_in.at[k - 3], net.peer(k))) for k in range(3, n)]
    agenda.spend(20.0)
    total = own[...]
    for k in range(1, n):
        other = flip(net.f, k, n)
        send_to(net, other, sb.at[other], rb.at[other], base, other).wait()
        total = total + rb[other].astype(F32)
    input_grad[...] = input_grad[...] + norm_back(x[...].astype(F32), g1_all[0:1, :].astype(F32), total)
    agenda.spend(2.0)
    for k in range(1, n):
        other = flip(net.f, k, n)
        place = vg.at[:, pl.ds(pl.multiple_of(other * cols, cols), cols)]
        piece = dqkv.at[pl.ds(pl.multiple_of(other * size, size), size), pl.ds(2 * cols, cols)]
        send_to(net, other, piece, place, value_base, other).wait()
    first_grad[...] = first_grad[...] + vg[...].astype(F32)
    result = base_out[...]
    for k, copy in late:
        copy.wait_recv()
        result = result + rest_in[k - 3].astype(F32)
    layer_out[...] = result.astype(BF)
    agenda.spend(1000.0)
    for arrive in arrivals:
        arrive()
    stores = []

    def mated(which):
        for slot, place in which:
            line.copy(place(net.c), place(1 - net.c), slot, slot, net.mate).wait()

    mated(finals[: -1 - len(thirds)])
    for src, dst in ((sum_down, out_down), (sum_gate, out_gate), (sum_up, out_up)):
        stores.append(net.local(src, dst))
    mated(finals[-1 - len(thirds) :])
    for src, dst in ((sum_out, out_out), (sum_qkv, out_qkv)):
        stores.append(net.local(src, dst))
    line.finish()
    net.drain()
    for copy in stores:
        copy.wait()


def finish_kernel(
    gate,
    up,
    down,
    qkv,
    out,
    wg,
    wu,
    wq,
    wk,
    wv,
    g1,
    g2,
    layer,
    inputs,
    first,
    f_layer,
    f_inputs,
    f_first,
    gain_one,
    f_query,
    f_key,
    f_value,
    f_out,
    gain_two,
    f_gate,
    f_up,
    f_down,
    sums,
):
    f_layer[...], f_inputs[...], f_first[...] = layer[...], inputs[...], first[...]
    f_down[...], f_out[...] = down[...].astype(F32), out[...].astype(F32)
    step, count = pl.program_id(0), gate.shape[0]

    def row_sums(pairs):
        total = None
        for w, into, grad in pairs:
            grad = grad.astype(F32)
            into[...] = grad
            part = jnp.sum(w[...].astype(F32) * grad, axis=1, keepdims=True)
            total = part if total is None else total + part
        return total

    one = row_sums(((wq, f_query, qkv[0]), (wk, f_key, qkv[1]), (wv, f_value, qkv[2])))
    two = row_sums(((wg, f_gate, gate[...]), (wu, f_up, up[...])))
    lane = lax.broadcasted_iota(jnp.int32, (1, 128), 1)
    at = pl.ds(pl.multiple_of(step * count, count), count)
    sums[at] = jnp.where(lane == 0, one, jnp.where(lane == 1, two, 0.0))

    @pl.when(step == pl.num_programs(0) - 1)
    def _():
        across = sums[...].T
        gain_one[...] = across[0] / g1[...].astype(F32)
        gain_two[...] = across[1] / g2[...].astype(F32)


def finish(sums, weights, gains, tokens):
    gate, up, down, qkv, out = sums
    rows, hidden, width = gate.shape[0], down.shape[0], out.shape[1]
    steps = next(c for c in (4, 2, 1) if rows % (16 * c) == 0 and hidden % (16 * c) == 0)
    size = tokens[0].shape[0]

    def block(array):
        if array.ndim == 3:
            return pl.BlockSpec((3, array.shape[1] // steps, array.shape[2]), lambda i: (0, i, 0))
        if array.ndim == 1:
            return pl.BlockSpec(array.shape, lambda i: (0,))
        return pl.BlockSpec((array.shape[0] // steps, array.shape[1]), lambda i: (i, 0))

    args = (*sums, *weights, *gains, *tokens)
    square, wide = jax.ShapeDtypeStruct((rows, width), F32), jax.ShapeDtypeStruct(gate.shape, F32)
    flat = jax.ShapeDtypeStruct((rows,), F32)
    outs = [jax.ShapeDtypeStruct(t.shape, t.dtype) for t in tokens]
    outs += [flat] + [square] * 4 + [flat, wide, wide, jax.ShapeDtypeStruct(down.shape, F32)]
    return pl.pallas_call(
        finish_kernel,
        grid=(steps,),
        out_shape=outs,
        in_specs=[block(a) for a in args],
        out_specs=[block(o) for o in outs],
        scratch_shapes=[pltpu.VMEM((rows, 128), F32)],
        compiler_params=pltpu.CompilerParams(vmem_limit_bytes=LIMIT),
        name="finish",
    )(*args)


def rope_table(length, lanes):
    half = HD // 2
    frequency = np.float32(10000.0) ** (-np.arange(half, dtype=np.float32) / np.float32(half))
    angle = np.arange(length, dtype=np.float32)[:, None] * frequency[None, :].astype(np.float32)
    angle = angle.astype(np.float64)
    cos, sin = np.cos(angle), np.sin(angle)
    cos = np.tile(np.concatenate([cos, cos], axis=1), (1, lanes // HD))
    sin = np.tile(np.concatenate([-sin, sin], axis=1), (1, lanes // HD))
    return cos.astype(np.float32), sin.astype(np.float32)


def call(kernel, name, ident, outs, scratch, args, smem=(), far=(), far_outs=(), dmas=(64, 8), limit=LIMIT):
    vmem, smem_spec = pl.BlockSpec(memory_space=pltpu.VMEM), pl.BlockSpec(memory_space=pltpu.SMEM)
    hbm = pl.BlockSpec(memory_space=pl.ANY)
    return pl.pallas_call(
        kernel,
        out_shape=[jax.ShapeDtypeStruct(shape, dtype) for shape, dtype in outs],
        in_specs=[smem_spec if i in smem else hbm if i in far else vmem for i in range(len(args))],
        out_specs=[hbm if i in far_outs else vmem for i in range(len(outs))],
        scratch_shapes=[pltpu.VMEM(shape, dtype) for shape, dtype in scratch]
        + [
            pltpu.SemaphoreType.DMA((dmas[0],)),
            pltpu.SemaphoreType.DMA((dmas[0],)),
            pltpu.SemaphoreType.DMA((dmas[1],)),
        ],
        compiler_params=pltpu.CompilerParams(
            collective_id=ident, has_side_effects=True, vmem_limit_bytes=limit
        ),
        name=name,
    )(*args)


def body(
    tokens,
    value_first,
    window_split,
    cotangent,
    running_grad,
    gain_attn,
    w_query,
    w_key,
    w_value,
    w_out,
    gain_mlp,
    w_gate,
    w_up,
    w_down,
):
    n, copies = lax.axis_size("fsdp"), lax.axis_size("dp")
    size, width = tokens.shape
    length, cols = n * size, width // n
    rows = w_query.shape[0]
    half = rows // 2
    hidden = w_down.shape[0]
    wide = -(-hidden // 128) * 128
    tiles = (cols // HD, n * (n + 1) // 2, size, size)
    cos, sin = (jnp.asarray(t) for t in rope_table(length, 128))
    qkv, probs, att, nrm, mid, nm, wqkv, wgc, wuc, g1_all, g2_all, g_all = call(
        functools.partial(front_kernel, n, copies // 2),
        "front",
        1,
        [
            ((length, 3 * cols), BF),
            (tiles, BF),
            ((length, cols), BF),
            ((length, width), BF),
            ((size, width), F32),
            ((size, width), BF),
            ((width, 3 * cols), BF),
            ((width, wide), BF),
            ((width, wide), BF),
            ((16, width), BF),
            ((16, width), BF),
            ((length, width), BF),
        ],
        [
            ((length, 3 * cols), BF),
            ((length, cols), BF),
            ((length, width), BF),
            ((width, 3 * cols), BF),
            ((width, wide), BF),
            ((width, wide), BF),
            ((length, width), BF),
            (w_gate.shape, BF),
            (w_up.shape, BF),
            ((length, 128), F32),
            ((length, 128), F32),
            ((length, width), BF),
            ((length, cols), BF),
            ((width, width), BF),
            ((size, width), BF),
            ((n, rows, wide), BF),
            ((n, rows, wide), BF),
            (tiles, BF),
        ],
        (
            tokens,
            value_first,
            w_query,
            w_key,
            w_value,
            w_out,
            gain_attn,
            gain_mlp,
            window_split,
            cos,
            sin,
            w_gate,
            w_up,
            cotangent,
        ),
        smem=(8,),
        far=(0, 1, 2, 3, 4, 5, 9, 10, 11, 12, 13),
        far_outs=(0, 1, 2, 3, 6, 7, 8, 11),
        dmas=(256, 32),
    )
    partial, rest, base_out, rest_out, grad_gate, grad_up, grad_down = call(
        functools.partial(middle_kernel, n),
        "middle",
        2,
        [
            ((size, width), F32),
            ((n - 3, size, width), BF),
            ((size, width), F32),
            ((n - 3, size, width), BF),
            ((width, wide), BF),
            ((width, wide), BF),
            ((hidden, width), BF),
        ],
        [
            ((length, width), BF),
            ((length, wide), BF),
            ((length, wide), BF),
            ((length, wide), BF),
            ((length, wide), F32),
            ((length, wide), F32),
            ((wide, width), BF),
            ((3, size, width), BF),
            ((3, size, width), BF),
            ((3, size, width), BF),
            ((3, size, width), BF),
        ],
        (nm, mid, g_all, wgc, wuc, w_down),
        dmas=(48, 8),
    )
    pieces, third = (n, half, wide), (3, n, half, cols)
    ends = [(2, half, n * hidden), (2, half, n * hidden), (2, hidden // 2, width), (3, 2, half, width), (2, cols // 2, width)]
    lines = [pieces, pieces, (hidden // 2, width), third, (cols // 2, width)]
    layer_out, input_grad, first_grad, sum_gate, sum_up, sum_down, sum_qkv, sum_out = call(
        functools.partial(back_kernel, n, copies // 2),
        "back",
        3,
        [((size, width), BF), ((size, width), F32), ((size, width), F32)] + [(e, BF) for e in ends],
        [
            ((n - 3, size, width), BF),
            ((size, width), BF),
            ((length, 3 * cols), BF),
            (tiles, BF),
            ((length, cols), BF),
            ((length, width), BF),
            ((width, 3 * cols), BF),
            ((cols, width), BF),
            ((length, 128), F32),
            ((length, 128), F32),
            ((16, width), BF),
            ((size, width), F32),
            ((length, width), BF),
            ((length, cols), F32),
            ((length, cols), F32),
            ((length, 3 * cols), BF),
            ((size, width), BF),
            ((n, size, width), BF),
            ((n, size, width), BF),
            ((size, width), F32),
            ((3, width, cols), BF),
            ((2, cols // 2, width), BF),
        ]
        + [(e, BF) for e in ends]
        + [(shape, BF) for shape in (pieces, pieces, lines[2], third, lines[4])]
        + [(shape, BF) for shape in lines * 2]
        + [(pieces, BF), (pieces, BF), (third, BF), (pieces, BF), (pieces, BF)],
        (
            rest,
            partial,
            mid,
            cotangent,
            g2_all,
            window_split,
            tokens,
            qkv,
            probs,
            att,
            nrm,
            wqkv,
            w_out,
            cos,
            sin,
            running_grad,
            g1_all,
            base_out,
            rest_out,
            grad_gate.reshape(n, 2, half, wide),
            grad_up.reshape(n, 2, half, wide),
            grad_down.reshape(2, hidden // 2, width),
        ),
        smem=(5,),
        far=(0, *range(6, 22)),
        far_outs=range(3, 8),
        dmas=(160, 32),
    )
    sums = (
        sum_gate.reshape(rows, -1),
        sum_up.reshape(rows, -1),
        sum_down.reshape(hidden, width),
        sum_qkv.reshape(3, rows, width),
        sum_out.reshape(rows, width),
    )
    return tuple(
        finish(
            sums,
            (w_gate, w_up, w_query, w_key, w_value),
            (gain_attn, gain_mlp),
            (layer_out, input_grad, first_grad),
        )
    )


def solution(mesh):
    token, flat, matrix = P(("dp", "fsdp"), None), P("fsdp"), P("fsdp", None)
    return jax.shard_map(
        body,
        mesh=mesh,
        in_specs=(token, token, P("dp"), token, token, flat)
        + (matrix,) * 4
        + (flat,)
        + (matrix,) * 3,
        out_specs=(token, token, token, flat) + (matrix,) * 4 + (flat,) + (matrix,) * 3,
        check_vma=False,
    )
```

```python
import functools

import jax
import jax.numpy as jnp
import numpy as np
from jax import lax
from jax.experimental import pallas as pl
from jax.experimental.pallas import tpu as pltpu
from jax.sharding import PartitionSpec as P

HD = 64
EPS = 1e-06
MESH = pl.DeviceIdType.MESH
BF = jnp.bfloat16
F32 = jnp.float32
LIMIT = 60 * 1024 * 1024


def dot_nn(a, b):
    return lax.dot_general(a, b, (((1,), (0,)), ((), ())), preferred_element_type=F32)


def dot_nt(a, b):
    return lax.dot_general(a, b, (((1,), (1,)), ((), ())), preferred_element_type=F32)


def dot_tn(a, b):
    return lax.dot_general(a, b, (((0,), (0,)), ((), ())), preferred_element_type=F32)


def flip(f, k, n):
    out, bit = 0, 1
    while bit < n:
        have, want = lax.rem(f // bit, 2), (k // bit) % 2
        out = out + (1 - have if want else have) * bit
        bit *= 2
    return out


class Net:
    def __init__(self, n, ssem, rsem, lsem=None):
        self.n, self.ssem, self.rsem, self.lsem = n, ssem, rsem, lsem
        self.d, self.f = lax.axis_index("dp"), lax.axis_index("fsdp")
        self.c = lax.rem(self.d, 2)
        self.mate = (self.d + 1 - 2 * self.c, self.f)
        self.used, self.lused, self.sent = 0, 0, []

    def peer(self, k):
        return (self.d, flip(self.f, k, self.n))

    def take(self, count=1):
        self.used += count
        return self.used - count

    def push(self, src, dst, device, slot=None):
        slot = self.take() if slot is None else slot
        copy = pltpu.make_async_remote_copy(
            src_ref=src,
            dst_ref=dst,
            send_sem=self.ssem.at[slot],
            recv_sem=self.rsem.at[slot],
            device_id=device,
            device_id_type=MESH,
        )
        copy.start()
        self.sent.append(copy)
        return copy

    def local(self, src, dst):
        copy = pltpu.make_async_copy(src, dst, self.lsem.at[self.lused])
        self.lused += 1
        copy.start()
        return copy

    def barrier(self, devices):
        sem = pltpu.get_barrier_semaphore()
        for device in devices:
            pl.semaphore_signal(sem, inc=1, device_id=device, device_id_type=MESH)
        pl.semaphore_wait(sem, len(devices))

    def drain(self):
        for copy in self.sent:
            copy.wait_send()


def rows_of(ref, block, size):
    return ref.at[pl.ds(pl.multiple_of(block * size, size), size)]


class Gather:
    def __init__(self, net, own, into, size):
        self.net, self.into, self.size = net, into, size
        self.direct = [1, 2] if net.n == 4 else list(range(1, net.n))
        self.copies = {k: net.push(own, rows_of(into, net.f, size), net.peer(k)) for k in self.direct}
        self.halves = {}

    def part(self, block, half):
        start = pl.multiple_of(block * self.size + half * (self.size // 2), self.size // 2)
        return self.into.at[pl.ds(start, self.size // 2)]

    def wait(self, k):
        net = self.net
        if k in self.copies:
            self.copies[k].wait_recv()
            if net.n == 4:
                part = self.part(flip(net.f, k, 4), k - 1)
                self.halves[k] = net.push(part, part, net.peer(3 - k))
        else:
            for copy in self.halves.values():
                copy.wait_recv()


def lane_mask(width, head):
    lane = lax.broadcasted_iota(jnp.int32, (1, width), 1)
    return (lane // HD) == head


def turn(values, cos, sin):
    width = values.shape[1]
    lane = lax.broadcasted_iota(jnp.int32, (1, width), 1)
    first = lax.rem(lane, HD) < HD // 2
    other = jnp.where(
        first, pltpu.roll(values, width - HD // 2, 1), pltpu.roll(values, HD // 2, 1)
    )
    return values * cos + other * sin


def table_rows(net, cos_ref, sin_ref, flag, start, size, length, width):
    half = length // 2
    plain = pl.ds(pl.multiple_of(start, size), size)
    split = pl.ds(pl.multiple_of(lax.rem(start, half), size), size)
    out = []
    for ref in (cos_ref, sin_ref):
        rows = jnp.where(flag == 1, ref[split], ref[plain])
        out.append(jnp.concatenate([rows] * (width // rows.shape[1]), axis=1))
    return out


def block_bias(flag, r, kb, size, length):
    half = length // 2
    if kb == r:
        row = lax.broadcasted_iota(jnp.int32, (size, size), 0)
        col = lax.broadcasted_iota(jnp.int32, (size, size), 1)
        return jnp.where(col <= row, 0.0, -1e30)
    if (r * size >= half) != (kb * size >= half):
        return jnp.where(flag == 1, -1e30, 0.0)
    return None


def scores_of(query, key, bias):
    scores = dot_nt(query, key)
    return scores if bias is None else scores + bias


def factor_of(hidden):
    return lax.rsqrt(jnp.mean(hidden * hidden, axis=-1, keepdims=True) + EPS)


def norm_back(hidden, gain, grad):
    factor = factor_of(hidden)
    scaled = grad * gain
    return factor * scaled - hidden * (factor * factor * factor) * jnp.mean(
        scaled * hidden, axis=-1, keepdims=True
    )


class Agenda:
    def __init__(self):
        self.clock, self.items = 0.0, []

    def at(self, time, step):
        self.items.append((time, len(self.items), step))

    def until(self, time):
        self.clock = max(self.clock, time)
        due = sorted(item for item in self.items if item[0] <= self.clock)
        self.items = [item for item in self.items if item[0] > self.clock]
        for _, _, step in due:
            step()

    def spend(self, time):
        self.until(self.clock + time)


class Spread:
    def __init__(self, net, chips, rows, sources):
        self.net, self.rows = net, rows
        self.chip = net.d // 2
        self.chips = chips if rows % (32 * chips) == 0 else 1
        self.share = rows // (2 * self.chips)
        self.part = self.chip if self.chips > 1 else 0
        n = net.n
        self.right, self.left, self.mate = (net.take(self.chips * (n - 1)) for _ in range(3))
        self.into = sources[0][2]
        self.first = []
        for k in range(1, n):
            to = net.peer(k)
            for piece, place, _ in sources:
                mine = pl.ds(self.start(0, self.part, net.c), self.share)
                here = pl.ds(self.start(net.f, self.part, net.c), self.share)
                self.first.append(net.push(piece(to[1]).at[mine], place.at[here], to))

    def start(self, block, part, core):
        return pl.multiple_of(block * self.rows + (2 * part + core) * self.share, self.share)

    def view(self, k, part, core):
        return self.into.at[pl.ds(self.start(flip(self.net.f, k, self.net.n), part, core), self.share)]

    def copy(self, k, part, base, device):
        net = self.net
        slot = base + part * (net.n - 1) + k - 1
        view = self.view(k, part, net.c)
        return pltpu.make_async_remote_copy(
            src_ref=view,
            dst_ref=view,
            send_sem=net.ssem.at[slot],
            recv_sem=net.rsem.at[slot],
            device_id=device,
            device_id_type=MESH,
        )

    def along(self, step):
        return ((self.chip + step) * 2 + self.net.c, self.net.f)

    def pass_on(self, part, base, step, room):
        @pl.when(room)
        def _():
            for k in range(1, self.net.n):
                self.copy(k, part, base, self.along(step)).start()

    def own(self):
        for copy in self.first:
            copy.wait_recv()
        if self.chips > 1:
            self.pass_on(self.part, self.right, 1, self.chip + 1 < self.chips)
            self.pass_on(self.part, self.left, -1, self.chip > 0)
        for k in range(1, self.net.n):
            self.copy(k, self.part, self.mate, self.net.mate).start()

    def hop(self, j):
        if j >= self.chips:
            return
        for base, step in ((self.right, 1), (self.left, -1)):
            part = self.part - step * j

            @pl.when((part >= 0) & (part < self.chips))
            def _(base=base, step=step, part=part):
                for k in range(1, self.net.n):
                    self.copy(k, part, base, self.net.mate).wait_recv()
                room = self.chip + 1 < self.chips if step == 1 else self.chip > 0
                self.pass_on(part, base, step, room)
                for k in range(1, self.net.n):
                    self.copy(k, part, self.mate, self.net.mate).start()

    def finish(self):
        n = self.net.n
        for part in range(self.chips):
            for k in range(1, n):
                self.copy(k, part, self.mate, self.net.mate).wait()
            if self.chips > 1:

                @pl.when((part <= self.chip) & (self.chip + 1 < self.chips))
                def _(part=part):
                    for k in range(1, n):
                        self.copy(k, part, self.right, self.net.mate).wait_send()

                @pl.when((part >= self.chip) & (self.chip > 0))
                def _(part=part):
                    for k in range(1, n):
                        self.copy(k, part, self.left, self.net.mate).wait_send()


def gain_rows(net, src, dst, rows):
    place = dst.at[:, pl.ds(pl.multiple_of(net.f * rows, rows), rows)]
    dst[:, pl.ds(pl.multiple_of(net.f * rows, rows), rows)] = jnp.broadcast_to(src[...].reshape(1, rows), (16, rows))
    return [net.push(place, place, net.peer(k)) for k in range(1, net.n)]


def send_to(net, r, src, dst, base, away=None):
    return pltpu.make_async_remote_copy(
        src_ref=src,
        dst_ref=dst,
        send_sem=net.ssem.at[base + r],
        recv_sem=net.rsem.at[base + (net.f if away is None else away)],
        device_id=(net.d, r),
        device_id_type=MESH,
    )


def front_kernel(
    n,
    chips,
    x,
    vf,
    wq,
    wk,
    wv,
    wo,
    g1,
    g2,
    flag_ref,
    cos_hbm,
    sin_hbm,
    wg_hbm,
    wu_hbm,
    ct,
    qkv_out,
    probs,
    att_out,
    nrm_out,
    mid,
    nm,
    wqkv_out,
    wgc_out,
    wuc_out,
    g1_all,
    g2_all,
    g_out,
    qkv,
    att,
    nrm,
    wqkv,
    wgc,
    wuc,
    g_all,
    wg,
    wu,
    cos_ref,
    sin_ref,
    x_all,
    vfc,
    wo_all,
    att_own,
    wgr,
    wur,
    low_probs,
    ssem,
    rsem,
    lsem,
):
    net = Net(n, ssem, rsem, lsem)
    size, width = x.shape
    length = n * size
    cols = width // n
    rows = wq.shape[0]
    hidden = wg.shape[1] // n
    flag = flag_ref[0]
    chip = net.d // 2
    sem = pltpu.get_barrier_semaphore()
    near = [net.peer(k) for k in range(1, n)] + [net.mate]
    for device in near:
        pl.semaphore_signal(sem, inc=1, device_id=device, device_id_type=MESH)
    for step, room in ((1, chip + 1 < chips), (-1, chip > 0)):
        @pl.when(room)
        def _(step=step):
            device = ((chip + step) * 2 + net.c, net.f)
            pl.semaphore_signal(sem, inc=1, device_id=device, device_id_type=MESH)

    edge = (chip == 0) | (chip == chips - 1)

    @pl.when(edge)
    def _():
        pl.semaphore_wait(sem, len(near) + min(chips - 1, 1))

    @pl.when(jnp.logical_not(edge))
    def _():
        pl.semaphore_wait(sem, len(near) + 2)

    mine = pl.ds(pl.multiple_of(net.f * cols, cols), cols)
    sources = []
    for i, w in enumerate((wq, wk, wv)):
        piece = lambda to, w=w: w.at[:, pl.ds(pl.multiple_of(to * cols, cols), cols)]
        sources.append((piece, wqkv.at[:, pl.ds(i * cols, cols)], wqkv))
    spread_qkv = Spread(net, chips, rows, sources)
    gains = gain_rows(net, g1, g1_all, rows) + gain_rows(net, g2, g2_all, rows)
    x_gather = Gather(net, x, x_all, size)
    values = []
    for k in range(1, n):
        device = net.peer(k)
        src = vf.at[:, pl.ds(pl.multiple_of(device[1] * cols, cols), cols)]
        values.append(net.push(src, rows_of(vfc, net.f, size), device))
    spread_out = Spread(net, chips, rows, [(lambda to: wo, wo_all, wo_all)])
    own_x = net.local(x, rows_of(x_all, net.f, size))
    halves = [net.local(wg_hbm, wg), net.local(wu_hbm, wu)]
    locals_ = [net.local(vf.at[:, mine], rows_of(vfc, net.f, size))]
    for i, w in enumerate((wq, wk, wv)):
        into = rows_of(wqkv.at[:, pl.ds(i * cols, cols)], net.f, rows)
        locals_.append(net.local(w.at[:, mine], into))
    locals_.append(net.local(wo, rows_of(wo_all, net.f, rows)))
    locals_.append(net.local(ct, rows_of(g_all, net.f, size)))
    locals_ += [net.local(cos_hbm, cos_ref), net.local(sin_hbm, sin_ref)]
    stores = []
    agenda = Agenda()

    def plan(spread, begin, time):
        agenda.at(begin, spread.own)
        for j in range(1, chips):
            agenda.at(begin + j * time + 0.5, functools.partial(spread.hop, j))

    plan(spread_qkv, 8, 3.6)
    plan(spread_out, 19, 4.4)
    for copy in halves:
        copy.wait()
    for w, piece, into in ((wg, wgr, wgc), (wu, wur, wuc)):
        for r in range(n):
            piece[r, :, :hidden] = w[:, r * hidden : (r + 1) * hidden]
        if piece.shape[2] > hidden:
            piece[:, :, hidden:] = jnp.zeros((n, rows, piece.shape[2] - hidden), BF)
        into[pl.ds(pl.multiple_of(net.f * rows, rows), rows)] = piece[net.f]
    for copy in gains:
        copy.wait_recv()
    agenda.until(8)
    spread_gate = Spread(net, chips, rows, [(lambda to: wgr.at[to], wgc, wgc)])
    spread_up = Spread(net, chips, rows, [(lambda to: wur.at[to], wuc, wuc)])
    plan(spread_gate, 31, 3.4)
    plan(spread_up, 40, 3.4)
    own_x.wait()
    gain = g1_all[0:1, :].astype(F32)

    def normalize(block):
        at = pl.ds(pl.multiple_of(block * size, size), size)
        rows_in = x_all[at].astype(F32)
        nrm[at] = (rows_in * factor_of(rows_in) * gain).astype(BF)

    normalize(net.f)
    agenda.until(16)
    for k in range(1, n - 1):
        x_gather.wait(k)
        normalize(flip(net.f, k, n))
    for copy in locals_:
        copy.wait()
    agenda.until(26)
    x_gather.wait(n - 1)
    normalize(flip(net.f, n - 1, n))
    stores.append(net.local(nrm, nrm_out))
    spreads = [spread_out, spread_gate, spread_up]
    spread_qkv.finish()
    stores.append(net.local(wqkv, wqkv_out))
    for copy in values:
        copy.wait_recv()
    g_gather = Gather(net, ct, g_all, size)
    agenda.until(31)

    @pl.loop(0, n)
    def _(block):
        at = pl.ds(pl.multiple_of(block * size, size), size)
        pre = dot_nn(nrm[at], wqkv[...])
        cos, sin = table_rows(net, cos_ref, sin_ref, flag, block * size, size, length, 2 * cols)
        turned = turn(pre[:, : 2 * cols], cos, sin)
        mixed = 0.5 * pre[:, 2 * cols :] + 0.5 * vfc[at].astype(F32)
        qkv[at, :cols] = (turned[:, :cols] * HD**-0.5).astype(BF)
        qkv[at, cols : 2 * cols] = turned[:, cols:].astype(BF)
        qkv[at, 2 * cols :] = mixed.astype(BF)

    agenda.spend(2.5)
    stores.append(net.local(qkv, qkv_out))
    heads = cols // HD
    base = net.take(n)
    for r in range(n):
        at = slice(r * size, (r + 1) * size)
        query = qkv[at, :cols]
        total = jnp.zeros((size, cols), F32)
        biases = [block_bias(flag, r, kb, size, length) for kb in range(r + 1)]
        for h in range(heads):
            mask = lane_mask(cols, h)
            masked = jnp.where(mask, query, jnp.zeros_like(query))
            tiles = [
                scores_of(masked, qkv[kb * size : (kb + 1) * size, cols : 2 * cols], biases[kb])
                for kb in range(r + 1)
            ]
            top = tiles[0].max(axis=1, keepdims=True)
            for tile in tiles[1:]:
                top = jnp.maximum(top, tile.max(axis=1, keepdims=True))
            raw = [jnp.exp(tile - top) for tile in tiles]
            whole = raw[0].sum(axis=1, keepdims=True)
            for tile in raw[1:]:
                whole = whole + tile.sum(axis=1, keepdims=True)
            inverse = 1.0 / whole
            mixed = None
            for kb, tile in enumerate(raw):
                low = (tile * inverse).astype(BF)
                low_probs[h, r * (r + 1) // 2 + kb] = low
                term = dot_nn(low, qkv[kb * size : (kb + 1) * size, 2 * cols :])
                mixed = term if mixed is None else mixed + term
            total = jnp.where(mask, mixed, total)
        done = pl.ds(r * (r + 1) // 2, r + 1)
        stores.append(net.local(low_probs.at[:, done], probs.at[:, done]))
        att[at] = total.astype(BF)

        @pl.when(net.f == r)
        def _():
            att_own[:, mine] = att[at]

        @pl.when(net.f != r)
        def _():
            send_to(net, r, att.at[pl.ds(r * size, size)], att_own.at[:, mine], base).start()

        agenda.spend(1.2 * (r + 1))
        if r == n - 2:
            for k in (1, 2):
                g_gather.wait(k)
    agenda.spend(100.0)
    stores.append(net.local(att, att_out))
    spread_out.finish()
    rows_at = pl.ds(pl.multiple_of(net.f * size, size), size)
    for k in range(1, n):
        other = flip(net.f, k, n)
        place = att_own.at[:, pl.ds(pl.multiple_of(other * cols, cols), cols)]
        src = rows_of(att, other, size)
        send_to(net, other, src, place, base, other).wait()
    sums = x_all[rows_at].astype(F32) + dot_nn(att_own[...], wo_all[...])
    mid[...] = sums
    nm[...] = (sums * factor_of(sums) * g2_all[0:1, :].astype(F32)).astype(BF)
    for spread, into, out in ((spread_gate, wgc, wgc_out), (spread_up, wuc, wuc_out)):
        spread.finish()
        stores.append(net.local(into, out))
    for k in range(3, n):
        g_gather.wait(k)
    stores.append(net.local(g_all, g_out))
    for copy in stores:
        copy.wait()
    net.drain()


class Line:
    def __init__(self, net, chips):
        chip, middle = net.d // 2, chips // 2
        left = chip < middle
        inward = jnp.where(left, chip + 1, chip - 1)
        outward = jnp.where(left, chip - 1, chip + 1)
        self.net, self.chip, self.first_middle = net, chip, middle - 1
        self.edge = (chip == 0) | (chip == chips - 1)
        self.middle = (chip == middle - 1) | (chip == middle)
        self.inner = (inward * 2 + net.c, net.f)
        self.outer = (outward * 2 + net.c, net.f)
        self.chunks, self.paced, self.middle_ends = [], set(), chips == 2

    def barrier(self, others):
        net, sem = self.net, pltpu.get_barrier_semaphore()
        fixed = others + [self.inner]
        for device in fixed:
            pl.semaphore_signal(sem, inc=1, device_id=device, device_id_type=MESH)

        @pl.when(jnp.logical_not(self.edge))
        def _():
            pl.semaphore_signal(sem, inc=1, device_id=self.outer, device_id_type=MESH)
            pl.semaphore_wait(sem, len(fixed) + 1)

        @pl.when(self.edge)
        def _():
            pl.semaphore_wait(sem, len(fixed))

    def chunk(self, own, outer, total, deliver=None, kind="whole"):
        self.chunks.append((own, outer, total, deliver, kind, [self.net.take() for _ in range(3)]))
        return len(self.chunks) - 1

    def copy(self, src, dst, send, recv, device):
        return pltpu.make_async_remote_copy(
            src_ref=src,
            dst_ref=dst,
            send_sem=self.net.ssem.at[send],
            recv_sem=self.net.rsem.at[recv],
            device_id=device,
            device_id_type=MESH,
        )

    def inwards(self, i):
        own, outer, total, _, _, (up, down, _) = self.chunks[i]

        @pl.when(jnp.logical_not(self.edge))
        def _():
            self.copy(own, outer, up, up, self.outer).wait_recv()
            own[...] = own[...] + outer[...]

        if self.chunks[i][4] == "near":

            @pl.when(self.middle)
            def _():
                total[...] = own[...]

        else:
            self.exchange(i)

        @pl.when(jnp.logical_not(self.middle))
        def _():
            self.copy(own, outer, up, up, self.inner).start()

    def exchange(self, i):
        own, _, total, _, _, (_, down, _) = self.chunks[i]

        @pl.when(self.middle)
        def _():
            self.copy(own, total, down, down, self.inner).start()

    def pace(self, i):
        own, outer, _, _, _, (up, _, _) = self.chunks[i]
        self.paced.add(i)
        if not self.middle_ends:
            self.copy(own, outer, up, up, self.inner).wait_send()

    def meet(self, i):
        own, _, total, _, _, (_, down, _) = self.chunks[i]

        @pl.when(self.middle)
        def _():
            self.copy(own, total, down, down, self.inner).wait_recv()
            total[...] = own[...] + total[...]

    def outwards(self, i):
        _, _, total, deliver, kind, (_, down, away) = self.chunks[i]
        if kind in ("whole", "far"):
            self.meet(i)

        @pl.when(jnp.logical_not(self.middle))
        def _():
            self.copy(total, total, down, down, self.inner).wait_recv()

        @pl.when(jnp.logical_not(self.edge))
        def _():
            self.copy(total, total, away, down, self.outer).start()

        deliver()

    def finish(self):
        for i, (own, _, total, _, kind, (up, down, away)) in enumerate(self.chunks):
            if kind != "part":
                slot = jnp.where(self.middle, down, up)
                sent = jnp.logical_not(self.edge) | self.middle if i in self.paced else self.chip >= 0
                if kind == "near":
                    sent = sent & jnp.logical_not(self.middle)
                if kind == "far":
                    sent = self.middle

                @pl.when(sent)
                def _():
                    self.copy(own, total, slot, down, self.inner).wait_send()

            if kind not in ("meet", "near"):

                @pl.when(jnp.logical_not(self.edge))
                def _():
                    self.copy(total, total, away, down, self.outer).wait_send()


def cut(size):
    if size % 32 == 0:
        return [(0, size // 2), (size // 2, size // 2)]
    return [(0, size)]


def middle_kernel(
    n,
    chips,
    nm,
    mid,
    g_hbm,
    wgc_hbm,
    wuc_hbm,
    wd,
    partial,
    rest,
    base_out,
    rest_out,
    out_gate,
    out_up,
    total_down,
    g_all,
    wgc,
    wuc,
    grad_gate,
    grad_up,
    grad_down,
    m_down,
    l_down,
    o_down,
    nm_all,
    hid_all,
    gg_all,
    ug_all,
    coef,
    silus,
    wd_wide,
    sb1,
    rb1,
    relayed,
    sb2,
    rb2,
    ssem,
    rsem,
    lsem,
):
    net = Net(n, ssem, rsem, lsem)
    size, width = nm.shape
    line = Line(net, chips)
    line.barrier([net.peer(k) for k in range(1, n)] + [net.mate])

    @pl.when(jnp.logical_not(line.middle))
    def _():
        total_down[...] = jnp.zeros_like(total_down)

    gather = Gather(net, nm, nm_all, size)
    hidden = wd.shape[0]
    loads = [
        net.local(nm, rows_of(nm_all, net.f, size)),
        net.local(wgc_hbm, wgc),
        net.local(wuc_hbm, wuc),
        net.local(wd, wd_wide.at[pl.ds(0, hidden)]),
        net.local(g_hbm, g_all),
    ]
    if wd_wide.shape[0] > hidden:
        wd_wide[hidden:] = jnp.zeros((wd_wide.shape[0] - hidden, width), BF)

    def rows_at(k):
        return pl.ds(pl.multiple_of(flip(net.f, k, n) * size, size), size)

    def forward(k):
        at = rows_at(k)
        a = nm_all[at]
        gate = dot_nn(a, wgc[...])
        up = dot_nn(a, wuc[...])
        sig = jax.nn.sigmoid(gate)
        silu = gate * sig
        hid_all[at] = (silu * up).astype(BF)
        coef[at] = up * sig * (1.0 + gate * (1.0 - sig))
        silus[at] = silu
        part = dot_nn(hid_all[at], wd_wide[...])
        if k == 0:
            base_out[...] = mid[...] + part
        elif k < 3:
            sb1[k] = part.astype(BF)
        else:
            rest_out[k - 3] = part.astype(BF)
            if n == 4:
                for j in (1, 2):
                    part = pl.ds((j - 1) * (size // 2), size // 2)
                    relays.append(net.push(rest_out.at[0, part], relayed.at[j], net.peer(j)))

    soon, relays = [], []

    def backward(k):
        at = rows_at(k)
        grad = dot_nt(g_all[at], wd_wide[...])
        gg_all[at] = (grad * coef[at]).astype(BF)
        ug_all[at] = (grad * silus[at]).astype(BF)
        back = dot_nt(gg_all[at], wgc[...]) + dot_nt(ug_all[at], wuc[...])
        if k == 0:
            partial[...] = back
        elif k < 3:
            sb2[k] = back.astype(BF)
            soon.append((k, net.push(sb2.at[k], rb2.at[k], net.peer(k))))
        else:
            rest[k - 3] = back.astype(BF)

    for copy in loads:
        copy.wait()
    forward(0)
    backward(0)
    tile = 256 if width % 256 == 0 else width

    def columns(i):
        return pl.ds(pl.multiple_of(i * tile, tile), tile)

    def down_terms():
        for start in range(0, width, tile):
            at = slice(start, start + tile)
            grad = dot_tn(hid_all[...], g_all[:, at])[:hidden].astype(BF)
            grad_down[:, :, at] = grad.reshape(2, hidden // 2, tile)
        return net.push(grad_down.at[1 - net.c], m_down, net.mate)

    for k in range(1, n):
        gather.wait(k)
        for j in ([1] if k == 2 or n == 2 else []) + ([k] if k >= 2 else []):
            forward(j)
            if j == n - 1:
                mate = down_terms()
            backward(j)
    mate.wait_recv()
    l_down[...] = grad_down[net.c] + m_down[...]
    downs = []
    for start, count in cut(l_down.shape[0]):
        at = pl.ds(start, count)
        kind = "near" if downs else "meet"
        downs.append(line.chunk(l_down.at[at], o_down.at[at], total_down.at[at], kind=kind))

    @pl.when(line.edge)
    def _():
        line.inwards(downs[0])

    for j, copy in enumerate(relays, 1):
        copy.wait_recv()
        at = slice((j - 1) * (size // 2), j * (size // 2))
        sb1[3 - j, at] = (sb1[3 - j, at].astype(F32) + relayed[j].astype(F32)).astype(BF)
    late = [(k, net.push(sb1.at[k], rb1.at[k], net.peer(k))) for k in range(1, 3)]

    @pl.loop(0, width // tile)
    def _(i):
        grad_gate[columns(i)] = dot_tn(nm_all[:, columns(i)], gg_all[...]).astype(BF)

    stores = [net.local(grad_gate, out_gate)]

    @pl.loop(0, width // tile)
    def _(i):
        grad_up[columns(i)] = dot_tn(nm_all[:, columns(i)], ug_all[...]).astype(BF)

    stores.append(net.local(grad_up, out_up))

    @pl.when(line.edge)
    def _():
        for before, i in zip(downs, downs[1:]):
            line.pace(before)
            line.inwards(i)

    @pl.when(jnp.logical_not(line.edge))
    def _():
        for i in downs:
            line.inwards(i)

    grad = partial[...]
    for k, copy in soon:
        copy.wait_recv()
        grad = grad + rb2[k].astype(F32)
    partial[...] = grad
    result = base_out[...]
    for k, copy in late:
        copy.wait_recv()
        result = result + rb1[k].astype(F32)
    base_out[...] = result
    line.meet(downs[0])
    line.finish()
    for copy in stores:
        copy.wait()
    net.drain()


class Swap:
    def __init__(self, net, line, total, place, done, settle=None):
        self.net, self.line, self.total, self.place = net, line, total, place
        self.done, self.settle = done, settle
        self.base = net.take(net.n)

    def copy(self, k):
        to = self.net.peer(k)
        slot = self.base + k
        return self.line.copy(self.total(to[1]), self.place(self.net.f), slot, slot, to)

    def start(self):
        for k in range(1, self.net.n):
            self.copy(k).start()
        self.place(self.net.f)[...] = self.total(self.net.f)[...]

    def end(self):
        for k in range(1, self.net.n):
            self.copy(k).wait()
        if self.settle is not None:
            self.settle()


def back_kernel(
    n,
    chips,
    rest,
    partial,
    mid,
    ct,
    g2_all,
    flag_ref,
    x_hbm,
    qkv_hbm,
    probs_hbm,
    att_hbm,
    nrm_hbm,
    wqkv_hbm,
    wo_hbm,
    cos_hbm,
    sin_hbm,
    rg_hbm,
    g1_hbm,
    base_hbm,
    rest_out,
    grad_gate,
    grad_up,
    down_hbm,
    layer_out,
    input_grad,
    first_grad,
    out_gate,
    out_up,
    out_down,
    out_qkv,
    out_out,
    rest_in,
    x,
    qkv,
    probs,
    att,
    nrm,
    wqkv,
    wo,
    cos_ref,
    sin_ref,
    g1_all,
    base_out,
    gb_all,
    dk,
    dv,
    dqkv,
    vg,
    sb,
    rb,
    own,
    grad_qkv,
    grad_out,
    sum_gate,
    sum_up,
    sum_down,
    sum_qkv,
    sum_out,
    m_gate,
    m_up,
    m_qkv,
    m_out,
    l_gate,
    l_up,
    t_down,
    l_qkv,
    l_out,
    o_gate,
    o_up,
    o_qkv,
    o_out,
    t_gate,
    t_up,
    t_qkv,
    a_gate,
    a_up,
    ssem,
    rsem,
    lsem,
):
    net = Net(n, ssem, rsem, lsem)
    line = Line(net, chips)
    size, width = ct.shape
    length = n * size
    cols = width // n
    heads = cols // HD
    half, hidden = m_gate.shape[1], sum_gate.shape[2] // n
    flag = flag_ref[0]
    line.barrier([net.peer(k) for k in range(1, n)] + [net.mate])
    rests = [net.push(rest.at[k - 3], rest_in.at[k - 3], net.peer(k)) for k in range(3, n)]
    mates = [
        net.push(grad_gate.at[:, 1 - net.c], m_gate, net.mate),
        net.push(grad_up.at[:, 1 - net.c], m_up, net.mate),
    ]
    halves = [
        net.local(grad_gate.at[:, net.c], l_gate),
        net.local(grad_up.at[:, net.c], l_up),
    ]
    down_load = net.local(down_hbm, t_down)
    early = [
        net.local(src, dst)
        for src, dst in (
            (qkv_hbm, qkv),
            (wo_hbm, wo),
            (probs_hbm, probs),
            (cos_hbm, cos_ref),
            (sin_hbm, sin_ref),
            (wqkv_hbm, wqkv),
            (att_hbm, att),
        )
    ]
    later = [
        net.local(src, dst)
        for src, dst in (
            (nrm_hbm, nrm),
            (x_hbm, x),
            (g1_hbm, g1_all),
            (rg_hbm, first_grad),
            (base_hbm, base_out),
        )
    ]
    dk[...] = jnp.zeros_like(dk)
    dv[...] = jnp.zeros_like(dv)
    finals = []

    def to_mate(place):
        slot = net.take()
        finals.append((slot, place))
        return lambda: line.copy(place(net.c), place(net.c), slot, slot, net.mate).start()

    agenda = Agenda()
    hop = 8.2

    def edge_only(time, step, i):
        def run():
            @pl.when(line.edge)
            def _():
                step(i)

        agenda.at(time, run)

    def rest_only(time, step, i):
        def run():
            @pl.when(jnp.logical_not(line.edge))
            def _():
                step(i)

        agenda.at(time, run)

    def launch(i, before):
        if before is not None:
            line.pace(before)
        line.inwards(i)

    def plan(i, start, time, before):
        edge_only(start, functools.partial(launch, before=before), i)
        rest_only(start + time + 3, line.inwards, i)
        rest_only(start + 2 * time + 6, line.outwards, i)
        edge_only(start + 3 * time + 11, line.outwards, i)

    arrivals = []

    def change_over(swap, place):
        send = to_mate(place)

        def arrive():
            swap.end()
            send()

        arrivals.append(arrive)
        return swap.start

    def spread_rows(t, a, total, at, rows):
        def settle():
            for r in range(n):
                total[net.c, rows, r * hidden : (r + 1) * hidden] = a[r, rows, :hidden]

        return Swap(net, line, lambda r: t.at[r, at], lambda f: a.at[f, at], total.at[net.c, at], settle)

    down_load.wait()

    for start, count in cut(t_down.shape[0]):
        at = pl.ds(start, count)
        place = lambda c, at=at: sum_down.at[c, at]
        kind = "far" if start else "part"
        down = line.chunk(t_down.at[at], None, place(net.c), to_mate(place), kind)
        if start:
            line.exchange(down)
        else:

            @pl.when(line.middle)
            def _(at=at, place=place):
                place(net.c)[...] = t_down[at]

        rest_only(17 if start else 8, line.outwards, down)
        edge_only(34, line.outwards, down)
    begin, before = 9.0, None
    for mate, load, l, m, o, t, a, total in zip(
        mates,
        halves,
        (l_gate, l_up),
        (m_gate, m_up),
        (o_gate, o_up),
        (t_gate, t_up),
        (a_gate, a_up),
        (sum_gate, sum_up),
    ):
        load.wait()
        mate.wait_recv()
        l[...] = l[...] + m[...]
        for start, count in cut(half):
            at, rows = pl.ds(start, count), slice(start, start + count)
            place = lambda c, at=at, total=total: total.at[c, at]
            swap = spread_rows(t, a, total, at, rows)
            i = line.chunk(l.at[:, at], o.at[:, at], t.at[:, at], change_over(swap, place))
            plan(i, begin, hop, before)
            begin, before = begin + hop, i
        agenda.until(9)
    grad = partial[...]
    for i, copy in enumerate(rests):
        copy.wait_recv()
        grad = grad + rest_in[i].astype(F32)
    total = ct[...].astype(F32) + norm_back(mid[...], g2_all[0:1, :].astype(F32), grad)
    input_grad[...] = total
    gb_all[pl.ds(pl.multiple_of(net.f * size, size), size)] = total.astype(BF)
    gather = Gather(net, rows_of(gb_all, net.f, size), gb_all, size)
    for copy in early:
        copy.wait()
    agenda.until(17)
    agenda.until(25)
    for k in range(1, n - 1):
        gather.wait(k)
    agenda.until(29)
    gather.wait(n - 1)
    late = [(k, net.push(rest_out.at[k - 3], rest_in.at[k - 3], net.peer(k))) for k in range(3, n) if n != 4]
    agenda.until(34)

    base = net.take(n)
    value_base = net.take(n)

    def attend(r):
        at = slice(r * size, (r + 1) * size)
        query = qkv[at, :cols]
        grad = dot_nt(gb_all[at], wo[...]).astype(BF)
        total = jnp.zeros((size, cols), F32)
        for h in range(heads):
            mask = lane_mask(cols, h)
            qm = jnp.where(mask, query, jnp.zeros_like(query))
            gm = jnp.where(mask, grad, jnp.zeros_like(grad))
            tiles, grads = [], []
            inner = None
            for kb in range(r + 1):
                there = slice(kb * size, (kb + 1) * size)
                prob = probs[h, r * (r + 1) // 2 + kb]
                gprob = dot_nt(gm, qkv[there, 2 * cols :])
                part = (prob.astype(F32) * gprob).sum(axis=1, keepdims=True)
                inner = part if inner is None else inner + part
                tiles.append(prob)
                grads.append(gprob)
            mixed = None
            for kb in range(r + 1):
                there = slice(kb * size, (kb + 1) * size)
                low = (tiles[kb].astype(F32) * (grads[kb] - inner)).astype(BF)
                term = dot_nn(low, qkv[there, cols : 2 * cols])
                mixed = term if mixed is None else mixed + term
                dk[there] += dot_tn(low, qm)
                dv[there] += dot_tn(tiles[kb], gm)
            total = jnp.where(mask, mixed, total)
            agenda.spend(0.42 * (r + 1))
        cos, sin = table_rows(net, cos_ref, sin_ref, flag, r * size, size, length, cols)
        dqkv[at, :cols] = turn(total * HD**-0.5, cos, -sin).astype(BF)
        dqkv[at, cols : 2 * cols] = turn(dk[at], cos, -sin).astype(BF)
        dqkv[at, 2 * cols :] = (0.5 * dv[at]).astype(BF)
        part = dot_nt(dqkv[at], wqkv[...])
        sb[r] = part.astype(BF)
        place = vg.at[:, pl.ds(pl.multiple_of(net.f * cols, cols), cols)]

        @pl.when(net.f == r)
        def _():
            own[...] = part
            vg[:, pl.ds(pl.multiple_of(net.f * cols, cols), cols)] = dqkv[at, 2 * cols :]

        @pl.when(net.f != r)
        def _():
            send_to(net, r, sb.at[r], rb.at[net.f], base).start()
            piece = dqkv.at[pl.ds(r * size, size), pl.ds(2 * cols, cols)]
            send_to(net, r, piece, place, value_base).start()

        agenda.spend(1.0)

    attend(n - 1)
    grad_out[...] = dot_tn(att[...], gb_all[...]).astype(BF).reshape(grad_out.shape)
    mate_out = net.push(grad_out.at[1 - net.c], m_out, net.mate)
    attend(n - 2)
    mate_out.wait_recv()
    l_out[...] = grad_out[net.c] + m_out[...]
    out_place = lambda c: sum_out.at[c]
    square = line.chunk(l_out, o_out, out_place(net.c), to_mate(out_place))
    begin = max(begin, agenda.clock)
    plan(square, begin, 0.7 * hop, before)
    before = square
    for r in reversed(range(n - 2)):
        attend(r)
    for copy in later:
        copy.wait()
    tile = 256 if width % 256 == 0 else width

    @pl.loop(0, width // tile)
    def _(i):
        at = pl.ds(pl.multiple_of(i * tile, tile), tile)
        grad = dot_tn(nrm[:, at], dqkv[...]).astype(BF)
        for j in range(3):
            grad_qkv[j, at] = grad[:, j * cols : (j + 1) * cols]

    mate_qkv = []
    for j in range(3):
        mate_qkv.append([])
        for r in range(n):
            rows = pl.ds(pl.multiple_of(2 * half * r + half * (1 - net.c), half), half)
            mate_qkv[j].append(net.push(grad_qkv.at[j, rows], m_qkv.at[j, r], net.mate))
    agenda.spend(3.0)
    begin, small = agenda.clock, 0.7 * hop
    thirds = []
    for j, start, count in ((j, 0, half) for j in range(3)):
        if start == 0:
            for r in range(n):
                mate_qkv[j][r].wait_recv()
                rows = pl.ds(pl.multiple_of(2 * half * r + half * net.c, half), half)
                l_qkv[j, r] = grad_qkv[j, rows] + m_qkv[j, r]
        at = pl.ds(start, count)
        place = lambda c, j=j, at=at: sum_qkv.at[j, c, at]
        lanes = lambda f, j=j, at=at: sum_qkv.at[j, net.c, at, pl.ds(pl.multiple_of(f * cols, cols), cols)]
        swap = Swap(net, line, lambda r, j=j, at=at: t_qkv.at[j, r, at], lanes, place(net.c))
        thirds.append(
            line.chunk(l_qkv.at[j, :, at], o_qkv.at[j, :, at], t_qkv.at[j, :, at], change_over(swap, place))
        )
        time = small * count / half
        plan(thirds[-1], begin, time, before)
        begin, before = begin + time, thirds[-1]
        agenda.spend(0.0)
    agenda.spend(45.0)
    total = own[...]
    for k in range(1, n):
        other = flip(net.f, k, n)
        send_to(net, other, sb.at[other], rb.at[other], base, other).wait()
        total = total + rb[other].astype(F32)
    input_grad[...] = input_grad[...] + norm_back(x[...].astype(F32), g1_all[0:1, :].astype(F32), total)
    agenda.spend(2.0)
    for k in range(1, n):
        other = flip(net.f, k, n)
        place = vg.at[:, pl.ds(pl.multiple_of(other * cols, cols), cols)]
        piece = dqkv.at[pl.ds(pl.multiple_of(other * size, size), size), pl.ds(2 * cols, cols)]
        send_to(net, other, piece, place, value_base, other).wait()
    first_grad[...] = first_grad[...] + vg[...].astype(F32)
    result = base_out[...]
    for k, copy in late:
        copy.wait_recv()
        result = result + rest_in[k - 3].astype(F32)
    layer_out[...] = result.astype(BF)
    agenda.spend(1000.0)
    for arrive in arrivals:
        arrive()
    stores = []

    def mated(which):
        for slot, place in which:
            line.copy(place(net.c), place(1 - net.c), slot, slot, net.mate).wait()

    mated(finals[: -len(thirds)])
    for src, dst in ((sum_down, out_down), (sum_gate, out_gate), (sum_up, out_up), (sum_out, out_out)):
        stores.append(net.local(src, dst))
    mated(finals[-len(thirds) :])
    stores.append(net.local(sum_qkv, out_qkv))
    line.finish()
    net.drain()
    for copy in stores:
        copy.wait()


def finish_kernel(
    gate,
    up,
    down,
    qkv,
    out,
    wg,
    wu,
    wq,
    wk,
    wv,
    g1,
    g2,
    layer,
    inputs,
    first,
    f_layer,
    f_inputs,
    f_first,
    gain_one,
    f_query,
    f_key,
    f_value,
    f_out,
    gain_two,
    f_gate,
    f_up,
    f_down,
    sums,
):
    f_layer[...], f_inputs[...], f_first[...] = layer[...], inputs[...], first[...]
    f_down[...], f_out[...] = down[...].astype(F32), out[...].astype(F32)
    step, count = pl.program_id(0), gate.shape[0]

    def row_sums(pairs):
        total = None
        for w, into, grad in pairs:
            grad = grad.astype(F32)
            into[...] = grad
            part = jnp.sum(w[...].astype(F32) * grad, axis=1, keepdims=True)
            total = part if total is None else total + part
        return total

    one = row_sums(((wq, f_query, qkv[0]), (wk, f_key, qkv[1]), (wv, f_value, qkv[2])))
    two = row_sums(((wg, f_gate, gate[...]), (wu, f_up, up[...])))
    lane = lax.broadcasted_iota(jnp.int32, (1, 128), 1)
    at = pl.ds(pl.multiple_of(step * count, count), count)
    sums[at] = jnp.where(lane == 0, one, jnp.where(lane == 1, two, 0.0))

    @pl.when(step == pl.num_programs(0) - 1)
    def _():
        across = sums[...].T
        gain_one[...] = across[0] / g1[...].astype(F32)
        gain_two[...] = across[1] / g2[...].astype(F32)


def finish(sums, weights, gains, tokens):
    gate, up, down, qkv, out = sums
    rows, hidden, width = gate.shape[0], down.shape[0], out.shape[1]
    steps = next(c for c in (4, 2, 1) if rows % (16 * c) == 0 and hidden % (16 * c) == 0)
    size = tokens[0].shape[0]

    def block(array):
        if array.ndim == 3:
            return pl.BlockSpec((3, array.shape[1] // steps, array.shape[2]), lambda i: (0, i, 0))
        if array.ndim == 1:
            return pl.BlockSpec(array.shape, lambda i: (0,))
        return pl.BlockSpec((array.shape[0] // steps, array.shape[1]), lambda i: (i, 0))

    args = (*sums, *weights, *gains, *tokens)
    square, wide = jax.ShapeDtypeStruct((rows, width), F32), jax.ShapeDtypeStruct(gate.shape, F32)
    flat = jax.ShapeDtypeStruct((rows,), F32)
    outs = [jax.ShapeDtypeStruct(t.shape, t.dtype) for t in tokens]
    outs += [flat] + [square] * 4 + [flat, wide, wide, jax.ShapeDtypeStruct(down.shape, F32)]
    return pl.pallas_call(
        finish_kernel,
        grid=(steps,),
        out_shape=outs,
        in_specs=[block(a) for a in args],
        out_specs=[block(o) for o in outs],
        scratch_shapes=[pltpu.VMEM((rows, 128), F32)],
        compiler_params=pltpu.CompilerParams(vmem_limit_bytes=LIMIT),
        name="finish",
    )(*args)


def rope_table(length, lanes):
    half = HD // 2
    frequency = np.float32(10000.0) ** (-np.arange(half, dtype=np.float32) / np.float32(half))
    angle = np.arange(length, dtype=np.float32)[:, None] * frequency[None, :].astype(np.float32)
    angle = angle.astype(np.float64)
    cos, sin = np.cos(angle), np.sin(angle)
    cos = np.tile(np.concatenate([cos, cos], axis=1), (1, lanes // HD))
    sin = np.tile(np.concatenate([-sin, sin], axis=1), (1, lanes // HD))
    return cos.astype(np.float32), sin.astype(np.float32)


def call(kernel, name, ident, outs, scratch, args, smem=(), far=(), far_outs=(), dmas=(64, 8), limit=LIMIT):
    vmem, smem_spec = pl.BlockSpec(memory_space=pltpu.VMEM), pl.BlockSpec(memory_space=pltpu.SMEM)
    hbm = pl.BlockSpec(memory_space=pl.ANY)
    return pl.pallas_call(
        kernel,
        out_shape=[jax.ShapeDtypeStruct(shape, dtype) for shape, dtype in outs],
        in_specs=[smem_spec if i in smem else hbm if i in far else vmem for i in range(len(args))],
        out_specs=[hbm if i in far_outs else vmem for i in range(len(outs))],
        scratch_shapes=[pltpu.VMEM(shape, dtype) for shape, dtype in scratch]
        + [
            pltpu.SemaphoreType.DMA((dmas[0],)),
            pltpu.SemaphoreType.DMA((dmas[0],)),
            pltpu.SemaphoreType.DMA((dmas[1],)),
        ],
        compiler_params=pltpu.CompilerParams(
            collective_id=ident, has_side_effects=True, vmem_limit_bytes=limit
        ),
        name=name,
    )(*args)


def body(
    tokens,
    value_first,
    window_split,
    cotangent,
    running_grad,
    gain_attn,
    w_query,
    w_key,
    w_value,
    w_out,
    gain_mlp,
    w_gate,
    w_up,
    w_down,
):
    n, copies = lax.axis_size("fsdp"), lax.axis_size("dp")
    size, width = tokens.shape
    length, cols = n * size, width // n
    rows = w_query.shape[0]
    half = rows // 2
    hidden = w_down.shape[0]
    wide = hidden
    tiles = (cols // HD, n * (n + 1) // 2, size, size)
    cos, sin = (jnp.asarray(t) for t in rope_table(length, 128))
    qkv, probs, att, nrm, mid, nm, wqkv, wgc, wuc, g1_all, g2_all, g_all = call(
        functools.partial(front_kernel, n, copies // 2),
        "front",
        1,
        [
            ((length, 3 * cols), BF),
            (tiles, BF),
            ((length, cols), BF),
            ((length, width), BF),
            ((size, width), F32),
            ((size, width), BF),
            ((width, 3 * cols), BF),
            ((width, wide), BF),
            ((width, wide), BF),
            ((16, width), BF),
            ((16, width), BF),
            ((length, width), BF),
        ],
        [
            ((length, 3 * cols), BF),
            ((length, cols), BF),
            ((length, width), BF),
            ((width, 3 * cols), BF),
            ((width, wide), BF),
            ((width, wide), BF),
            ((length, width), BF),
            (w_gate.shape, BF),
            (w_up.shape, BF),
            ((length, 128), F32),
            ((length, 128), F32),
            ((length, width), BF),
            ((length, cols), BF),
            ((width, width), BF),
            ((size, width), BF),
            ((n, rows, wide), BF),
            ((n, rows, wide), BF),
            (tiles, BF),
        ],
        (
            tokens,
            value_first,
            w_query,
            w_key,
            w_value,
            w_out,
            gain_attn,
            gain_mlp,
            window_split,
            cos,
            sin,
            w_gate,
            w_up,
            cotangent,
        ),
        smem=(8,),
        far=(0, 1, 2, 3, 4, 5, 9, 10, 11, 12, 13),
        far_outs=(0, 1, 2, 3, 6, 7, 8, 11),
        dmas=(256, 32),
    )
    partial, rest, base_out, rest_out, grad_gate, grad_up, total_down = call(
        functools.partial(middle_kernel, n, copies // 2),
        "middle",
        2,
        [
            ((size, width), F32),
            ((n - 3, size, width), BF),
            ((size, width), F32),
            ((n - 3, size, width), BF),
            ((width, wide), BF),
            ((width, wide), BF),
            ((hidden // 2, width), BF),
        ],
        [
            ((length, width), BF),
            ((width, wide), BF),
            ((width, wide), BF),
            ((width, wide), BF),
            ((width, wide), BF),
            ((2, hidden // 2, width), BF),
            ((hidden // 2, width), BF),
            ((hidden // 2, width), BF),
            ((hidden // 2, width), BF),
            ((length, width), BF),
            ((length, wide), BF),
            ((length, wide), BF),
            ((length, wide), BF),
            ((length, wide), F32),
            ((length, wide), F32),
            ((wide, width), BF),
            ((3, size, width), BF),
            ((3, size, width), BF),
            ((3, size // 2, width), BF),
            ((3, size, width), BF),
            ((3, size, width), BF),
        ],
        (nm, mid, g_all, wgc, wuc, w_down),
        far=(0, 2, 3, 4, 5),
        far_outs=(4, 5),
        dmas=(48, 12),
    )
    pieces, third = (n, half, wide), (3, n, half, cols)
    ends = [(2, half, n * hidden), (2, half, n * hidden), (2, hidden // 2, width), (3, 2, half, width), (2, cols // 2, width)]
    lines = [pieces, pieces, (hidden // 2, width), third, (cols // 2, width)]
    layer_out, input_grad, first_grad, sum_gate, sum_up, sum_down, sum_qkv, sum_out = call(
        functools.partial(back_kernel, n, copies // 2),
        "back",
        3,
        [((size, width), BF), ((size, width), F32), ((size, width), F32)] + [(e, BF) for e in ends],
        [
            ((n - 3, size, width), BF),
            ((size, width), BF),
            ((length, 3 * cols), BF),
            (tiles, BF),
            ((length, cols), BF),
            ((length, width), BF),
            ((width, 3 * cols), BF),
            ((cols, width), BF),
            ((length, 128), F32),
            ((length, 128), F32),
            ((16, width), BF),
            ((size, width), F32),
            ((length, width), BF),
            ((length, cols), F32),
            ((length, cols), F32),
            ((length, 3 * cols), BF),
            ((size, width), BF),
            ((n, size, width), BF),
            ((n, size, width), BF),
            ((size, width), F32),
            ((3, width, cols), BF),
            ((2, cols // 2, width), BF),
        ]
        + [(e, BF) for e in ends]
        + [(shape, BF) for shape in (pieces, pieces, third, lines[4])]
        + [(shape, BF) for shape in lines]
        + [(shape, BF) for shape in (pieces, pieces, third, lines[4])]
        + [(pieces, BF), (pieces, BF), (third, BF), (pieces, BF), (pieces, BF)],
        (
            rest,
            partial,
            mid,
            cotangent,
            g2_all,
            window_split,
            tokens,
            qkv,
            probs,
            att,
            nrm,
            wqkv,
            w_out,
            cos,
            sin,
            running_grad,
            g1_all,
            base_out,
            rest_out,
            grad_gate.reshape(n, 2, half, wide),
            grad_up.reshape(n, 2, half, wide),
            total_down,
        ),
        smem=(5,),
        far=(0, *range(6, 22)),
        far_outs=range(3, 8),
        dmas=(160, 32),
    )
    sums = (
        sum_gate.reshape(rows, -1),
        sum_up.reshape(rows, -1),
        sum_down.reshape(hidden, width),
        sum_qkv.reshape(3, rows, width),
        sum_out.reshape(rows, width),
    )
    return tuple(
        finish(
            sums,
            (w_gate, w_up, w_query, w_key, w_value),
            (gain_attn, gain_mlp),
            (layer_out, input_grad, first_grad),
        )
    )


def solution(mesh):
    token, flat, matrix = P(("dp", "fsdp"), None), P("fsdp"), P("fsdp", None)
    return jax.shard_map(
        body,
        mesh=mesh,
        in_specs=(token, token, P("dp"), token, token, flat)
        + (matrix,) * 4
        + (flat,)
        + (matrix,) * 3,
        out_specs=(token, token, token, flat) + (matrix,) * 4 + (flat,) + (matrix,) * 3,
        check_vma=False,
    )
```

```python
import functools

import jax
import jax.numpy as jnp
import numpy as np
from jax import lax
from jax.experimental import pallas as pl
from jax.experimental.pallas import tpu as pltpu
from jax.sharding import PartitionSpec as P

HD = 64
EPS = 1e-06
MESH = pl.DeviceIdType.MESH
BF = jnp.bfloat16
F32 = jnp.float32
LIMIT = 60 * 1024 * 1024


def dot_nn(a, b):
    return lax.dot_general(a, b, (((1,), (0,)), ((), ())), preferred_element_type=F32)


def dot_nt(a, b):
    return lax.dot_general(a, b, (((1,), (1,)), ((), ())), preferred_element_type=F32)


def dot_tn(a, b):
    return lax.dot_general(a, b, (((0,), (0,)), ((), ())), preferred_element_type=F32)


def flip(f, k, n):
    out, bit = 0, 1
    while bit < n:
        have, want = lax.rem(f // bit, 2), (k // bit) % 2
        out = out + (1 - have if want else have) * bit
        bit *= 2
    return out


class Net:
    def __init__(self, n, ssem, rsem, lsem=None):
        self.n, self.ssem, self.rsem, self.lsem = n, ssem, rsem, lsem
        self.d, self.f = lax.axis_index("dp"), lax.axis_index("fsdp")
        self.c = lax.rem(self.d, 2)
        self.mate = (self.d + 1 - 2 * self.c, self.f)
        self.used, self.lused, self.sent = 0, 0, []

    def peer(self, k):
        return (self.d, flip(self.f, k, self.n))

    def take(self, count=1):
        self.used += count
        return self.used - count

    def push(self, src, dst, device, slot=None):
        slot = self.take() if slot is None else slot
        copy = pltpu.make_async_remote_copy(
            src_ref=src,
            dst_ref=dst,
            send_sem=self.ssem.at[slot],
            recv_sem=self.rsem.at[slot],
            device_id=device,
            device_id_type=MESH,
        )
        copy.start()
        self.sent.append(copy)
        return copy

    def local(self, src, dst):
        copy = pltpu.make_async_copy(src, dst, self.lsem.at[self.lused])
        self.lused += 1
        copy.start()
        return copy

    def barrier(self, devices):
        sem = pltpu.get_barrier_semaphore()
        for device in devices:
            pl.semaphore_signal(sem, inc=1, device_id=device, device_id_type=MESH)
        pl.semaphore_wait(sem, len(devices))

    def drain(self):
        for copy in self.sent:
            copy.wait_send()


def rows_of(ref, block, size):
    return ref.at[pl.ds(pl.multiple_of(block * size, size), size)]


class Gather:
    def __init__(self, net, own, into, size):
        self.net, self.into, self.size = net, into, size
        self.direct = [1, 2] if net.n == 4 else list(range(1, net.n))
        self.copies = {k: net.push(own, rows_of(into, net.f, size), net.peer(k)) for k in self.direct}
        self.halves = {}

    def part(self, block, half):
        start = pl.multiple_of(block * self.size + half * (self.size // 2), self.size // 2)
        return self.into.at[pl.ds(start, self.size // 2)]

    def wait(self, k):
        net = self.net
        if k in self.copies:
            self.copies[k].wait_recv()
            if net.n == 4:
                part = self.part(flip(net.f, k, 4), k - 1)
                self.halves[k] = net.push(part, part, net.peer(3 - k))
        else:
            for copy in self.halves.values():
                copy.wait_recv()


def lane_mask(width, head):
    lane = lax.broadcasted_iota(jnp.int32, (1, width), 1)
    return (lane // HD) == head


def turn(values, cos, sin):
    width = values.shape[1]
    lane = lax.broadcasted_iota(jnp.int32, (1, width), 1)
    first = lax.rem(lane, HD) < HD // 2
    other = jnp.where(
        first, pltpu.roll(values, width - HD // 2, 1), pltpu.roll(values, HD // 2, 1)
    )
    return values * cos + other * sin


def table_rows(net, cos_ref, sin_ref, flag, start, size, length, width):
    half = length // 2
    plain = pl.ds(pl.multiple_of(start, size), size)
    split = pl.ds(pl.multiple_of(lax.rem(start, half), size), size)
    out = []
    for ref in (cos_ref, sin_ref):
        rows = jnp.where(flag == 1, ref[split], ref[plain])
        out.append(jnp.concatenate([rows] * (width // rows.shape[1]), axis=1))
    return out


def block_bias(flag, r, kb, size, length):
    half = length // 2
    if kb == r:
        row = lax.broadcasted_iota(jnp.int32, (size, size), 0)
        col = lax.broadcasted_iota(jnp.int32, (size, size), 1)
        return jnp.where(col <= row, 0.0, -1e30)
    if (r * size >= half) != (kb * size >= half):
        return jnp.where(flag == 1, -1e30, 0.0)
    return None


def scores_of(query, key, bias):
    scores = dot_nt(query, key)
    return scores if bias is None else scores + bias


def factor_of(hidden):
    return lax.rsqrt(jnp.mean(hidden * hidden, axis=-1, keepdims=True) + EPS)


def norm_back(hidden, gain, grad):
    factor = factor_of(hidden)
    scaled = grad * gain
    return factor * scaled - hidden * (factor * factor * factor) * jnp.mean(
        scaled * hidden, axis=-1, keepdims=True
    )


class Agenda:
    def __init__(self):
        self.clock, self.items = 0.0, []

    def at(self, time, step):
        self.items.append((time, len(self.items), step))

    def until(self, time):
        self.clock = max(self.clock, time)
        due = sorted(item for item in self.items if item[0] <= self.clock)
        self.items = [item for item in self.items if item[0] > self.clock]
        for _, _, step in due:
            step()

    def spend(self, time):
        self.until(self.clock + time)


class Spread:
    def __init__(self, net, chips, rows, sources):
        self.net, self.rows = net, rows
        self.chip = net.d // 2
        self.chips = chips if rows % (32 * chips) == 0 else 1
        self.share = rows // (2 * self.chips)
        self.part = self.chip if self.chips > 1 else 0
        n = net.n
        self.right, self.left, self.mate = (net.take(self.chips * (n - 1)) for _ in range(3))
        self.into = sources[0][2]
        self.first = []
        for k in range(1, n):
            to = net.peer(k)
            for piece, place, _ in sources:
                mine = pl.ds(self.start(0, self.part, net.c), self.share)
                here = pl.ds(self.start(net.f, self.part, net.c), self.share)
                self.first.append(net.push(piece(to[1]).at[mine], place.at[here], to))

    def start(self, block, part, core):
        return pl.multiple_of(block * self.rows + (2 * part + core) * self.share, self.share)

    def view(self, k, part, core):
        return self.into.at[pl.ds(self.start(flip(self.net.f, k, self.net.n), part, core), self.share)]

    def copy(self, k, part, base, device):
        net = self.net
        slot = base + part * (net.n - 1) + k - 1
        view = self.view(k, part, net.c)
        return pltpu.make_async_remote_copy(
            src_ref=view,
            dst_ref=view,
            send_sem=net.ssem.at[slot],
            recv_sem=net.rsem.at[slot],
            device_id=device,
            device_id_type=MESH,
        )

    def along(self, step):
        return ((self.chip + step) * 2 + self.net.c, self.net.f)

    def pass_on(self, part, base, step, room):
        @pl.when(room)
        def _():
            for k in range(1, self.net.n):
                self.copy(k, part, base, self.along(step)).start()

    def own(self):
        for copy in self.first:
            copy.wait_recv()
        if self.chips > 1:
            self.pass_on(self.part, self.right, 1, self.chip + 1 < self.chips)
            self.pass_on(self.part, self.left, -1, self.chip > 0)
        for k in range(1, self.net.n):
            self.copy(k, self.part, self.mate, self.net.mate).start()

    def hop(self, j):
        if j >= self.chips:
            return
        for base, step in ((self.right, 1), (self.left, -1)):
            part = self.part - step * j

            @pl.when((part >= 0) & (part < self.chips))
            def _(base=base, step=step, part=part):
                for k in range(1, self.net.n):
                    self.copy(k, part, base, self.net.mate).wait_recv()
                room = self.chip + 1 < self.chips if step == 1 else self.chip > 0
                self.pass_on(part, base, step, room)
                for k in range(1, self.net.n):
                    self.copy(k, part, self.mate, self.net.mate).start()

    def finish(self):
        n = self.net.n
        for part in range(self.chips):
            for k in range(1, n):
                self.copy(k, part, self.mate, self.net.mate).wait()
            if self.chips > 1:

                @pl.when((part <= self.chip) & (self.chip + 1 < self.chips))
                def _(part=part):
                    for k in range(1, n):
                        self.copy(k, part, self.right, self.net.mate).wait_send()

                @pl.when((part >= self.chip) & (self.chip > 0))
                def _(part=part):
                    for k in range(1, n):
                        self.copy(k, part, self.left, self.net.mate).wait_send()


def gain_rows(net, src, dst, rows):
    place = dst.at[:, pl.ds(pl.multiple_of(net.f * rows, rows), rows)]
    dst[:, pl.ds(pl.multiple_of(net.f * rows, rows), rows)] = jnp.broadcast_to(src[...].reshape(1, rows), (16, rows))
    return [net.push(place, place, net.peer(k)) for k in range(1, net.n)]


def send_to(net, r, src, dst, base, away=None):
    return pltpu.make_async_remote_copy(
        src_ref=src,
        dst_ref=dst,
        send_sem=net.ssem.at[base + r],
        recv_sem=net.rsem.at[base + (net.f if away is None else away)],
        device_id=(net.d, r),
        device_id_type=MESH,
    )


def front_kernel(
    n,
    chips,
    x,
    vf,
    wq,
    wk,
    wv,
    wo,
    g1,
    g2,
    flag_ref,
    cos_hbm,
    sin_hbm,
    wg_hbm,
    wu_hbm,
    ct,
    qkv_out,
    probs,
    att_out,
    nrm_out,
    mid,
    nm,
    wqkv_out,
    wgc_out,
    wuc_out,
    g1_all,
    g2_all,
    g_out,
    qkv,
    att,
    nrm,
    wqkv,
    wgc,
    wuc,
    g_all,
    wg,
    wu,
    cos_ref,
    sin_ref,
    x_all,
    vfc,
    wo_all,
    att_own,
    wgr,
    wur,
    low_probs,
    ssem,
    rsem,
    lsem,
):
    net = Net(n, ssem, rsem, lsem)
    size, width = x.shape
    length = n * size
    cols = width // n
    rows = wq.shape[0]
    hidden = wg.shape[1] // n
    flag = flag_ref[0]
    chip = net.d // 2
    sem = pltpu.get_barrier_semaphore()
    near = [net.peer(k) for k in range(1, n)] + [net.mate]
    for device in near:
        pl.semaphore_signal(sem, inc=1, device_id=device, device_id_type=MESH)
    for step, room in ((1, chip + 1 < chips), (-1, chip > 0)):
        @pl.when(room)
        def _(step=step):
            device = ((chip + step) * 2 + net.c, net.f)
            pl.semaphore_signal(sem, inc=1, device_id=device, device_id_type=MESH)

    edge = (chip == 0) | (chip == chips - 1)

    @pl.when(edge)
    def _():
        pl.semaphore_wait(sem, len(near) + min(chips - 1, 1))

    @pl.when(jnp.logical_not(edge))
    def _():
        pl.semaphore_wait(sem, len(near) + 2)

    mine = pl.ds(pl.multiple_of(net.f * cols, cols), cols)
    sources = []
    for i, w in enumerate((wq, wk, wv)):
        piece = lambda to, w=w: w.at[:, pl.ds(pl.multiple_of(to * cols, cols), cols)]
        sources.append((piece, wqkv.at[:, pl.ds(i * cols, cols)], wqkv))
    spread_qkv = Spread(net, chips, rows, sources)
    gains = gain_rows(net, g1, g1_all, rows) + gain_rows(net, g2, g2_all, rows)
    x_gather = Gather(net, x, x_all, size)
    values = []
    for k in range(1, n):
        device = net.peer(k)
        src = vf.at[:, pl.ds(pl.multiple_of(device[1] * cols, cols), cols)]
        values.append(net.push(src, rows_of(vfc, net.f, size), device))
    spread_out = Spread(net, chips, rows, [(lambda to: wo, wo_all, wo_all)])
    own_x = net.local(x, rows_of(x_all, net.f, size))
    halves = [net.local(wg_hbm, wg), net.local(wu_hbm, wu)]
    locals_ = [net.local(vf.at[:, mine], rows_of(vfc, net.f, size))]
    for i, w in enumerate((wq, wk, wv)):
        into = rows_of(wqkv.at[:, pl.ds(i * cols, cols)], net.f, rows)
        locals_.append(net.local(w.at[:, mine], into))
    locals_.append(net.local(wo, rows_of(wo_all, net.f, rows)))
    locals_.append(net.local(ct, rows_of(g_all, net.f, size)))
    locals_ += [net.local(cos_hbm, cos_ref), net.local(sin_hbm, sin_ref)]
    stores = []
    agenda = Agenda()

    def plan(spread, begin, time):
        agenda.at(begin, spread.own)
        for j in range(1, chips):
            agenda.at(begin + j * time + 0.5, functools.partial(spread.hop, j))

    plan(spread_qkv, 8, 3.6)
    plan(spread_out, 19, 4.4)
    for copy in halves:
        copy.wait()
    for w, piece, into in ((wg, wgr, wgc), (wu, wur, wuc)):
        for r in range(n):
            piece[r, :, :hidden] = w[:, r * hidden : (r + 1) * hidden]
        if piece.shape[2] > hidden:
            piece[:, :, hidden:] = jnp.zeros((n, rows, piece.shape[2] - hidden), BF)
        into[pl.ds(pl.multiple_of(net.f * rows, rows), rows)] = piece[net.f]
    for copy in gains:
        copy.wait_recv()
    agenda.until(8)
    spread_gate = Spread(net, chips, rows, [(lambda to: wgr.at[to], wgc, wgc)])
    spread_up = Spread(net, chips, rows, [(lambda to: wur.at[to], wuc, wuc)])
    plan(spread_gate, 31, 3.4)
    plan(spread_up, 40, 3.4)
    own_x.wait()
    gain = g1_all[0:1, :].astype(F32)

    def normalize(block):
        at = pl.ds(pl.multiple_of(block * size, size), size)
        rows_in = x_all[at].astype(F32)
        nrm[at] = (rows_in * factor_of(rows_in) * gain).astype(BF)

    normalize(net.f)
    agenda.until(16)
    for k in range(1, n - 1):
        x_gather.wait(k)
        normalize(flip(net.f, k, n))
    for copy in locals_:
        copy.wait()
    agenda.until(26)
    x_gather.wait(n - 1)
    normalize(flip(net.f, n - 1, n))
    stores.append(net.local(nrm, nrm_out))
    spreads = [spread_out, spread_gate, spread_up]
    spread_qkv.finish()
    stores.append(net.local(wqkv, wqkv_out))
    for copy in values:
        copy.wait_recv()
    g_gather = Gather(net, ct, g_all, size)
    agenda.until(31)

    @pl.loop(0, n)
    def _(block):
        at = pl.ds(pl.multiple_of(block * size, size), size)
        pre = dot_nn(nrm[at], wqkv[...])
        cos, sin = table_rows(net, cos_ref, sin_ref, flag, block * size, size, length, 2 * cols)
        turned = turn(pre[:, : 2 * cols], cos, sin)
        mixed = 0.5 * pre[:, 2 * cols :] + 0.5 * vfc[at].astype(F32)
        qkv[at, :cols] = (turned[:, :cols] * HD**-0.5).astype(BF)
        qkv[at, cols : 2 * cols] = turned[:, cols:].astype(BF)
        qkv[at, 2 * cols :] = mixed.astype(BF)

    agenda.spend(2.5)
    stores.append(net.local(qkv, qkv_out))
    heads = cols // HD
    base = net.take(n)
    for r in range(n):
        at = slice(r * size, (r + 1) * size)
        query = qkv[at, :cols]
        total = jnp.zeros((size, cols), F32)
        biases = [block_bias(flag, r, kb, size, length) for kb in range(r + 1)]
        for h in range(heads):
            mask = lane_mask(cols, h)
            masked = jnp.where(mask, query, jnp.zeros_like(query))
            tiles = [
                scores_of(masked, qkv[kb * size : (kb + 1) * size, cols : 2 * cols], biases[kb])
                for kb in range(r + 1)
            ]
            top = tiles[0].max(axis=1, keepdims=True)
            for tile in tiles[1:]:
                top = jnp.maximum(top, tile.max(axis=1, keepdims=True))
            raw = [jnp.exp(tile - top) for tile in tiles]
            whole = raw[0].sum(axis=1, keepdims=True)
            for tile in raw[1:]:
                whole = whole + tile.sum(axis=1, keepdims=True)
            inverse = 1.0 / whole
            mixed = None
            for kb, tile in enumerate(raw):
                low = (tile * inverse).astype(BF)
                low_probs[h, r * (r + 1) // 2 + kb] = low
                term = dot_nn(low, qkv[kb * size : (kb + 1) * size, 2 * cols :])
                mixed = term if mixed is None else mixed + term
            total = jnp.where(mask, mixed, total)
        done = pl.ds(r * (r + 1) // 2, r + 1)
        stores.append(net.local(low_probs.at[:, done], probs.at[:, done]))
        att[at] = total.astype(BF)

        @pl.when(net.f == r)
        def _():
            att_own[:, mine] = att[at]

        @pl.when(net.f != r)
        def _():
            send_to(net, r, att.at[pl.ds(r * size, size)], att_own.at[:, mine], base).start()

        agenda.spend(1.2 * (r + 1))
        if r == n - 2:
            for k in (1, 2):
                g_gather.wait(k)
    agenda.spend(100.0)
    stores.append(net.local(att, att_out))
    spread_out.finish()
    rows_at = pl.ds(pl.multiple_of(net.f * size, size), size)
    for k in range(1, n):
        other = flip(net.f, k, n)
        place = att_own.at[:, pl.ds(pl.multiple_of(other * cols, cols), cols)]
        src = rows_of(att, other, size)
        send_to(net, other, src, place, base, other).wait()
    sums = x_all[rows_at].astype(F32) + dot_nn(att_own[...], wo_all[...])
    mid[...] = sums
    nm[...] = (sums * factor_of(sums) * g2_all[0:1, :].astype(F32)).astype(BF)
    for spread, into, out in ((spread_gate, wgc, wgc_out), (spread_up, wuc, wuc_out)):
        spread.finish()
        stores.append(net.local(into, out))
    for k in range(3, n):
        g_gather.wait(k)
    stores.append(net.local(g_all, g_out))
    for copy in stores:
        copy.wait()
    net.drain()


class Line:
    def __init__(self, net, chips):
        chip, middle = net.d // 2, chips // 2
        left = chip < middle
        inward = jnp.where(left, chip + 1, chip - 1)
        outward = jnp.where(left, chip - 1, chip + 1)
        self.net, self.chip, self.first_middle = net, chip, middle - 1
        self.edge = (chip == 0) | (chip == chips - 1)
        self.middle = (chip == middle - 1) | (chip == middle)
        self.inner = (inward * 2 + net.c, net.f)
        self.outer = (outward * 2 + net.c, net.f)
        self.chunks, self.paced, self.middle_ends = [], set(), chips == 2

    def barrier(self, others):
        net, sem = self.net, pltpu.get_barrier_semaphore()
        fixed = others + [self.inner]
        for device in fixed:
            pl.semaphore_signal(sem, inc=1, device_id=device, device_id_type=MESH)

        @pl.when(jnp.logical_not(self.edge))
        def _():
            pl.semaphore_signal(sem, inc=1, device_id=self.outer, device_id_type=MESH)
            pl.semaphore_wait(sem, len(fixed) + 1)

        @pl.when(self.edge)
        def _():
            pl.semaphore_wait(sem, len(fixed))

    def chunk(self, own, outer, total, deliver=None, kind="whole"):
        self.chunks.append((own, outer, total, deliver, kind, [self.net.take() for _ in range(3)]))
        return len(self.chunks) - 1

    def copy(self, src, dst, send, recv, device):
        return pltpu.make_async_remote_copy(
            src_ref=src,
            dst_ref=dst,
            send_sem=self.net.ssem.at[send],
            recv_sem=self.net.rsem.at[recv],
            device_id=device,
            device_id_type=MESH,
        )

    def inwards(self, i):
        own, outer, total, _, _, (up, down, _) = self.chunks[i]

        @pl.when(jnp.logical_not(self.edge))
        def _():
            self.copy(own, outer, up, up, self.outer).wait_recv()
            own[...] = own[...] + outer[...]

        if self.chunks[i][4] == "near":

            @pl.when(self.middle)
            def _():
                total[...] = own[...]

        else:
            self.exchange(i)

        @pl.when(jnp.logical_not(self.middle))
        def _():
            self.copy(own, outer, up, up, self.inner).start()

    def exchange(self, i):
        own, _, total, _, _, (_, down, _) = self.chunks[i]

        @pl.when(self.middle)
        def _():
            self.copy(own, total, down, down, self.inner).start()

    def pace(self, i):
        own, outer, _, _, _, (up, _, _) = self.chunks[i]
        self.paced.add(i)
        if not self.middle_ends:
            self.copy(own, outer, up, up, self.inner).wait_send()

    def meet(self, i):
        own, _, total, _, _, (_, down, _) = self.chunks[i]

        @pl.when(self.middle)
        def _():
            self.copy(own, total, down, down, self.inner).wait_recv()
            total[...] = own[...] + total[...]

    def outwards(self, i):
        _, _, total, deliver, kind, (_, down, away) = self.chunks[i]
        if kind in ("whole", "far"):
            self.meet(i)

        @pl.when(jnp.logical_not(self.middle))
        def _():
            self.copy(total, total, down, down, self.inner).wait_recv()

        @pl.when(jnp.logical_not(self.edge))
        def _():
            self.copy(total, total, away, down, self.outer).start()

        deliver()

    def finish(self):
        for i, (own, _, total, _, kind, (up, down, away)) in enumerate(self.chunks):
            if kind != "part":
                slot = jnp.where(self.middle, down, up)
                sent = jnp.logical_not(self.edge) | self.middle if i in self.paced else self.chip >= 0
                if kind == "near":
                    sent = sent & jnp.logical_not(self.middle)
                if kind == "far":
                    sent = self.middle

                @pl.when(sent)
                def _():
                    self.copy(own, total, slot, down, self.inner).wait_send()

            if kind not in ("meet", "near"):

                @pl.when(jnp.logical_not(self.edge))
                def _():
                    self.copy(total, total, away, down, self.outer).wait_send()


def cut(size):
    if size % 32 == 0:
        return [(0, size // 2), (size // 2, size // 2)]
    return [(0, size)]


def middle_kernel(
    n,
    chips,
    nm,
    mid,
    g_hbm,
    wgc_hbm,
    wuc_hbm,
    wd,
    partial,
    rest,
    base_out,
    rest_out,
    out_gate,
    out_up,
    total_down,
    g_all,
    wgc,
    wuc,
    grad_gate,
    grad_up,
    grad_down,
    m_down,
    l_down,
    o_down,
    nm_all,
    hid_all,
    gg_all,
    ug_all,
    coef,
    silus,
    wd_wide,
    sb1,
    rb1,
    relayed,
    sb2,
    rb2,
    ssem,
    rsem,
    lsem,
):
    net = Net(n, ssem, rsem, lsem)
    size, width = nm.shape
    line = Line(net, chips)
    line.barrier([net.peer(k) for k in range(1, n)] + [net.mate])

    @pl.when(jnp.logical_not(line.middle))
    def _():
        total_down[...] = jnp.zeros_like(total_down)

    gather = Gather(net, nm, nm_all, size)
    hidden = wd.shape[0]
    loads = [
        net.local(nm, rows_of(nm_all, net.f, size)),
        net.local(wgc_hbm, wgc),
        net.local(wuc_hbm, wuc),
        net.local(wd, wd_wide.at[pl.ds(0, hidden)]),
        net.local(g_hbm, g_all),
    ]
    if wd_wide.shape[0] > hidden:
        wd_wide[hidden:] = jnp.zeros((wd_wide.shape[0] - hidden, width), BF)

    def rows_at(k):
        return pl.ds(pl.multiple_of(flip(net.f, k, n) * size, size), size)

    def forward(k):
        at = rows_at(k)
        a = nm_all[at]
        gate = dot_nn(a, wgc[...])
        up = dot_nn(a, wuc[...])
        sig = jax.nn.sigmoid(gate)
        silu = gate * sig
        hid_all[at] = (silu * up).astype(BF)
        coef[at] = up * sig * (1.0 + gate * (1.0 - sig))
        silus[at] = silu
        part = dot_nn(hid_all[at], wd_wide[...])
        if k == 0:
            base_out[...] = mid[...] + part
        elif k < 3:
            sb1[k] = part.astype(BF)
        else:
            rest_out[k - 3] = part.astype(BF)
            if n == 4:
                for j in (1, 2):
                    part = pl.ds((j - 1) * (size // 2), size // 2)
                    relays.append(net.push(rest_out.at[0, part], relayed.at[j], net.peer(j)))

    soon, relays = [], []

    def backward(k):
        at = rows_at(k)
        grad = dot_nt(g_all[at], wd_wide[...])
        gg_all[at] = (grad * coef[at]).astype(BF)
        ug_all[at] = (grad * silus[at]).astype(BF)
        back = dot_nt(gg_all[at], wgc[...]) + dot_nt(ug_all[at], wuc[...])
        if k == 0:
            partial[...] = back
        elif k < 3:
            sb2[k] = back.astype(BF)
            soon.append((k, net.push(sb2.at[k], rb2.at[k], net.peer(k))))
        else:
            rest[k - 3] = back.astype(BF)

    for copy in loads:
        copy.wait()
    forward(0)
    backward(0)
    tile = 256 if width % 256 == 0 else width

    def columns(i):
        return pl.ds(pl.multiple_of(i * tile, tile), tile)

    def down_terms():
        for start in range(0, width, tile):
            at = slice(start, start + tile)
            grad = dot_tn(hid_all[...], g_all[:, at])[:hidden].astype(BF)
            grad_down[:, :, at] = grad.reshape(2, hidden // 2, tile)
        return net.push(grad_down.at[1 - net.c], m_down, net.mate)

    for k in range(1, n):
        gather.wait(k)
        for j in ([1] if k == 2 or n == 2 else []) + ([k] if k >= 2 else []):
            forward(j)
            if j == n - 1:
                mate = down_terms()
            backward(j)
    mate.wait_recv()
    l_down[...] = grad_down[net.c] + m_down[...]
    downs = []
    for start, count in cut(l_down.shape[0]):
        at = pl.ds(start, count)
        kind = "near" if downs else "meet"
        downs.append(line.chunk(l_down.at[at], o_down.at[at], total_down.at[at], kind=kind))

    @pl.when(line.edge)
    def _():
        line.inwards(downs[0])

    for j, copy in enumerate(relays, 1):
        copy.wait_recv()
        at = slice((j - 1) * (size // 2), j * (size // 2))
        sb1[3 - j, at] = (sb1[3 - j, at].astype(F32) + relayed[j].astype(F32)).astype(BF)
    late = [(k, net.push(sb1.at[k], rb1.at[k], net.peer(k))) for k in range(1, 3)]

    @pl.loop(0, width // tile)
    def _(i):
        grad_gate[columns(i)] = dot_tn(nm_all[:, columns(i)], gg_all[...]).astype(BF)

    stores = [net.local(grad_gate, out_gate)]

    @pl.loop(0, width // tile)
    def _(i):
        grad_up[columns(i)] = dot_tn(nm_all[:, columns(i)], ug_all[...]).astype(BF)

    stores.append(net.local(grad_up, out_up))

    @pl.when(line.edge)
    def _():
        for before, i in zip(downs, downs[1:]):
            line.pace(before)
            line.inwards(i)

    @pl.when(jnp.logical_not(line.edge))
    def _():
        for i in downs:
            line.inwards(i)

    grad = partial[...]
    for k, copy in soon:
        copy.wait_recv()
        grad = grad + rb2[k].astype(F32)
    partial[...] = grad
    result = base_out[...]
    for k, copy in late:
        copy.wait_recv()
        result = result + rb1[k].astype(F32)
    base_out[...] = result
    line.meet(downs[0])
    line.finish()
    for copy in stores:
        copy.wait()
    net.drain()


class Swap:
    def __init__(self, net, line, total, place, done, settle=None):
        self.net, self.line, self.total, self.place = net, line, total, place
        self.done, self.settle = done, settle
        self.base = net.take(net.n)

    def copy(self, k):
        to = self.net.peer(k)
        slot = self.base + k
        return self.line.copy(self.total(to[1]), self.place(self.net.f), slot, slot, to)

    def start(self):
        for k in range(1, self.net.n):
            self.copy(k).start()
        self.place(self.net.f)[...] = self.total(self.net.f)[...]

    def end(self):
        for k in range(1, self.net.n):
            self.copy(k).wait()
        if self.settle is not None:
            self.settle()


def back_kernel(
    n,
    chips,
    rest,
    partial_hbm,
    mid_hbm,
    ct_hbm,
    g2_all,
    flag_ref,
    x_hbm,
    qkv_hbm,
    probs_hbm,
    att_hbm,
    nrm_hbm,
    wqkv_hbm,
    wo_hbm,
    cos_hbm,
    sin_hbm,
    rg_hbm,
    g1_hbm,
    base_hbm,
    rest_out,
    grad_gate,
    grad_up,
    down_hbm,
    layer_out,
    input_grad,
    first_grad,
    out_gate,
    out_up,
    out_down,
    out_qkv,
    out_out,
    partial,
    mid,
    ct,
    rest_in,
    x,
    qkv,
    probs,
    att,
    nrm,
    wqkv,
    wo,
    cos_ref,
    sin_ref,
    g1_all,
    base_out,
    gb_all,
    dk,
    dv,
    dqkv,
    vg,
    sb,
    rb,
    own,
    grad_qkv,
    grad_out,
    sum_gate,
    sum_up,
    sum_down,
    sum_qkv,
    sum_out,
    m_gate,
    m_up,
    m_qkv,
    m_out,
    l_gate,
    l_up,
    t_down,
    l_qkv,
    l_out,
    o_gate,
    o_up,
    o_qkv,
    o_out,
    t_gate,
    t_up,
    t_qkv,
    a_gate,
    a_up,
    ssem,
    rsem,
    lsem,
):
    net = Net(n, ssem, rsem, lsem)
    line = Line(net, chips)
    size, width = ct.shape
    length = n * size
    cols = width // n
    heads = cols // HD
    half, hidden = m_gate.shape[1], sum_gate.shape[2] // n
    flag = flag_ref[0]
    line.barrier([net.peer(k) for k in range(1, n)] + [net.mate])
    rests = [net.push(rest.at[k - 3], rest_in.at[k - 3], net.peer(k)) for k in range(3, n)]
    mates = [
        net.push(grad_gate.at[:, 1 - net.c], m_gate, net.mate),
        net.push(grad_up.at[:, 1 - net.c], m_up, net.mate),
    ]
    halves = [
        net.local(grad_gate.at[:, net.c], l_gate),
        net.local(grad_up.at[:, net.c], l_up),
    ]
    down_load = net.local(down_hbm, t_down)
    inputs = [net.local(partial_hbm, partial), net.local(mid_hbm, mid), net.local(ct_hbm, ct)]
    early = [
        net.local(src, dst)
        for src, dst in (
            (qkv_hbm, qkv),
            (wo_hbm, wo),
            (probs_hbm, probs),
            (cos_hbm, cos_ref),
            (sin_hbm, sin_ref),
            (wqkv_hbm, wqkv),
            (att_hbm, att),
        )
    ]
    later = [
        net.local(src, dst)
        for src, dst in (
            (nrm_hbm, nrm),
            (x_hbm, x),
            (g1_hbm, g1_all),
            (rg_hbm, first_grad),
            (base_hbm, base_out),
        )
    ]
    dk[...] = jnp.zeros_like(dk)
    dv[...] = jnp.zeros_like(dv)
    finals = []

    def to_mate(place):
        slot = net.take()
        finals.append((slot, place))
        return lambda: line.copy(place(net.c), place(net.c), slot, slot, net.mate).start()

    agenda = Agenda()
    hop = 8.2

    def edge_only(time, step, i):
        def run():
            @pl.when(line.edge)
            def _():
                step(i)

        agenda.at(time, run)

    def rest_only(time, step, i):
        def run():
            @pl.when(jnp.logical_not(line.edge))
            def _():
                step(i)

        agenda.at(time, run)

    def launch(i, before):
        if before is not None:
            line.pace(before)
        line.inwards(i)

    def plan(i, start, time, before):
        edge_only(start, functools.partial(launch, before=before), i)
        rest_only(start + time + 3, line.inwards, i)
        rest_only(start + 2 * time + 6, line.outwards, i)
        edge_only(start + 3 * time + 11, line.outwards, i)

    arrivals = []

    def change_over(swap, place):
        send = to_mate(place)

        def arrive():
            swap.end()
            send()

        arrivals.append(arrive)
        return swap.start

    def spread_rows(t, a, total, at, rows):
        def settle():
            for r in range(n):
                total[net.c, rows, r * hidden : (r + 1) * hidden] = a[r, rows, :hidden]

        return Swap(net, line, lambda r: t.at[r, at], lambda f: a.at[f, at], total.at[net.c, at], settle)

    down_load.wait()

    for start, count in cut(t_down.shape[0]):
        at = pl.ds(start, count)
        place = lambda c, at=at: sum_down.at[c, at]
        kind = "far" if start else "part"
        down = line.chunk(t_down.at[at], None, place(net.c), to_mate(place), kind)
        if start:
            line.exchange(down)
        else:

            @pl.when(line.middle)
            def _(at=at, place=place):
                place(net.c)[...] = t_down[at]

        rest_only(17 if start else 8, line.outwards, down)
        edge_only(34, line.outwards, down)
    begin, before = 9.0, None
    for mate, load, l, m, o, t, a, total in zip(
        mates,
        halves,
        (l_gate, l_up),
        (m_gate, m_up),
        (o_gate, o_up),
        (t_gate, t_up),
        (a_gate, a_up),
        (sum_gate, sum_up),
    ):
        load.wait()
        mate.wait_recv()
        l[...] = l[...] + m[...]
        for start, count in cut(half):
            at, rows = pl.ds(start, count), slice(start, start + count)
            place = lambda c, at=at, total=total: total.at[c, at]
            swap = spread_rows(t, a, total, at, rows)
            i = line.chunk(l.at[:, at], o.at[:, at], t.at[:, at], change_over(swap, place))
            plan(i, begin, hop, before)
            begin, before = begin + hop, i
        agenda.until(9)
    for copy in inputs:
        copy.wait()
    grad = partial[...]
    for i, copy in enumerate(rests):
        copy.wait_recv()
        grad = grad + rest_in[i].astype(F32)
    total = ct[...].astype(F32) + norm_back(mid[...], g2_all[0:1, :].astype(F32), grad)
    input_grad[...] = total
    gb_all[pl.ds(pl.multiple_of(net.f * size, size), size)] = total.astype(BF)
    gather = Gather(net, rows_of(gb_all, net.f, size), gb_all, size)
    for copy in early:
        copy.wait()
    agenda.until(17)
    agenda.until(25)
    for k in range(1, n - 1):
        gather.wait(k)
    agenda.until(29)
    gather.wait(n - 1)
    late = [(k, net.push(rest_out.at[k - 3], rest_in.at[k - 3], net.peer(k))) for k in range(3, n) if n != 4]
    agenda.until(34)

    base = net.take(n)
    value_base = net.take(n)

    def attend(r):
        at = slice(r * size, (r + 1) * size)
        query = qkv[at, :cols]
        grad = dot_nt(gb_all[at], wo[...]).astype(BF)
        total = jnp.zeros((size, cols), F32)
        for h in range(heads):
            mask = lane_mask(cols, h)
            qm = jnp.where(mask, query, jnp.zeros_like(query))
            gm = jnp.where(mask, grad, jnp.zeros_like(grad))
            tiles, grads = [], []
            inner = None
            for kb in range(r + 1):
                there = slice(kb * size, (kb + 1) * size)
                prob = probs[h, r * (r + 1) // 2 + kb]
                gprob = dot_nt(gm, qkv[there, 2 * cols :])
                part = (prob.astype(F32) * gprob).sum(axis=1, keepdims=True)
                inner = part if inner is None else inner + part
                tiles.append(prob)
                grads.append(gprob)
            mixed = None
            for kb in range(r + 1):
                there = slice(kb * size, (kb + 1) * size)
                low = (tiles[kb].astype(F32) * (grads[kb] - inner)).astype(BF)
                term = dot_nn(low, qkv[there, cols : 2 * cols])
                mixed = term if mixed is None else mixed + term
                dk[there] += dot_tn(low, qm)
                dv[there] += dot_tn(tiles[kb], gm)
            total = jnp.where(mask, mixed, total)
            agenda.spend(0.42 * (r + 1))
        cos, sin = table_rows(net, cos_ref, sin_ref, flag, r * size, size, length, cols)
        dqkv[at, :cols] = turn(total * HD**-0.5, cos, -sin).astype(BF)
        dqkv[at, cols : 2 * cols] = turn(dk[at], cos, -sin).astype(BF)
        dqkv[at, 2 * cols :] = (0.5 * dv[at]).astype(BF)
        part = dot_nt(dqkv[at], wqkv[...])
        sb[r] = part.astype(BF)
        place = vg.at[:, pl.ds(pl.multiple_of(net.f * cols, cols), cols)]

        @pl.when(net.f == r)
        def _():
            own[...] = part
            vg[:, pl.ds(pl.multiple_of(net.f * cols, cols), cols)] = dqkv[at, 2 * cols :]

        @pl.when(net.f != r)
        def _():
            send_to(net, r, sb.at[r], rb.at[net.f], base).start()
            piece = dqkv.at[pl.ds(r * size, size), pl.ds(2 * cols, cols)]
            send_to(net, r, piece, place, value_base).start()

        agenda.spend(1.0)

    attend(n - 1)
    grad_out[...] = dot_tn(att[...], gb_all[...]).astype(BF).reshape(grad_out.shape)
    mate_out = net.push(grad_out.at[1 - net.c], m_out, net.mate)
    attend(n - 2)
    mate_out.wait_recv()
    l_out[...] = grad_out[net.c] + m_out[...]
    out_place = lambda c: sum_out.at[c]
    square = line.chunk(l_out, o_out, out_place(net.c), to_mate(out_place))
    begin = max(begin, agenda.clock)
    plan(square, begin, 0.7 * hop, before)
    before = square
    for r in reversed(range(n - 2)):
        attend(r)
    for copy in later:
        copy.wait()
    tile = 256 if width % 256 == 0 else width

    @pl.loop(0, width // tile)
    def _(i):
        at = pl.ds(pl.multiple_of(i * tile, tile), tile)
        grad = dot_tn(nrm[:, at], dqkv[...]).astype(BF)
        for j in range(3):
            grad_qkv[j, at] = grad[:, j * cols : (j + 1) * cols]

    mate_qkv = []
    for j in range(3):
        mate_qkv.append([])
        for r in range(n):
            rows = pl.ds(pl.multiple_of(2 * half * r + half * (1 - net.c), half), half)
            mate_qkv[j].append(net.push(grad_qkv.at[j, rows], m_qkv.at[j, r], net.mate))
    agenda.spend(3.0)
    begin, small = agenda.clock, 0.7 * hop
    thirds = []
    for j, start, count in ((j, 0, half) for j in range(3)):
        if start == 0:
            for r in range(n):
                mate_qkv[j][r].wait_recv()
                rows = pl.ds(pl.multiple_of(2 * half * r + half * net.c, half), half)
                l_qkv[j, r] = grad_qkv[j, rows] + m_qkv[j, r]
        at = pl.ds(start, count)
        place = lambda c, j=j, at=at: sum_qkv.at[j, c, at]
        lanes = lambda f, j=j, at=at: sum_qkv.at[j, net.c, at, pl.ds(pl.multiple_of(f * cols, cols), cols)]
        swap = Swap(net, line, lambda r, j=j, at=at: t_qkv.at[j, r, at], lanes, place(net.c))
        thirds.append(
            line.chunk(l_qkv.at[j, :, at], o_qkv.at[j, :, at], t_qkv.at[j, :, at], change_over(swap, place))
        )
        time = small * count / half
        plan(thirds[-1], begin, time, before)
        begin, before = begin + time, thirds[-1]
        agenda.spend(0.0)
    agenda.spend(45.0)
    total = own[...]
    for k in range(1, n):
        other = flip(net.f, k, n)
        send_to(net, other, sb.at[other], rb.at[other], base, other).wait()
        total = total + rb[other].astype(F32)
    input_grad[...] = input_grad[...] + norm_back(x[...].astype(F32), g1_all[0:1, :].astype(F32), total)
    agenda.spend(2.0)
    for k in range(1, n):
        other = flip(net.f, k, n)
        place = vg.at[:, pl.ds(pl.multiple_of(other * cols, cols), cols)]
        piece = dqkv.at[pl.ds(pl.multiple_of(other * size, size), size), pl.ds(2 * cols, cols)]
        send_to(net, other, piece, place, value_base, other).wait()
    first_grad[...] = first_grad[...] + vg[...].astype(F32)
    result = base_out[...]
    for k, copy in late:
        copy.wait_recv()
        result = result + rest_in[k - 3].astype(F32)
    layer_out[...] = result.astype(BF)
    agenda.spend(1000.0)
    for arrive in arrivals:
        arrive()
    stores = []

    def mated(which):
        for slot, place in which:
            line.copy(place(net.c), place(1 - net.c), slot, slot, net.mate).wait()

    mated(finals[: -len(thirds)])
    for src, dst in ((sum_down, out_down), (sum_gate, out_gate), (sum_up, out_up), (sum_out, out_out)):
        stores.append(net.local(src, dst))
    mated(finals[-len(thirds) :])
    stores.append(net.local(sum_qkv, out_qkv))
    line.finish()
    net.drain()
    for copy in stores:
        copy.wait()


def finish_kernel(
    gate,
    up,
    down,
    qkv,
    out,
    wg,
    wu,
    wq,
    wk,
    wv,
    g1,
    g2,
    layer,
    inputs,
    first,
    f_layer,
    f_inputs,
    f_first,
    gain_one,
    f_query,
    f_key,
    f_value,
    f_out,
    gain_two,
    f_gate,
    f_up,
    f_down,
    sums,
):
    f_layer[...], f_inputs[...], f_first[...] = layer[...], inputs[...], first[...]
    f_down[...], f_out[...] = down[...].astype(F32), out[...].astype(F32)
    step, count = pl.program_id(0), gate.shape[0]

    def row_sums(pairs):
        total = None
        for w, into, grad in pairs:
            grad = grad.astype(F32)
            into[...] = grad
            part = jnp.sum(w[...].astype(F32) * grad, axis=1, keepdims=True)
            total = part if total is None else total + part
        return total

    one = row_sums(((wq, f_query, qkv[0]), (wk, f_key, qkv[1]), (wv, f_value, qkv[2])))
    two = row_sums(((wg, f_gate, gate[...]), (wu, f_up, up[...])))
    lane = lax.broadcasted_iota(jnp.int32, (1, 128), 1)
    at = pl.ds(pl.multiple_of(step * count, count), count)
    sums[at] = jnp.where(lane == 0, one, jnp.where(lane == 1, two, 0.0))

    @pl.when(step == pl.num_programs(0) - 1)
    def _():
        across = sums[...].T
        gain_one[...] = across[0] / g1[...].astype(F32)
        gain_two[...] = across[1] / g2[...].astype(F32)


def finish(sums, weights, gains, tokens):
    gate, up, down, qkv, out = sums
    rows, hidden, width = gate.shape[0], down.shape[0], out.shape[1]
    steps = next(c for c in (2, 1) if rows % (16 * c) == 0 and hidden % (16 * c) == 0)
    size = tokens[0].shape[0]

    def block(array):
        if array.ndim == 3:
            return pl.BlockSpec((3, array.shape[1] // steps, array.shape[2]), lambda i: (0, i, 0))
        if array.ndim == 1:
            return pl.BlockSpec(array.shape, lambda i: (0,))
        return pl.BlockSpec((array.shape[0] // steps, array.shape[1]), lambda i: (i, 0))

    args = (*sums, *weights, *gains, *tokens)
    square, wide = jax.ShapeDtypeStruct((rows, width), F32), jax.ShapeDtypeStruct(gate.shape, F32)
    flat = jax.ShapeDtypeStruct((rows,), F32)
    outs = [jax.ShapeDtypeStruct(t.shape, t.dtype) for t in tokens]
    outs += [flat] + [square] * 4 + [flat, wide, wide, jax.ShapeDtypeStruct(down.shape, F32)]
    return pl.pallas_call(
        finish_kernel,
        grid=(steps,),
        out_shape=outs,
        in_specs=[block(a) for a in args],
        out_specs=[block(o) for o in outs],
        scratch_shapes=[pltpu.VMEM((rows, 128), F32)],
        compiler_params=pltpu.CompilerParams(vmem_limit_bytes=LIMIT),
        name="finish",
    )(*args)


def rope_table(length, lanes):
    half = HD // 2
    frequency = np.float32(10000.0) ** (-np.arange(half, dtype=np.float32) / np.float32(half))
    angle = np.arange(length, dtype=np.float32)[:, None] * frequency[None, :].astype(np.float32)
    angle = angle.astype(np.float64)
    cos, sin = np.cos(angle), np.sin(angle)
    cos = np.tile(np.concatenate([cos, cos], axis=1), (1, lanes // HD))
    sin = np.tile(np.concatenate([-sin, sin], axis=1), (1, lanes // HD))
    return cos.astype(np.float32), sin.astype(np.float32)


def call(kernel, name, ident, outs, scratch, args, smem=(), far=(), far_outs=(), dmas=(64, 8), limit=LIMIT):
    vmem, smem_spec = pl.BlockSpec(memory_space=pltpu.VMEM), pl.BlockSpec(memory_space=pltpu.SMEM)
    hbm = pl.BlockSpec(memory_space=pl.ANY)
    return pl.pallas_call(
        kernel,
        out_shape=[jax.ShapeDtypeStruct(shape, dtype) for shape, dtype in outs],
        in_specs=[smem_spec if i in smem else hbm if i in far else vmem for i in range(len(args))],
        out_specs=[hbm if i in far_outs else vmem for i in range(len(outs))],
        scratch_shapes=[pltpu.VMEM(shape, dtype) for shape, dtype in scratch]
        + [
            pltpu.SemaphoreType.DMA((dmas[0],)),
            pltpu.SemaphoreType.DMA((dmas[0],)),
            pltpu.SemaphoreType.DMA((dmas[1],)),
        ],
        compiler_params=pltpu.CompilerParams(
            collective_id=ident, has_side_effects=True, vmem_limit_bytes=limit
        ),
        name=name,
    )(*args)


def body(
    tokens,
    value_first,
    window_split,
    cotangent,
    running_grad,
    gain_attn,
    w_query,
    w_key,
    w_value,
    w_out,
    gain_mlp,
    w_gate,
    w_up,
    w_down,
):
    n, copies = lax.axis_size("fsdp"), lax.axis_size("dp")
    size, width = tokens.shape
    length, cols = n * size, width // n
    rows = w_query.shape[0]
    half = rows // 2
    hidden = w_down.shape[0]
    wide = hidden
    tiles = (cols // HD, n * (n + 1) // 2, size, size)
    cos, sin = (jnp.asarray(t) for t in rope_table(length, 128))
    qkv, probs, att, nrm, mid, nm, wqkv, wgc, wuc, g1_all, g2_all, g_all = call(
        functools.partial(front_kernel, n, copies // 2),
        "front",
        1,
        [
            ((length, 3 * cols), BF),
            (tiles, BF),
            ((length, cols), BF),
            ((length, width), BF),
            ((size, width), F32),
            ((size, width), BF),
            ((width, 3 * cols), BF),
            ((width, wide), BF),
            ((width, wide), BF),
            ((16, width), BF),
            ((16, width), BF),
            ((length, width), BF),
        ],
        [
            ((length, 3 * cols), BF),
            ((length, cols), BF),
            ((length, width), BF),
            ((width, 3 * cols), BF),
            ((width, wide), BF),
            ((width, wide), BF),
            ((length, width), BF),
            (w_gate.shape, BF),
            (w_up.shape, BF),
            ((length, 128), F32),
            ((length, 128), F32),
            ((length, width), BF),
            ((length, cols), BF),
            ((width, width), BF),
            ((size, width), BF),
            ((n, rows, wide), BF),
            ((n, rows, wide), BF),
            (tiles, BF),
        ],
        (
            tokens,
            value_first,
            w_query,
            w_key,
            w_value,
            w_out,
            gain_attn,
            gain_mlp,
            window_split,
            cos,
            sin,
            w_gate,
            w_up,
            cotangent,
        ),
        smem=(8,),
        far=(0, 1, 2, 3, 4, 5, 9, 10, 11, 12, 13),
        far_outs=(0, 1, 2, 3, 6, 7, 8, 11),
        dmas=(256, 32),
    )
    partial, rest, base_out, rest_out, grad_gate, grad_up, total_down = call(
        functools.partial(middle_kernel, n, copies // 2),
        "middle",
        2,
        [
            ((size, width), F32),
            ((n - 3, size, width), BF),
            ((size, width), F32),
            ((n - 3, size, width), BF),
            ((width, wide), BF),
            ((width, wide), BF),
            ((hidden // 2, width), BF),
        ],
        [
            ((length, width), BF),
            ((width, wide), BF),
            ((width, wide), BF),
            ((width, wide), BF),
            ((width, wide), BF),
            ((2, hidden // 2, width), BF),
            ((hidden // 2, width), BF),
            ((hidden // 2, width), BF),
            ((hidden // 2, width), BF),
            ((length, width), BF),
            ((length, wide), BF),
            ((length, wide), BF),
            ((length, wide), BF),
            ((length, wide), F32),
            ((length, wide), F32),
            ((wide, width), BF),
            ((3, size, width), BF),
            ((3, size, width), BF),
            ((3, size // 2, width), BF),
            ((3, size, width), BF),
            ((3, size, width), BF),
        ],
        (nm, mid, g_all, wgc, wuc, w_down),
        far=(0, 2, 3, 4, 5),
        far_outs=(4, 5),
        dmas=(48, 12),
    )
    pieces, third = (n, half, wide), (3, n, half, cols)
    ends = [(2, half, n * hidden), (2, half, n * hidden), (2, hidden // 2, width), (3, 2, half, width), (2, cols // 2, width)]
    lines = [pieces, pieces, (hidden // 2, width), third, (cols // 2, width)]
    layer_out, input_grad, first_grad, sum_gate, sum_up, sum_down, sum_qkv, sum_out = call(
        functools.partial(back_kernel, n, copies // 2),
        "back",
        3,
        [((size, width), BF), ((size, width), F32), ((size, width), F32)] + [(e, BF) for e in ends],
        [
            ((size, width), F32),
            ((size, width), F32),
            ((size, width), BF),
            ((n - 3, size, width), BF),
            ((size, width), BF),
            ((length, 3 * cols), BF),
            (tiles, BF),
            ((length, cols), BF),
            ((length, width), BF),
            ((width, 3 * cols), BF),
            ((cols, width), BF),
            ((length, 128), F32),
            ((length, 128), F32),
            ((16, width), BF),
            ((size, width), F32),
            ((length, width), BF),
            ((length, cols), F32),
            ((length, cols), F32),
            ((length, 3 * cols), BF),
            ((size, width), BF),
            ((n, size, width), BF),
            ((n, size, width), BF),
            ((size, width), F32),
            ((3, width, cols), BF),
            ((2, cols // 2, width), BF),
        ]
        + [(e, BF) for e in ends]
        + [(shape, BF) for shape in (pieces, pieces, third, lines[4])]
        + [(shape, BF) for shape in lines]
        + [(shape, BF) for shape in (pieces, pieces, third, lines[4])]
        + [(pieces, BF), (pieces, BF), (third, BF), (pieces, BF), (pieces, BF)],
        (
            rest,
            partial,
            mid,
            cotangent,
            g2_all,
            window_split,
            tokens,
            qkv,
            probs,
            att,
            nrm,
            wqkv,
            w_out,
            cos,
            sin,
            running_grad,
            g1_all,
            base_out,
            rest_out,
            grad_gate.reshape(n, 2, half, wide),
            grad_up.reshape(n, 2, half, wide),
            total_down,
        ),
        smem=(5,),
        far=(0, 1, 2, 3, *range(6, 22)),
        far_outs=range(3, 8),
        dmas=(160, 32),
    )
    sums = (
        sum_gate.reshape(rows, -1),
        sum_up.reshape(rows, -1),
        sum_down.reshape(hidden, width),
        sum_qkv.reshape(3, rows, width),
        sum_out.reshape(rows, width),
    )
    return tuple(
        finish(
            sums,
            (w_gate, w_up, w_query, w_key, w_value),
            (gain_attn, gain_mlp),
            (layer_out, input_grad, first_grad),
        )
    )


def solution(mesh):
    token, flat, matrix = P(("dp", "fsdp"), None), P("fsdp"), P("fsdp", None)
    return jax.shard_map(
        body,
        mesh=mesh,
        in_specs=(token, token, P("dp"), token, token, flat)
        + (matrix,) * 4
        + (flat,)
        + (matrix,) * 3,
        out_specs=(token, token, token, flat) + (matrix,) * 4 + (flat,) + (matrix,) * 3,
        check_vma=False,
    )
```
